32 devices in a mesh: dp: 8 (over y, x, core), seq: 4 (over z).
Axes of the slice: x: 2, y: 2, z: 4, core: 2. Of those that a mesh axis runs over, the one named last changes fastest.
Arguments:
- hidden: float32 [16, 1024, 1536], P('dp', 'seq'), may hold values from -6 to 6
- out_grad: float32 [16, 1024, 1536], P('dp', 'seq'), may hold values from -6 to 6
- lengths: int32 [16], P('dp'), may hold values from 256 to 1024, as said below
- norm_gain: bfloat16 [2, 1536], P(None, ('dp', 'seq')), may hold values from 0.5 to 1.5
- in_proj: bfloat16 [2, 1536, 6448], P(None, ('dp', 'seq')), may hold values from -0.15625 to 0.15625
- conv_weight: bfloat16 [2, 4, 3328], P(None, None, ('dp', 'seq')), may hold values from -3 to 3
- gate_gain: bfloat16 [2, 3072], P(None, ('dp', 'seq')), may hold values from 0.5 to 1.5
- out_proj: bfloat16 [2, 3072, 1536], P(None, ('dp', 'seq')), may hold values from -0.109375 to 0.109375
- dt_bias: float32 [2, 48], replicated, may hold values from -9.5 to -3.5
- a_log: float32 [2, 48], replicated, may hold values from 0 to 1.5
- d_skip: float32 [2, 48], replicated, may hold values from 0.5 to 1.5
Outputs:
- result: float32 [16, 1024, 1536], P('dp', 'seq')
- grad_hidden: float32 [16, 1024, 1536], P('dp', 'seq')
- grad_norm_gain: float32 [2, 1536], P(None, ('dp', 'seq'))
- grad_in_proj: float32 [2, 1536, 6448], P(None, ('dp', 'seq'))
- grad_conv_weight: float32 [2, 4, 3328], P(None, None, ('dp', 'seq'))
- grad_gate_gain: float32 [2, 3072], P(None, ('dp', 'seq'))
- grad_out_proj: float32 [2, 3072, 1536], P(None, ('dp', 'seq'))
- grad_dt_bias: float32 [2, 48], replicated
- grad_a_log: float32 [2, 48], replicated
- grad_d_skip: float32 [2, 48], replicated
The draws below stay inside these ranges and needn't reach their ends.
Inputs may be any that keep to these rules, and one draw needn't show every extreme that they name: Positions from lengths[b] on are padding. Among the 2 slots of each index of dp, one has length 1024 and another 256.
All inputs are finite; a program needn't handle non-finite values.
Results may differ from the reference program's by a relative error of at most 0.0084.
Values may be sent and summed in bfloat16 or wider, within the bound.
A program may use at most 448 MiB of HBM per device.

```python
import jax
import jax.numpy as jnp
from jax import lax

D = 1536
HEADS = 48
HEADDIM = 64
NSTATE = 128
CONV = 4
LAYERS = 2
SEQLEN = 1024
SLOTS_DEV = 2
INNER = 3072
CONVCH = 3328
PROJ = 6448
MINLEN = 256
BATCH = 16
N_SEQ = 4


def draw_lengths(key, part):
    key = jax.random.fold_in(key, 7)
    first_key, second_key = jax.random.split(key)
    group_count = BATCH // SLOTS_DEV
    drawn = jax.random.randint(first_key, (group_count, SLOTS_DEV), MINLEN, SEQLEN + 1)
    scores = jax.random.randint(second_key, (group_count, SLOTS_DEV), 0, 1 << 20) * SLOTS_DEV
    scores = scores + jnp.arange(SLOTS_DEV, dtype=jnp.int32)[None, :]
    ranking = jnp.argsort(jnp.argsort(scores, axis=1), axis=1)
    chosen = jnp.where(ranking == 0, SEQLEN, jnp.where(ranking == 1, MINLEN, drawn))
    return chosen.reshape(BATCH).astype(jnp.int32)


def shard_levels(key, extent, cuts, low, top_value):
    level = 1.0
    for position, blocks in cuts:
        heights = jax.random.uniform(jax.random.fold_in(jax.random.fold_in(key, 6), position), (blocks,), jnp.float32, low / len(cuts), top_value / len(cuts))
        level = level * jnp.repeat(jnp.exp(heights), extent[position] // blocks).reshape((-1,) + (1,) * (len(extent) - 1 - position))
    return level


def bell_draw(stream_key, dims, scale, reach, shards=(), kind=jnp.bfloat16):
    values = scale * jax.random.normal(stream_key, dims, jnp.float32)
    if shards:
        values = values * shard_levels(stream_key, dims, shards, -0.22, 0.18)
    return jnp.clip(values, -reach, reach).astype(kind)


def setup_inputs(seed: int = 0) -> dict:
    keys = jax.random.split(jax.random.key(seed), 12)
    return {
        "hidden": bell_draw(keys[0], (BATCH, SEQLEN, D), 1.0, 6.0, ((0, 8), (1, 4)), jnp.float32),
        "out_grad": bell_draw(keys[1], (BATCH, SEQLEN, D), 1.0, 6.0, ((0, 8), (1, 4)), jnp.float32),
        "lengths": draw_lengths(jax.random.fold_in(keys[11], 71), 0),
        "norm_gain": jnp.clip(1.0 + 0.1 * jax.random.normal(keys[3], (LAYERS, D), jnp.float32), 0.5, 1.5).astype(jnp.bfloat16),
        "in_proj": bell_draw(keys[4], (LAYERS, D, PROJ), D ** -0.5, 0.15625, ((1, 32),)),
        "conv_weight": bell_draw(keys[5], (LAYERS, CONV, CONVCH), CONV ** -0.5, 3.0, ((2, 32),)),
        "gate_gain": jnp.clip(1.0 + 0.1 * jax.random.normal(keys[6], (LAYERS, INNER), jnp.float32), 0.5, 1.5).astype(jnp.bfloat16),
        "out_proj": bell_draw(keys[7], (LAYERS, INNER, D), INNER ** -0.5, 0.109375, ((1, 32),)),
        "dt_bias": jnp.clip(jax.random.uniform(keys[8], (LAYERS, HEADS), jnp.float32, -9.5, -3.5), -9.5, -3.5),
        "a_log": jnp.clip(jax.random.uniform(keys[9], (LAYERS, HEADS), jnp.float32, 0.0, 1.5), 0.0, 1.5),
        "d_skip": jnp.clip(jax.random.uniform(keys[10], (LAYERS, HEADS), jnp.float32, 0.5, 1.5), 0.5, 1.5),
    }


epsilon = 1e-05
exact_product = lax.Precision.HIGHEST

@jax.custom_vjp
def low(v):
    return lax.optimization_barrier(v.astype(jnp.bfloat16)).astype(jnp.float32)

@jax.custom_vjp
def low_back(v):
    return v

def low_keep(v):
    return (low(v), None)

def low_pass(kept, grad):
    return (grad,)

def back_keep(v):
    return (v, None)

def back_low(kept, grad):
    return (low(grad),)
low.defvjp(low_keep, low_pass)
low_back.defvjp(back_keep, back_low)

def norm_rows(vector, gain_row):
    inverse_rms = lax.rsqrt(lax.optimization_barrier(jnp.mean(vector * vector, axis=-1, keepdims=True)) + epsilon)
    return vector * inverse_rms * gain_row

def front_part(extended, raw_step, conv_kernel, step_bias, decay_log):
    length = extended.shape[1] - conv_kernel.shape[0] + 1
    convolved = conv_kernel[0] * extended[:, 0:length]
    for offset in range(1, conv_kernel.shape[0]):
        convolved = convolved + conv_kernel[offset] * extended[:, offset:offset + length]
    activated = jax.nn.silu(convolved)
    values = activated[..., :INNER].reshape(activated.shape[0], length, HEADS, HEADDIM)
    input_map = activated[..., INNER:INNER + NSTATE]
    output_map = activated[..., INNER + NSTATE:]
    step_size = jax.nn.softplus(raw_step + step_bias)
    log_decay = -step_size * jnp.exp(decay_log)
    return (values, input_map, output_map, step_size, log_decay)

def mix_out(values, input_map, output_map, step_size, log_decay, skip_gain, state_in):
    cumulative = jnp.cumsum(log_decay, axis=1)
    length = log_decay.shape[1]
    causal = (jnp.arange(length)[:, None] >= jnp.arange(length)[None, :])[None, :, :, None]
    spread = cumulative[:, :, None, :] - cumulative[:, None, :, :]
    decays = jnp.where(causal, jnp.exp(jnp.where(causal, spread, 0.0)), 0.0)
    intersection = jnp.einsum('stn,srn->str', output_map, input_map, precision=exact_product)
    weights = decays * intersection[..., None] * step_size[:, None, :, :]
    mixture = jnp.einsum('strh,srhp->sthp', weights, values, precision=exact_product)
    carried = jnp.einsum('stn,shpn->sthp', output_map, state_in, precision=exact_product)
    return mixture + carried * jnp.exp(cumulative)[..., None] + skip_gain[:, None] * values

def state_part(values, input_map, step_size, log_decay):
    cumulative = jnp.cumsum(log_decay, axis=1)
    remaining = jnp.exp(cumulative[:, -1:, :] - cumulative) * step_size
    weighted = remaining[..., None] * values
    return jnp.einsum('srhp,srn->shpn', weighted, input_map, precision=exact_product)

def mixing(values, input_map, output_map, step_size, log_decay, skip_gain, state_in):
    mixture = mix_out(values, input_map, output_map, step_size, log_decay, skip_gain, state_in)
    total_decay = jnp.exp(lax.optimization_barrier(jnp.sum(log_decay, axis=1)))
    state_out = total_decay[..., None, None] * state_in + state_part(values, input_map, step_size, log_decay)
    return (mixture, state_out)

def gate_part(mixture, gate_in, gate_gain):
    gated = mixture.reshape(gate_in.shape) * jax.nn.silu(gate_in)
    return norm_rows(gated, gate_gain)

def scan_mix(values, input_map, output_map, step_size, log_decay, skip_gain):
    slot_count, length = (log_decay.shape[0], log_decay.shape[1])
    block_len = length // N_SEQ

    def blocked(array):
        shaped = array.reshape((slot_count, N_SEQ, block_len) + array.shape[2:])
        return jnp.moveaxis(shaped, 1, 0)

    @jax.checkpoint
    def advance(carry_state, pieces):
        block_values, block_input, block_output, block_step, block_log = pieces
        mixture, state_next = mixing(block_values, block_input, block_output, block_step, block_log, skip_gain, carry_state)
        return (state_next, mixture)
    initial = jnp.zeros((slot_count, HEADS, HEADDIM, NSTATE), jnp.float32)
    pieces = (blocked(values), blocked(input_map), blocked(output_map), blocked(step_size), blocked(log_decay))
    last_state, mixture = lax.scan(advance, initial, pieces)
    return jnp.moveaxis(mixture, 0, 1).reshape(values.shape)

def layer_forward(hidden_in, valid_rows, layer_params):
    gain_norm, input_weight, conv_kernel, gain_gate, output_weight, step_bias, decay_log, skip_gain = layer_params
    normalized_input = low(norm_rows(hidden_in, gain_norm))
    projected_rows = low_back(jnp.einsum('yji,ip->yjp', normalized_input, input_weight, precision=exact_product))
    gate_in = projected_rows[..., :INNER]
    conv_in = projected_rows[..., INNER:INNER + CONVCH]
    raw_step = projected_rows[..., INNER + CONVCH:]
    extended = jnp.pad(conv_in, ((0, 0), (CONV - 1, 0), (0, 0)))
    values, input_map, output_map, step_size, log_decay = front_part(extended, raw_step, conv_kernel, step_bias, decay_log)
    mixture = scan_mix(values, input_map, output_map, step_size, log_decay, skip_gain)
    normalized_output = low(gate_part(mixture, gate_in, gain_gate))
    branch_output = low_back(jnp.einsum('nrc,co->nro', normalized_output, output_weight, precision=exact_product))
    return hidden_in + valid_rows * branch_output

def reference(hidden, out_grad, lengths, norm_gain, in_proj, conv_weight, gate_gain, out_proj, dt_bias, a_log, d_skip):
    params = (norm_gain.astype(jnp.float32), in_proj.astype(jnp.float32), conv_weight.astype(jnp.float32), gate_gain.astype(jnp.float32), out_proj.astype(jnp.float32), dt_bias, a_log, d_skip)
    group_count = BATCH // SLOTS_DEV

    def one_group(totals, pieces):
        hidden_group, grad_group, length_group = pieces
        valid_rows = (jnp.arange(SEQLEN)[None, :] < length_group[:, None]).astype(jnp.float32)[..., None]

        def apply_group(hidden_start, all_params):
            current = hidden_start
            for layer_index in range(LAYERS):
                current = layer_forward(current, valid_rows, [param[layer_index] for param in all_params])
            return current
        outcome, pullback = jax.vjp(apply_group, hidden_group, params)
        grad_start, grad_params = pullback(grad_group)
        totals = jax.tree.map(lambda first_part, second_part: first_part + second_part, totals, grad_params)
        return (totals, (outcome, grad_start))
    zeros_tree = jax.tree.map(jnp.zeros_like, params)
    groups = (hidden.reshape(group_count, SLOTS_DEV, SEQLEN, D), out_grad.reshape(group_count, SLOTS_DEV, SEQLEN, D), lengths.reshape(group_count, SLOTS_DEV))
    totals, stacked = lax.scan(one_group, zeros_tree, groups)
    result = stacked[0].reshape(BATCH, SEQLEN, D)
    grad_hidden = stacked[1].reshape(BATCH, SEQLEN, D)
    return (result, grad_hidden, totals[0], totals[1], totals[2], totals[3], totals[4], totals[5], totals[6], totals[7])
```

```python
import functools

import jax
import jax.numpy as jnp
from jax import lax
from jax.experimental import pallas as pl
from jax.experimental.pallas import tpu as pltpu
from jax.sharding import PartitionSpec as P

D = 1536
HEADS = 48
HEADDIM = 64
NSTATE = 128
CONV = 4
LAYERS = 2
INNER = 3072
CONVCH = 3328
PROJ = 6448
SLOTS = 2
SHORT = 256

LANES = 128
WIDE = 6656
BLK = 256
NB = INNER // BLK
COLS = 512
PER = BLK // HEADDIM
CHAIN = 512
PARTS = CHAIN // BLK

f32 = jnp.float32
bf16 = jnp.bfloat16
epsilon = 1e-05
VMEM_LIMIT = 58 << 20


def params(**more):
    return pltpu.CompilerParams(vmem_limit_bytes=VMEM_LIMIT, **more)


def for_rows(total, size, function):
    def step(index, carry):
        function(pl.ds(pl.multiple_of(index * size, size), size))
        return carry

    lax.fori_loop(0, total // size, step, 0)


def dot(left, right):
    return jnp.dot(left, right, preferred_element_type=f32)


def dot_nt(left, right):
    return lax.dot_general(left, right, (((1,), (1,)), ((), ())), preferred_element_type=f32)


def dot_tn(left, right):
    return lax.dot_general(left, right, (((0,), (0,)), ((), ())), preferred_element_type=f32)


def dot_exact(left, right):
    return jnp.dot(left, right, preferred_element_type=f32, precision=lax.Precision.HIGHEST)


def halves(array):
    high = array.astype(bf16)
    return high, (array - high.astype(f32)).astype(bf16)


def dot_halves(left, right, product=dot):
    left_high, left_low = left
    right_high, right_low = right
    return product(left_high, right_high) + product(left_high, right_low) + product(left_low, right_high)


def dot_member(array, member):
    high, low = halves(array)
    return dot(high, member) + dot(low, member)


def sigmoid(vector):
    return 0.5 + 0.5 * jnp.tanh(0.5 * vector)


def softplus(vector):
    return jnp.maximum(vector, 0.0) + jnp.log1p(jnp.exp(-jnp.abs(vector)))


def spread(columns):
    length = columns.shape[0]
    return jnp.concatenate(
        [jnp.broadcast_to(columns[:, j : j + 1], (length, HEADDIM)) for j in range(PER)], axis=1
    )


def heads_first(columns, block):
    return pltpu.roll(columns, lax.rem(LANES - PER * block, LANES), 1)


def load_extended(scratch, edge_ref, rows_ref):
    scratch[0:8, :] = edge_ref[0]
    scratch[8:, :] = rows_ref[0]


def convolve(scratch, taps, length):
    total = taps[0:1] * scratch[5 : 5 + length, :]
    for k in range(1, CONV):
        total = total + taps[k : k + 1] * scratch[5 + k : 5 + k + length, :]
    return total


def lower(length):
    first = lax.broadcasted_iota(jnp.int32, (length, length), 0)
    second = lax.broadcasted_iota(jnp.int32, (length, length), 1)
    return first >= second


def project_kernel(h_ref, gain_ref, w_ref, proj_ref, raw_ref, normed_ref):
    step = pl.program_id(0)
    total = h_ref.shape[0]

    @pl.when(step == 0)
    def _():
        def one(rows):
            h = h_ref[rows, :]
            inverse = lax.rsqrt(jnp.mean(h * h, axis=-1, keepdims=True) + epsilon)
            normed_ref[rows, :] = (h * inverse * gain_ref[...]).astype(bf16)

        for_rows(total, 32, one)

    product = dot(normed_ref[...], w_ref[...])
    proj_ref[...] = product

    @pl.when(step == pl.num_programs(0) - 1)
    def _():
        raw_ref[...] = product[:, COLS - 2 * LANES : COLS - LANES]


def project(h, gain_row, weight):
    total = h.shape[0]
    return pl.pallas_call(
        project_kernel,
        name="project",
        grid=(WIDE // COLS,),
        in_specs=[
            pl.BlockSpec((total, D), lambda n: (0, 0)),
            pl.BlockSpec((1, D), lambda n: (0, 0)),
            pl.BlockSpec((D, COLS), lambda n: (0, n)),
        ],
        out_specs=[
            pl.BlockSpec((total, COLS), lambda n: (0, n)),
            pl.BlockSpec((total, LANES), lambda n: (0, 0)),
            pl.BlockSpec((total, D), lambda n: (0, 0)),
        ],
        out_shape=[
            jax.ShapeDtypeStruct((total, WIDE), f32),
            jax.ShapeDtypeStruct((total, LANES), f32),
            jax.ShapeDtypeStruct((total, D), bf16),
        ],
        compiler_params=params(),
        cost_estimate=pl.CostEstimate(
            flops=2 * total * D * WIDE, bytes_accessed=2 * D * WIDE, transcendentals=0
        ),
    )(h, gain_row, weight)


def mix_kernel(
    rows_ref, edge_ref, taps_ref, maps_ref, maps_edge_ref, maps_taps_ref, raw_ref, heads_ref, skip_ref,
    y_ref, state_ref, cum_ref, step_ref, act_ref, decay_ref,
    extended, inner, cum_t, input_t,
):
    block = pl.program_id(1)
    length = rows_ref.shape[1]

    @pl.when(block == 0)
    def _():
        load_extended(extended, maps_edge_ref, maps_ref)
        convolved = convolve(extended, maps_taps_ref[...], length)
        maps = convolved * sigmoid(convolved)
        act_ref[0] = maps
        products = dot_halves(halves(maps[:, NSTATE:]), halves(maps[:, :NSTATE]), dot_nt)
        input_t[0], input_t[1] = halves(maps[:, :NSTATE].T)
        causal = lower(length)
        inner[...] = jnp.where(causal, products, 0.0)
        size = softplus(raw_ref[0] + heads_ref[0:1, :])
        decay = -size * jnp.exp(heads_ref[1:2, :])
        cum = dot_exact(causal.astype(f32), decay)
        cum_ref[0] = cum
        step_ref[0] = size
        cum_t[...] = cum.T

    load_extended(extended, edge_ref, rows_ref)
    convolved = convolve(extended, taps_ref[...], length)
    values = convolved * sigmoid(convolved)
    cum = heads_first(cum_ref[0], block)
    stepped = values * spread(heads_first(step_ref[0], block))
    low = stepped.astype(bf16)
    parts = []
    for j in range(PER):
        row = cum_t[pl.ds(block * PER + j, 1), :]
        column = cum[:, j : j + 1]
        pieces = []
        for first in range(0, length, LANES):
            end = first + LANES
            decays = jnp.exp(jnp.minimum(column[first:end] - row[:, :end], 0.0))
            weights = (inner[first:end, :end] * decays).astype(bf16)
            pieces.append(dot(weights, low[:end, j * HEADDIM : (j + 1) * HEADDIM]))
        parts.append(jnp.concatenate(pieces, axis=0))
    y_ref[0] = jnp.concatenate(parts, axis=1) + skip_ref[...] * values
    final = cum[length - 1 :, :]
    remaining = jnp.exp(final - cum)
    state_ref[0] = dot_halves((input_t[0], input_t[1]), halves(stepped * spread(remaining)))
    decay_ref[0] = jnp.broadcast_to(spread(jnp.exp(final)), (8, BLK))


def mix(proj, edge, taps, raw, heads, skip_row):
    length = proj.shape[1]
    return pl.pallas_call(
        mix_kernel,
        name="mix",
        grid=(SLOTS, NB),
        in_specs=[
            pl.BlockSpec((1, length, BLK), lambda s, b: (s, 0, NB + b)),
            pl.BlockSpec((1, 8, BLK), lambda s, b: (s, 0, b)),
            pl.BlockSpec((8, BLK), lambda s, b: (0, b)),
            pl.BlockSpec((1, length, BLK), lambda s, b: (s, 0, 2 * NB)),
            pl.BlockSpec((1, 8, BLK), lambda s, b: (s, 0, NB)),
            pl.BlockSpec((8, BLK), lambda s, b: (0, NB)),
            pl.BlockSpec((1, length, LANES), lambda s, b: (s, 0, 0)),
            pl.BlockSpec((8, LANES), lambda s, b: (0, 0)),
            pl.BlockSpec((1, BLK), lambda s, b: (0, b)),
        ],
        out_specs=[
            pl.BlockSpec((1, length, BLK), lambda s, b: (s, 0, b)),
            pl.BlockSpec((1, NSTATE, BLK), lambda s, b: (s, 0, b)),
            pl.BlockSpec((1, length, LANES), lambda s, b: (s, 0, 0)),
            pl.BlockSpec((1, length, LANES), lambda s, b: (s, 0, 0)),
            pl.BlockSpec((1, length, BLK), lambda s, b: (s, 0, 0)),
            pl.BlockSpec((1, 8, BLK), lambda s, b: (s, 0, b)),
        ],
        out_shape=[
            jax.ShapeDtypeStruct((SLOTS, length, INNER), f32),
            jax.ShapeDtypeStruct((SLOTS, NSTATE, INNER), f32),
            jax.ShapeDtypeStruct((SLOTS, length, LANES), f32),
            jax.ShapeDtypeStruct((SLOTS, length, LANES), f32),
            jax.ShapeDtypeStruct((SLOTS, length, BLK), f32),
            jax.ShapeDtypeStruct((SLOTS, 8, INNER), f32),
        ],
        scratch_shapes=[
            pltpu.VMEM((length + 8, BLK), f32),
            pltpu.VMEM((length, length), f32),
            pltpu.VMEM((LANES, length), f32),
            pltpu.VMEM((2, NSTATE, length), bf16),
        ],
        compiler_params=params(),
        cost_estimate=pl.CostEstimate(flops=6 * 10**9, bytes_accessed=10**7, transcendentals=10**7),
    )(proj, edge, taps, proj, edge, taps, raw, heads, skip_row)


def branch_kernel(
    y_ref, gate_ref, act_ref, cum_ref, state_ref, gain_ref, w_ref, h_ref, valid_ref,
    out_ref, mixture_ref, inverse_ref,
    total, squares, gated_low,
):
    block = pl.program_id(0)
    count = state_ref.shape[0]
    rows = y_ref.shape[0]
    length = rows // SLOTS

    @pl.when(block == 0)
    def _():
        total[...] = jnp.zeros_like(total)
        squares[...] = jnp.zeros_like(squares)

    for slot in range(SLOTS):
        span = slice(slot * length, (slot + 1) * length)
        mixture = y_ref[span, :]
        if slot < count:
            cum = heads_first(cum_ref[span, :], block)
            carried = dot_member(act_ref[span, NSTATE:], state_ref[slot, 0])
            mixture = mixture + carried * spread(jnp.exp(cum))
        gate = gate_ref[span, :]
        gated = mixture * gate * sigmoid(gate)
        mixture_ref[span, :] = mixture
        square = gated * gated
        squares[span, :] += square[:, :LANES] + square[:, LANES:]
        gated_low[span, :] = (gated * gain_ref[...]).astype(bf16)
    total[...] += dot(gated_low[...], w_ref[...])

    @pl.when(block == NB - 1)
    def _():
        def one(span):
            mean = jnp.sum(squares[span, :], axis=-1, keepdims=True) / INNER
            inverse = lax.rsqrt(mean + epsilon)
            inverse_ref[span, :] = jnp.broadcast_to(inverse, (32, LANES))
            factor = inverse * valid_ref[span, 0:1]
            out_ref[span, :] = h_ref[span, :] + factor * total[span, :]

        for_rows(rows, 32, one)


def branch(y, proj, act, cum, state, gain_row, weight, h, valid):
    rows = h.shape[0]
    count = state.shape[0]
    return pl.pallas_call(
        branch_kernel,
        name="branch",
        grid=(NB,),
        in_specs=[
            pl.BlockSpec((rows, BLK), lambda b: (0, b)),
            pl.BlockSpec((rows, BLK), lambda b: (0, b)),
            pl.BlockSpec((rows, BLK), lambda b: (0, 0)),
            pl.BlockSpec((rows, LANES), lambda b: (0, 0)),
            pl.BlockSpec((count, 1, NSTATE, BLK), lambda b: (0, b // PARTS, 0, b % PARTS)),
            pl.BlockSpec((1, BLK), lambda b: (0, b)),
            pl.BlockSpec((BLK, D), lambda b: (b, 0)),
            pl.BlockSpec((rows, D), lambda b: (0, 0)),
            pl.BlockSpec((rows, LANES), lambda b: (0, 0)),
        ],
        out_specs=[
            pl.BlockSpec((rows, D), lambda b: (0, 0)),
            pl.BlockSpec((rows, BLK), lambda b: (0, b)),
            pl.BlockSpec((rows, LANES), lambda b: (0, 0)),
        ],
        out_shape=[
            jax.ShapeDtypeStruct((rows, D), f32),
            jax.ShapeDtypeStruct((rows, INNER), f32),
            jax.ShapeDtypeStruct((rows, LANES), f32),
        ],
        scratch_shapes=[
            pltpu.VMEM((rows, D), f32),
            pltpu.VMEM((rows, LANES), f32),
            pltpu.VMEM((rows, BLK), bf16),
        ],
        compiler_params=params(),
        cost_estimate=pl.CostEstimate(
            flops=2 * rows * D * INNER, bytes_accessed=2 * D * INNER, transcendentals=10**6
        ),
    )(y, proj, act, cum, state, gain_row, weight, h, valid)


def unbranch_kernel(
    g_ref, valid_ref, mixture_ref, gate_ref, inverse_ref, gain_ref, w_ref,
    back_ref, mean_ref, gain_out_ref, w_out_ref,
    low, norm_low,
):
    block = pl.program_id(0)
    rows = g_ref.shape[0]

    @pl.when(block == 0)
    def _():
        def one(span):
            low[span, :] = (valid_ref[span, 0:1] * g_ref[span, :]).astype(bf16)

        for_rows(rows, 32, one)
        mean_ref[...] = jnp.zeros_like(mean_ref)

    back_ref[...] = dot_nt(low[...], w_ref[...])
    gain_out_ref[...] = jnp.zeros_like(gain_out_ref)

    def one(span):
        gate = gate_ref[span, :]
        gated = mixture_ref[span, :] * gate * sigmoid(gate)
        back = back_ref[span, :]
        unit = gated * inverse_ref[span, 0:1]
        norm_low[span, :] = (unit * gain_ref[...]).astype(bf16)
        gain_out_ref[0:1, :] += jnp.sum(back * unit, axis=0, keepdims=True)
        product = gated * back * gain_ref[...]
        mean_ref[span, :] += product[:, :LANES] + product[:, LANES:]

    for_rows(rows, 128, one)
    w_out_ref[...] = dot_tn(norm_low[...], low[...]).astype(bf16)

    @pl.when(block == NB - 1)
    def _():
        mean_ref[...] = jnp.broadcast_to(
            jnp.sum(mean_ref[...], axis=-1, keepdims=True) / INNER, mean_ref.shape
        )


def unbranch(g, valid, mixture, proj, inverse, gain_row, weight):
    rows = g.shape[0]
    return pl.pallas_call(
        unbranch_kernel,
        name="unbranch",
        grid=(NB,),
        in_specs=[
            pl.BlockSpec((rows, D), lambda b: (0, 0)),
            pl.BlockSpec((rows, LANES), lambda b: (0, 0)),
            pl.BlockSpec((rows, BLK), lambda b: (0, b)),
            pl.BlockSpec((rows, BLK), lambda b: (0, b)),
            pl.BlockSpec((rows, LANES), lambda b: (0, 0)),
            pl.BlockSpec((1, BLK), lambda b: (0, b)),
            pl.BlockSpec((BLK, D), lambda b: (b, 0)),
        ],
        out_specs=[
            pl.BlockSpec((rows, BLK), lambda b: (0, b)),
            pl.BlockSpec((rows, LANES), lambda b: (0, 0)),
            pl.BlockSpec((8, BLK), lambda b: (0, b)),
            pl.BlockSpec((BLK, D), lambda b: (b, 0)),
        ],
        out_shape=[
            jax.ShapeDtypeStruct((rows, INNER), f32),
            jax.ShapeDtypeStruct((rows, LANES), f32),
            jax.ShapeDtypeStruct((8, INNER), f32),
            jax.ShapeDtypeStruct((INNER, D), bf16),
        ],
        scratch_shapes=[pltpu.VMEM((rows, D), bf16), pltpu.VMEM((rows, BLK), bf16)],
        compiler_params=params(),
        cost_estimate=pl.CostEstimate(
            flops=4 * rows * D * INNER, bytes_accessed=4 * D * INNER, transcendentals=10**6
        ),
    )(g, valid, mixture, proj, inverse, gain_row, weight)


def ungate_kernel(
    back_ref, mixture_ref, gate_ref, inverse_ref, mean_ref, gain_ref, act_ref, cum_ref,
    dy_ref, dgate_ref, state_ref,
    output_t,
):
    block = pl.program_id(0)
    rows = back_ref.shape[0]
    length = rows // SLOTS

    @pl.when(block == 0)
    def _():
        for slot in range(state_ref.shape[0]):
            span = slice(slot * length, (slot + 1) * length)
            output_t[slot, 0], output_t[slot, 1] = halves(act_ref[span, NSTATE:].T)

    for slot in range(SLOTS):
        span = slice(slot * length, (slot + 1) * length)
        gate = gate_ref[span, :]
        curve = sigmoid(gate)
        mixture = mixture_ref[span, :]
        swish = gate * curve
        inverse = inverse_ref[span, 0:1]
        back = back_ref[span, :] * gain_ref[...]
        pull = inverse * inverse * inverse * mean_ref[span, 0:1]
        grad = inverse * back - (mixture * swish) * pull
        dy = grad * swish
        dy_ref[span, :] = dy
        dgate_ref[span, :] = (grad * mixture * curve * (1.0 + gate * (1.0 - curve))).astype(bf16)
        if slot < state_ref.shape[0]:
            grown = spread(jnp.exp(heads_first(cum_ref[span, :], block)))
            state_ref[slot] = dot_halves((output_t[slot, 0], output_t[slot, 1]), halves(dy * grown))


def ungate(back, mixture, proj, inverse, mean, gain_row, act, cum, count):
    rows = back.shape[0]
    length = rows // SLOTS
    return pl.pallas_call(
        ungate_kernel,
        name="ungate",
        grid=(NB,),
        in_specs=[
            pl.BlockSpec((rows, BLK), lambda b: (0, b)),
            pl.BlockSpec((rows, BLK), lambda b: (0, b)),
            pl.BlockSpec((rows, BLK), lambda b: (0, b)),
            pl.BlockSpec((rows, LANES), lambda b: (0, 0)),
            pl.BlockSpec((rows, LANES), lambda b: (0, 0)),
            pl.BlockSpec((1, BLK), lambda b: (0, b)),
            pl.BlockSpec((rows, BLK), lambda b: (0, 0)),
            pl.BlockSpec((rows, LANES), lambda b: (0, 0)),
        ],
        out_specs=[
            pl.BlockSpec((rows, BLK), lambda b: (0, b)),
            pl.BlockSpec((rows, BLK), lambda b: (0, b)),
            pl.BlockSpec((count, NSTATE, BLK), lambda b: (0, 0, b)),
        ],
        out_shape=[
            jax.ShapeDtypeStruct((rows, INNER), f32),
            jax.ShapeDtypeStruct((rows, WIDE), bf16),
            jax.ShapeDtypeStruct((count, NSTATE, INNER), f32),
        ],
        scratch_shapes=[pltpu.VMEM((count, 2, NSTATE, length), bf16)],
        compiler_params=params(),
        cost_estimate=pl.CostEstimate(flops=10**9, bytes_accessed=2 * 10**7, transcendentals=10**7),
    )(back, mixture, proj, inverse, mean, gain_row, act, cum)


def unmix_kernel(
    rows_ref, edge_ref, taps_ref, maps_ref, maps_edge_ref, maps_taps_ref, raw_ref, heads_ref, skip_ref,
    dy_ref, state_ref, later_ref, cum_ref, step_ref, act_ref, grads_in_ref,
    grads_ref, edge_out_ref, taps_out_ref, heads_out_ref,
    extended, inner, d_inner, cum_t, grad_ext, d_maps, d_cum, d_step, over_rows, sums,
):
    del grads_in_ref
    block = pl.program_id(1)
    length = rows_ref.shape[1]
    count = state_ref.shape[0]

    def conv_back(gradient, taps):
        grad_ext[8 : 8 + length, :] = gradient
        back = taps[0:1] * grad_ext[3 : 3 + length + 8, :]
        for k in range(1, CONV):
            back = back + taps[k : k + 1] * grad_ext[3 - k : 3 - k + length + 8, :]
        edge_out_ref[0] = back[:8]
        grads_ref[0] = back[8:].astype(bf16)
        lines = [
            jnp.sum(gradient * extended[5 + k : 5 + k + length, :], axis=0, keepdims=True)
            for k in range(CONV)
        ]
        lines.append(jnp.zeros((8 - CONV, BLK), f32))
        taps_out_ref[0] = jnp.concatenate(lines, axis=0)

    @pl.when(block == 0)
    def _():
        grad_ext[0:8, :] = jnp.zeros((8, BLK), f32)
        grad_ext[8 + length :, :] = jnp.zeros((8, BLK), f32)
        maps = act_ref[0]
        products = dot_halves(halves(maps[:, :NSTATE]), halves(maps[:, NSTATE:]), dot_nt)
        inner[...] = jnp.where(lower(length).T, products, 0.0)
        cum_t[...] = cum_ref[0].T
        d_inner[...] = jnp.zeros_like(d_inner)
        d_maps[...] = jnp.zeros_like(d_maps)
        d_cum[...] = jnp.zeros_like(d_cum)
        d_step[...] = jnp.zeros_like(d_step)
        over_rows[...] = jnp.zeros_like(over_rows)
        sums[...] = jnp.zeros_like(sums)

    @pl.when(block < NB)
    def _():
        load_extended(extended, edge_ref, rows_ref)
        convolved = convolve(extended, taps_ref[...], length)
        curve = sigmoid(convolved)
        values = convolved * curve
        cum = heads_first(cum_ref[0], block)
        size = spread(heads_first(step_ref[0], block))
        stepped = values * size
        low = stepped.astype(bf16)
        dy = dy_ref[0]
        dy_low = dy.astype(bf16)
        lane = lax.broadcasted_iota(jnp.int32, (1, LANES), 1)
        parts = []
        for j in range(PER):
            head = block * PER + j
            row = cum_t[pl.ds(head, 1), :]
            column = cum[:, j : j + 1]
            dy_head = dy_low[:, j * HEADDIM : (j + 1) * HEADDIM]
            low_head = low[:, j * HEADDIM : (j + 1) * HEADDIM]
            pieces = []
            row_sums = []
            column_sums = None
            for first in range(0, length, LANES):
                end = first + LANES
                decays = jnp.exp(jnp.minimum(row[:, first:] - column[first:end], 0.0))
                products = inner[first:end, first:]
                weights = (products * decays).astype(bf16)
                grads = dot_nt(low_head[first:end], dy_head[first:]) * decays
                d_inner[first:end, first:] += grads
                pieces.append(dot(weights, dy_head[first:]))
                moved = grads * products
                row_sums.append(jnp.sum(moved, axis=1, keepdims=True))
                found = jnp.sum(moved, axis=0, keepdims=True)
                if first:
                    found = jnp.concatenate([jnp.zeros((1, first), f32), found], axis=1)
                column_sums = found if column_sums is None else column_sums + found
            parts.append(jnp.concatenate(pieces, axis=0))
            over_rows[pl.ds(head, 1), :] = column_sums
            d_cum[...] -= jnp.where(lane == head, jnp.concatenate(row_sums, axis=0), 0.0)
        d_stepped = jnp.concatenate(parts, axis=1)
        which = lax.broadcasted_iota(jnp.int32, (BLK, LANES), 0) // HEADDIM + block * PER
        chosen = which == lax.broadcasted_iota(jnp.int32, (BLK, LANES), 1)
        member = chosen.astype(f32)
        member_low = chosen.astype(bf16)
        state = state_ref[0, 0]
        later = later_ref[0, 0]
        maps = act_ref[0]
        remaining = spread(jnp.exp(cum[length - 1 :, :] - cum))
        grown = spread(jnp.exp(cum))
        from_later = dot_member(maps[:, :NSTATE], later) * remaining
        d_stepped = d_stepped + from_later
        left = stepped * remaining
        grown_dy = dy * grown
        used = stepped * from_later
        d_cum[...] += dot_member(grown_dy * dot_member(maps[:, NSTATE:], state) - used, member_low)
        d_maps[:, :NSTATE] += dot_nt(left.astype(bf16), later)
        d_maps[:, NSTATE:] += dot_nt(grown_dy.astype(bf16), state)
        d_step[...] += dot_member(d_stepped * values, member_low)
        lines = jnp.concatenate(
            [
                jnp.sum(used, axis=0, keepdims=True),
                jnp.sum(dy * values, axis=0, keepdims=True),
                jnp.sum(later.astype(f32) * state.astype(f32), axis=0, keepdims=True),
                jnp.zeros((5, BLK), f32),
            ],
            axis=0,
        )
        sums[...] += dot_exact(lines, member)
        d_values = d_stepped * size + skip_ref[...] * dy
        conv_back(d_values * curve * (1.0 + convolved * (1.0 - curve)), taps_ref[...])

    @pl.when(block == NB)
    def _():
        load_extended(extended, maps_edge_ref, maps_ref)
        convolved = convolve(extended, maps_taps_ref[...], length)
        curve = sigmoid(convolved)
        maps = act_ref[0]
        d_both = jnp.where(lower(length).T, d_inner[...], 0.0)
        d_input = d_maps[:, :NSTATE] + dot_halves(halves(d_both), halves(maps[:, NSTATE:]))
        d_output = d_maps[:, NSTATE:] + dot_halves(halves(d_both.T), halves(maps[:, :NSTATE]))
        d_both = jnp.concatenate([d_input, d_output], axis=1)
        conv_back(d_both * curve * (1.0 + convolved * (1.0 - curve)), maps_taps_ref[...])

    @pl.when(block == NB + 1)
    def _():
        final = cum_ref[0][length - 1 :, :]
        at_end = sums[0:1, :] + jnp.exp(final) * sums[2:3, :]
        d_total = d_cum[...] + over_rows[...].T
        position = lax.broadcasted_iota(jnp.int32, (length, 1), 0)
        d_total = d_total + jnp.where(position == length - 1, at_end, 0.0)
        d_decay = dot_exact(lower(length).T.astype(f32), d_total)
        rate = jnp.exp(heads_ref[1:2, :])
        size = step_ref[0]
        d_raw = (d_step[...] - d_decay * rate) * sigmoid(raw_ref[0] + heads_ref[0:1, :])
        grads_ref[0] = jnp.concatenate([d_raw, jnp.zeros_like(d_raw)], axis=1).astype(bf16)
        heads_out_ref[0] = jnp.concatenate(
            [
                jnp.sum(d_raw, axis=0, keepdims=True),
                jnp.sum(d_decay * (-size * rate), axis=0, keepdims=True),
                sums[1:2, :],
                jnp.zeros((5, LANES), f32),
            ],
            axis=0,
        )


def unmix(proj, edge, taps, raw, heads, skip_row, dy, state, later, cum, size, act, grads):
    length = proj.shape[1]
    inside = lambda b: jnp.minimum(b, NB - 1)
    upto = lambda b: jnp.minimum(b, NB)
    return pl.pallas_call(
        unmix_kernel,
        name="unmix",
        grid=(SLOTS, NB + 2),
        in_specs=[
            pl.BlockSpec((1, length, BLK), lambda s, b: (s, 0, NB + inside(b))),
            pl.BlockSpec((1, 8, BLK), lambda s, b: (s, 0, inside(b))),
            pl.BlockSpec((8, BLK), lambda s, b: (0, inside(b))),
            pl.BlockSpec((1, length, BLK), lambda s, b: (s, 0, 2 * NB)),
            pl.BlockSpec((1, 8, BLK), lambda s, b: (s, 0, NB)),
            pl.BlockSpec((8, BLK), lambda s, b: (0, NB)),
            pl.BlockSpec((1, length, LANES), lambda s, b: (s, 0, 0)),
            pl.BlockSpec((8, LANES), lambda s, b: (0, 0)),
            pl.BlockSpec((1, BLK), lambda s, b: (0, inside(b))),
            pl.BlockSpec((1, length, BLK), lambda s, b: (s, 0, inside(b))),
            pl.BlockSpec((1, 1, NSTATE, BLK), lambda s, b: (s, inside(b) // PARTS, 0, inside(b) % PARTS)),
            pl.BlockSpec((1, 1, NSTATE, BLK), lambda s, b: (s, inside(b) // PARTS, 0, inside(b) % PARTS)),
            pl.BlockSpec((1, length, LANES), lambda s, b: (s, 0, 0)),
            pl.BlockSpec((1, length, LANES), lambda s, b: (s, 0, 0)),
            pl.BlockSpec((1, length, BLK), lambda s, b: (s, 0, 0)),
            pl.BlockSpec(memory_space=pl.ANY),
        ],
        out_specs=[
            pl.BlockSpec((1, length, BLK), lambda s, b: (s, 0, NB + b)),
            pl.BlockSpec((1, 8, BLK), lambda s, b: (s, 0, upto(b))),
            pl.BlockSpec((1, 8, BLK), lambda s, b: (s, 0, upto(b))),
            pl.BlockSpec((1, 8, LANES), lambda s, b: (s, 0, 0)),
        ],
        out_shape=[
            jax.ShapeDtypeStruct((SLOTS, length, WIDE), bf16),
            jax.ShapeDtypeStruct((SLOTS, 8, CONVCH), f32),
            jax.ShapeDtypeStruct((SLOTS, 8, CONVCH), f32),
            jax.ShapeDtypeStruct((SLOTS, 8, LANES), f32),
        ],
        input_output_aliases={15: 0},
        scratch_shapes=[
            pltpu.VMEM((length + 8, BLK), f32),
            pltpu.VMEM((length, length), f32),
            pltpu.VMEM((length, length), f32),
            pltpu.VMEM((LANES, length), f32),
            pltpu.VMEM((length + 16, BLK), f32),
            pltpu.VMEM((length, 2 * NSTATE), f32),
            pltpu.VMEM((length, LANES), f32),
            pltpu.VMEM((length, LANES), f32),
            pltpu.VMEM((LANES, length), f32),
            pltpu.VMEM((8, LANES), f32),
        ],
        compiler_params=params(),
        cost_estimate=pl.CostEstimate(flops=2 * 10**10, bytes_accessed=2 * 10**7, transcendentals=10**7),
    )(proj, edge, taps, proj, edge, taps, raw, heads, skip_row, dy, state, later, cum, size, act, grads)


def unproject_kernel(
    grads_ref, late_ref, w_ref, normed_ref, h_ref, g_ref, gain_ref,
    out_ref, gain_out_ref, w_out_ref,
    total, turned, mended,
):
    step = pl.program_id(0)
    rows = h_ref.shape[0]
    length = rows // SLOTS

    @pl.when(step == 0)
    def _():
        total[...] = jnp.zeros_like(total)
        turned[...] = normed_ref[...].T

    mended[...] = grads_ref[...]
    for slot in range(SLOTS):
        span = slice((slot + 1) * length - 16, (slot + 1) * length)
        extra = jnp.concatenate([jnp.zeros((8, COLS), f32), late_ref[slot]], axis=0)
        mended[span, :] = (grads_ref[span, :].astype(f32) + extra).astype(bf16)
    w_out_ref[...] = dot(turned[...], mended[...]).astype(bf16)
    total[...] += dot_nt(mended[...], w_ref[...])

    @pl.when(step == pl.num_programs(0) - 1)
    def _():
        gain_out_ref[...] = jnp.zeros_like(gain_out_ref)

        def one(span):
            h = h_ref[span, :]
            inverse = lax.rsqrt(jnp.mean(h * h, axis=-1, keepdims=True) + epsilon)
            back = total[span, :]
            unit = h * inverse
            gain_out_ref[0:1, :] += jnp.sum(back * unit, axis=0, keepdims=True)
            wanted = back * gain_ref[...]
            mean = jnp.mean(unit * wanted, axis=-1, keepdims=True)
            out_ref[span, :] = g_ref[span, :] + inverse * (wanted - unit * mean)

        for_rows(rows, 32, one)


def unproject(grads, late, weight, normed, h, g, gain_row):
    rows = h.shape[0]
    return pl.pallas_call(
        unproject_kernel,
        name="unproject",
        grid=(WIDE // COLS,),
        in_specs=[
            pl.BlockSpec((rows, COLS), lambda n: (0, n)),
            pl.BlockSpec((SLOTS, 8, COLS), lambda n: (0, 0, n)),
            pl.BlockSpec((D, COLS), lambda n: (0, n)),
            pl.BlockSpec((rows, D), lambda n: (0, 0)),
            pl.BlockSpec((rows, D), lambda n: (0, 0)),
            pl.BlockSpec((rows, D), lambda n: (0, 0)),
            pl.BlockSpec((1, D), lambda n: (0, 0)),
        ],
        out_specs=[
            pl.BlockSpec((rows, D), lambda n: (0, 0)),
            pl.BlockSpec((8, D), lambda n: (0, 0)),
            pl.BlockSpec((D, COLS), lambda n: (0, n)),
        ],
        out_shape=[
            jax.ShapeDtypeStruct((rows, D), f32),
            jax.ShapeDtypeStruct((8, D), f32),
            jax.ShapeDtypeStruct((D, WIDE), bf16),
        ],
        scratch_shapes=[
            pltpu.VMEM((rows, D), f32),
            pltpu.VMEM((D, rows), bf16),
            pltpu.VMEM((rows, COLS), bf16),
        ],
        compiler_params=params(),
        cost_estimate=pl.CostEstimate(
            flops=4 * rows * D * WIDE, bytes_accessed=4 * D * WIDE, transcendentals=0
        ),
    )(grads, late, weight, normed, h, g, gain_row)


MESH = pl.DeviceIdType.MESH
DP_BITS = {"core": 1, "x": 2, "y": 4}
STEPS = ("z1", "z2", "x", "y", "core")


def place():
    dp, z = lax.axis_index("dp"), lax.axis_index("seq")
    return {"y": dp // 4, "x": lax.rem(dp // 2, 2), "core": lax.rem(dp, 2), "z": z, "dp": dp}


def partner(here, step):
    if step == "z1":
        return (here["dp"], here["z"] + 1 - 2 * lax.rem(here["z"], 2))
    if step == "z2":
        return (here["dp"], here["z"] + 2 - 4 * (here["z"] // 2))
    return (here["dp"] + DP_BITS[step] * (1 - 2 * here[step]), here["z"])


def greet(here):
    barrier = pltpu.get_barrier_semaphore()
    for step in STEPS:
        pl.semaphore_signal(barrier, inc=1, device_id=partner(here, step), device_id_type=MESH)
    pl.semaphore_wait(barrier, len(STEPS))


def pieces_of(shapes, split):
    jobs = []
    for index, (rows, columns) in enumerate(shapes):
        parts, colours = split[index]
        height, width = rows // parts, columns // colours
        for part in range(parts):
            for colour in range(colours):
                jobs.append((index, part, colour, part * height, height, colour * width, width))
    waves = []
    for job in jobs:
        if job[2] == 0:
            waves.append([])
        waves[-1].append(job)
    return jobs, waves


def gather_kernel(shapes, split, *refs):
    count = len(shapes)
    shards, wholes = refs[:count], refs[count : 2 * count]
    local_sems, send_sems, recv_sems = refs[2 * count :]
    here = place()
    greet(here)
    jobs, waves = pieces_of(shapes, split)
    own = [
        pltpu.make_async_copy(
            shards[i], wholes[i].at[here["y"], here["x"], here["core"], here["z"]], local_sems.at[i]
        )
        for i in range(count)
    ]
    for copy in own:
        copy.start()

    def make(job, stage):
        index, _, colour, top, height, left, width = job
        order = ("z1", "z2", "x", "y", "core") if colour == 0 else ("z1", "z2", "y", "x", "core")
        done = order[:stage]
        axis = lambda name: slice(None) if name in done else here[name]
        depth = here["z"]
        if "z2" in done:
            depth = slice(None)
        elif "z1" in done:
            depth = pl.ds(here["z"] // 2 * 2, 2)
        rows, columns = pl.ds(top, height), pl.ds(left, width)
        target = wholes[index].at[axis("y"), axis("x"), axis("core"), depth, rows, columns]
        source = shards[index].at[rows, columns] if stage == 0 else target
        number = jobs.index(job)
        return pltpu.make_async_remote_copy(
            src_ref=source,
            dst_ref=target,
            send_sem=send_sems.at[number, stage],
            recv_sem=recv_sems.at[number, stage],
            device_id=partner(here, order[stage]),
            device_id_type=MESH,
        )

    stages = len(STEPS)
    for tick in range(len(waves) + stages):
        if tick == 1:
            for copy in own:
                copy.wait()
        for stage in reversed(range(stages + 1)):
            wave = tick - stage
            if not 0 <= wave < len(waves):
                continue
            for job in waves[wave]:
                if stage:
                    make(job, stage - 1).wait()
                if stage < stages:
                    make(job, stage).start()


def gather(shards, split, identity):
    shapes = tuple(shard.shape for shard in shards)
    jobs, _ = pieces_of(shapes, split)
    count = len(shards)
    wholes = pl.pallas_call(
        functools.partial(gather_kernel, shapes, split),
        name="gather",
        in_specs=[pl.BlockSpec(memory_space=pl.ANY)] * count,
        out_specs=[pl.BlockSpec(memory_space=pl.ANY)] * count,
        out_shape=[jax.ShapeDtypeStruct((2, 2, 2, 4) + s.shape, s.dtype) for s in shards],
        scratch_shapes=[
            pltpu.SemaphoreType.DMA((count,)),
            pltpu.SemaphoreType.DMA((len(jobs), len(STEPS))),
            pltpu.SemaphoreType.DMA((len(jobs), len(STEPS))),
        ],
        compiler_params=params(collective_id=identity, has_side_effects=True),
    )(*shards)
    return [whole.reshape((-1,) + whole.shape[4:]) for whole in wholes]


def reduce_kernel(shapes, split, *refs):
    count = len(shapes)
    jobs, waves = pieces_of(shapes, split)
    number = len(jobs)
    partials, heads_in = refs[:count], refs[count]
    totals, heads_out = refs[count + 1 : 2 * count + 1], refs[2 * count + 1]
    rest = refs[2 * count + 2 :]
    kept = rest[:number]
    landed = rest[number : 6 * number]
    heads_landed, local_sems, send_sems, recv_sems, head_send, head_recv = rest[6 * number :]
    here = place()
    greet(here)
    y, x, core, z = here["y"], here["x"], here["core"], here["z"]
    half, odd = z // 2, lax.rem(z, 2)
    stages = len(STEPS)

    def order(job):
        return ("core", "y", "x", "z2", "z1") if job[2] == 0 else ("core", "x", "y", "z2", "z1")

    def area(job, stage, mine):
        pick = lambda value: value if mine else 1 - value
        if stage == 1:
            return (pick(y), slice(None), slice(None)) if job[2] == 0 else (slice(None), pick(x), slice(None))
        if stage == 2:
            return (y, pick(x), slice(None)) if job[2] == 0 else (pick(y), x, slice(None))
        if stage == 3:
            return (y, x, pl.ds(pick(half) * 2, 2))
        return (y, x, half * 2 + pick(odd))

    def load(job):
        index, _, _, top, height, left, width = job
        place_in = partials[index].at[:, :, core, :, pl.ds(top, height), pl.ds(left, width)]
        k = jobs.index(job)
        return pltpu.make_async_copy(place_in, kept[k], local_sems.at[k])

    def make(job, stage):
        index, _, _, top, height, left, width = job
        k = jobs.index(job)
        if stage == 0:
            source = partials[index].at[:, :, 1 - core, :, pl.ds(top, height), pl.ds(left, width)]
        else:
            source = kept[k].at[area(job, stage, False)]
        return pltpu.make_async_remote_copy(
            src_ref=source,
            dst_ref=landed[stage * number + k],
            send_sem=send_sems.at[k, stage],
            recv_sem=recv_sems.at[k, stage],
            device_id=partner(here, order(job)[stage]),
            device_id_type=MESH,
        )

    def add(job, stage, mine):
        k = jobs.index(job)
        into, came = kept[k], landed[(stage - 1) * number + k]
        pick = lambda value: value if mine else 1 - value
        first = job[2] == 0

        def accumulate(target, source):
            into[target] = (into[target].astype(f32) + came[source].astype(f32)).astype(into.dtype)

        if stage == 1:
            def one(i, carry):
                a, b = i // 4, lax.rem(i, 4)
                where = (pick(y), a, b) if first else (a, pick(x), b)
                accumulate(where, where)
                return carry

            lax.fori_loop(0, 8, one, 0)
        elif stage == 2:
            def one(b, carry):
                if first:
                    accumulate((y, pick(x), b), (pick(x), b))
                else:
                    accumulate((pick(y), x, b), (pick(y), b))
                return carry

            lax.fori_loop(0, 4, one, 0)
        elif stage == 3:
            for b in range(2):
                accumulate((y, x, pick(half) * 2 + b), (pick(half) * 2 + b,))
        else:
            accumulate((y, x, half * 2 + pick(odd)), (pick(odd),))

    def finish(job):
        index, _, _, top, height, left, width = job
        k = jobs.index(job)
        summed = kept[k][y, x, z].astype(f32) + landed[4 * number + k][...].astype(f32)
        totals[index][top : top + height, left : left + width] = summed

    def heads_copy(stage):
        return pltpu.make_async_remote_copy(
            src_ref=heads_out,
            dst_ref=heads_landed.at[stage],
            send_sem=head_send.at[stage],
            recv_sem=head_recv.at[stage],
            device_id=partner(here, STEPS[stage]),
            device_id_type=MESH,
        )

    heads_out[...] = heads_in[...]
    for tick in range(len(waves) + stages):
        if tick < stages:
            heads_copy(tick).start()
        for stage in reversed(range(stages + 1)):
            wave = tick - stage
            if not 0 <= wave < len(waves):
                continue
            for job in waves[wave]:
                if stage == 0:
                    make(job, 0).start()
                    load(job).start()
                    continue
                if stage == 1:
                    load(job).wait()
                make(job, stage - 1).wait()
                if stage == stages:
                    finish(job)
                else:
                    add(job, stage, False)
                    make(job, stage).start()
                    add(job, stage, True)
        if tick < stages:
            heads_copy(tick).wait()
            heads_out[...] = heads_out[...] + heads_landed[tick]


def reduce(partials, heads, split, identity):
    shapes = tuple(partial.shape[1:] for partial in partials)
    jobs, _ = pieces_of(shapes, split)
    count = len(partials)
    kept, landed = [], [[] for _ in range(5)]
    for index, _, colour, _, height, _, width in jobs:
        kind = partials[index].dtype
        kept.append(pltpu.VMEM((2, 2, 4, height, width), kind))
        for stage, lead in enumerate(((2, 2, 4), (2, 4), (4,), (2,), ())):
            landed[stage].append(pltpu.VMEM(lead + (height, width), kind))
    tile = pltpu.SemaphoreType.DMA((len(jobs), 5))
    return pl.pallas_call(
        functools.partial(reduce_kernel, shapes, split),
        name="reduce",
        in_specs=[pl.BlockSpec(memory_space=pl.ANY)] * count + [pl.BlockSpec(memory_space=pltpu.VMEM)],
        out_specs=[pl.BlockSpec(memory_space=pltpu.VMEM)] * (count + 1),
        out_shape=[jax.ShapeDtypeStruct(s, f32) for s in shapes] + [jax.ShapeDtypeStruct(heads.shape, f32)],
        scratch_shapes=kept
        + sum(landed, [])
        + [
            pltpu.VMEM((5,) + heads.shape, f32),
            pltpu.SemaphoreType.DMA((len(jobs),)),
            tile,
            tile,
            pltpu.SemaphoreType.DMA((5,)),
            pltpu.SemaphoreType.DMA((5,)),
        ],
        compiler_params=params(collective_id=identity, has_side_effects=True),
    )(*[partial.reshape((2, 2, 2, 4) + partial.shape[1:]) for partial in partials], heads)


def chain_kernel(steps, last, local_ref, decay_ref, state_ref, send_ref, send_sems, recv_sems):
    dp, me = lax.axis_index("dp"), lax.axis_index("seq")
    slots = local_ref.shape[0]
    receives = me > 0 if steps > 0 else me < last
    sends = me < last if steps > 0 else me > 0
    barrier = pltpu.get_barrier_semaphore()

    @pl.when(receives)
    def _():
        pl.semaphore_signal(barrier, inc=1, device_id=(dp, me - steps), device_id_type=MESH)

    @pl.when(sends)
    def _():
        pl.semaphore_wait(barrier, 1)

    def make(slot, part):
        columns = pl.ds(part * CHAIN, CHAIN)
        return pltpu.make_async_remote_copy(
            src_ref=send_ref.at[slot, part],
            dst_ref=state_ref.at[slot, part],
            send_sem=send_sems.at[slot, part],
            recv_sem=recv_sems.at[slot, part],
            device_id=(dp, me + steps),
            device_id_type=MESH,
        )

    parts = [(slot, part) for slot in range(slots) for part in range(INNER // CHAIN)]

    @pl.when(jnp.logical_not(receives))
    def _():
        state_ref[...] = jnp.zeros_like(state_ref)

    for slot, part in parts:
        @pl.when(receives)
        def _():
            make(slot, part).wait_recv()

        @pl.when(sends)
        def _():
            decay = decay_ref[slot, 0:1, part * CHAIN : (part + 1) * CHAIN]
            local = local_ref[slot, :, part * CHAIN : (part + 1) * CHAIN]
            send_ref[slot, part] = (decay * state_ref[slot, part].astype(f32) + local).astype(bf16)
            make(slot, part).start()

    for slot, part in parts:
        @pl.when(sends)
        def _():
            make(slot, part).wait_send()


def chained(local, decay, steps, identity):
    slots = local.shape[0]
    parts = INNER // CHAIN
    shape = (slots, parts, NSTATE, CHAIN)
    return pl.pallas_call(
        functools.partial(chain_kernel, steps, lax.axis_size("seq") - 1),
        name="chain",
        in_specs=[pl.BlockSpec(memory_space=pltpu.VMEM)] * 2,
        out_specs=pl.BlockSpec(memory_space=pltpu.VMEM),
        out_shape=jax.ShapeDtypeStruct(shape, bf16),
        scratch_shapes=[
            pltpu.VMEM(shape, bf16),
            pltpu.SemaphoreType.DMA((slots, parts)),
            pltpu.SemaphoreType.DMA((slots, parts)),
        ],
        compiler_params=params(collective_id=identity, has_side_effects=True),
    )(local, decay)


def passed_along(value, steps):
    count = lax.axis_size("seq")
    initial, last = (max(0, -steps), min(count, count - steps))
    return lax.ppermute(value, "seq", [(source, source + steps) for source in range(initial, last)])


def all_slots(state):
    missing = SLOTS - state.shape[0]
    if missing:
        state = jnp.concatenate([state, jnp.zeros((missing,) + state.shape[1:], state.dtype)], axis=0)
    return state


def padded_rows(array, rows):
    return jnp.pad(array, ((0, rows - array.shape[0]), (0, 0)))


def pack_small(norm_gain, conv_weight, gate_gain):
    pieces = [norm_gain, conv_weight.reshape(LAYERS, -1), gate_gain]
    flat = jnp.concatenate(pieces, axis=1).reshape(-1)
    size = flat.shape[0]
    tiles = -(-size // (16 * LANES)) * 16
    return jnp.pad(flat, (0, tiles * LANES - size)).reshape(tiles, LANES)


def unpack_small(everything, norm_gain, conv_weight, gate_gain):
    count = everything.shape[0]
    size = LAYERS * (norm_gain.shape[1] + conv_weight.shape[1] * conv_weight.shape[2] + gate_gain.shape[1])
    everything = everything.reshape(count, -1)[:, :size].reshape(count, LAYERS, -1)
    everything = jnp.swapaxes(everything, 0, 1).astype(f32)
    first = norm_gain.shape[1]
    second = first + conv_weight.shape[1] * conv_weight.shape[2]
    norm = everything[..., :first].reshape(LAYERS, -1)
    conv = everything[..., first:second].reshape(LAYERS, count, CONV, -1)
    conv = jnp.swapaxes(conv, 1, 2).reshape(LAYERS, CONV, -1)
    gate = everything[..., second:].reshape(LAYERS, -1)
    return norm, conv, gate


def share_small(norm, conv, gate):
    count = lax.axis_size("dp") * lax.axis_size("seq")
    conv = jnp.swapaxes(conv.reshape(LAYERS, CONV, count, -1), 1, 2).reshape(LAYERS, count, -1)
    pieces = [norm.reshape(LAYERS, count, -1), conv, gate.reshape(LAYERS, count, -1)]
    flat = jnp.swapaxes(jnp.concatenate(pieces, axis=-1), 0, 1).reshape(count, -1)
    size = flat.shape[1]
    tiles = -(-size // (16 * LANES)) * 16
    return jnp.pad(flat, ((0, 0), (0, tiles * LANES - size))).reshape(count, tiles, LANES)


def own_small(mine, norm_gain, conv_weight, gate_gain):
    first = norm_gain.shape[1]
    second = first + conv_weight.shape[1] * conv_weight.shape[2]
    width = second + gate_gain.shape[1]
    mine = mine.reshape(-1)[: LAYERS * width].reshape(LAYERS, width)
    return mine[:, :first], mine[:, first:second].reshape(LAYERS, CONV, -1), mine[:, second:]


def body(
    hidden,
    out_grad,
    lengths,
    norm_gain,
    in_proj,
    conv_weight,
    gate_gain,
    out_proj,
    dt_bias,
    a_log,
    d_skip,
):
    length = hidden.shape[1]
    rows = SLOTS * length
    count = 1 if length >= SHORT else SLOTS
    swap = lengths[0] < lengths[1]

    def ordered(array):
        return jnp.where(swap, array[::-1], array)

    positions = lax.axis_index("seq") * length + jnp.arange(length, dtype=jnp.int32)
    valid = (positions[None, :] < ordered(lengths)[:, None]).astype(f32).reshape(rows, 1)
    valid = jnp.broadcast_to(valid, (rows, LANES))
    wide_in = jnp.pad(in_proj, ((0, 0), (0, 0), (0, WIDE - PROJ)))
    small_mesh = lax.axis_size("dp") == 8 and lax.axis_size("seq") == 4
    packed = pack_small(norm_gain, conv_weight, gate_gain)
    if small_mesh:
        shards, split = [packed], [(1, 1)]
        for layer in range(LAYERS):
            shards += [wide_in[layer], out_proj[layer]]
            split += [(3, 2), (3, 2)]
        everything, *wholes = gather(shards, split, 2 * LAYERS)
        wholes = [whole.reshape(-1, whole.shape[-1]) for whole in wholes]
    else:
        everything = lax.all_gather(packed, ("dp", "seq"), axis=0, tiled=False)
        wholes = [
            lax.all_gather(shard, ("dp", "seq"), axis=0, tiled=True)
            for layer in range(LAYERS)
            for shard in (wide_in[layer], out_proj[layer])
        ]
    weights_in, weights_out = wholes[0::2], wholes[1::2]
    norm_all, conv_all, gate_all = unpack_small(everything, norm_gain, conv_weight, gate_gain)
    h = ordered(hidden).reshape(rows, D)
    kept = []
    for layer in range(LAYERS):
        gain_row = norm_all[layer].reshape(1, D)
        gate_row = gate_all[layer].reshape(1, INNER)
        taps = padded_rows(conv_all[layer], 8)
        heads = padded_rows(
            jnp.pad(
                jnp.stack([dt_bias[layer], a_log[layer]]), ((0, 0), (0, LANES - HEADS))
            ),
            8,
        )
        skip_row = jnp.repeat(d_skip[layer], HEADDIM).reshape(1, INNER)
        proj, raw, normed = project(h, gain_row, weights_in[layer])
        cube = proj.reshape(SLOTS, length, WIDE)
        raw = raw.reshape(SLOTS, length, LANES)
        edge = passed_along(cube[:, length - (CONV - 1) :, INNER : INNER + CONVCH], 1)
        edge = jnp.pad(edge.astype(f32), ((0, 0), (8 - (CONV - 1), 0), (0, 0)))
        y, local, cum, size, act, decay = mix(cube, edge, taps, raw, heads, skip_row)
        state = chained(local[:count], decay[:count], 1, layer)
        flat = lambda array: array.reshape(rows, -1)
        h_next, mixture, inverse = branch(
            flat(y), proj, flat(act), flat(cum), state, gate_row, weights_out[layer], h, valid
        )
        kept.append(
            (h, gain_row, gate_row, taps, heads, skip_row, proj, raw, normed, edge, cum, size, act,
             decay, state, mixture, inverse)
        )
        h = h_next
    result = ordered(h.reshape(SLOTS, length, D))

    g = ordered(out_grad).reshape(rows, D)
    small = [None] * LAYERS
    partials = [None] * LAYERS
    for layer in reversed(range(LAYERS)):
        (h, gain_row, gate_row, taps, heads, skip_row, proj, raw, normed, edge, cum, size, act,
         decay, state, mixture, inverse) = kept[layer]
        cube = proj.reshape(SLOTS, length, WIDE)
        flat = lambda array: array.reshape(rows, -1)
        back, mean, grad_gate, partial_out = unbranch(
            g, valid, mixture, proj, inverse, gate_row, weights_out[layer]
        )
        dy, grads, local = ungate(
            back, mixture, proj, inverse, mean, gate_row, flat(act), flat(cum), count
        )
        later = chained(local, decay[:count], -1, LAYERS + layer)
        shaped = lambda array: array.reshape(SLOTS, length, -1)
        grads, edge_grad, grad_taps, grad_heads = unmix(
            cube, edge, taps, raw, heads, skip_row, shaped(dy), all_slots(state), all_slots(later),
            cum, size, act, shaped(grads),
        )
        late = passed_along(edge_grad[:, 8 - (CONV - 1) :].astype(bf16), -1).astype(f32)
        late = jnp.pad(late, ((0, 0), (8 - (CONV - 1), 0), (INNER, WIDE - INNER - CONVCH)))
        g, grad_norm, partial_in = unproject(
            flat(grads), late, weights_in[layer], normed, h, g, gain_row
        )
        small[layer] = (
            grad_norm[0], jnp.sum(grad_taps, axis=0)[:CONV], grad_gate[0],
            jnp.sum(grad_heads, axis=0)[:3, :HEADS],
        )
        partials[layer] = (partial_in, partial_out)
    grad_hidden = ordered(g.reshape(SLOTS, length, D))
    stacked = [jnp.stack([small[layer][member] for layer in range(LAYERS)]) for member in range(4)]
    shares = share_small(*stacked[:3])
    head_sums = jnp.pad(stacked[3].reshape(-1, HEADS), ((0, 8 - 3 * LAYERS), (0, LANES - HEADS)))
    grads_in, grads_out = [None] * LAYERS, [None] * LAYERS
    if small_mesh:
        cut = lambda partial: partial.reshape(lax.axis_size("dp") * lax.axis_size("seq"), -1, partial.shape[-1])
        for layer in reversed(range(LAYERS)):
            sent, split = [cut(partial) for partial in partials[layer]], [(3, 2), (3, 2)]
            if layer == 0:
                sent, split = sent + [shares], split + [(1, 1)]
            grads_in[layer], grads_out[layer], *others = reduce(sent, head_sums, split, 2 * LAYERS + 1 + layer)
        mine, head_sums = others
    else:
        for layer in range(LAYERS):
            grads_in[layer], grads_out[layer] = [
                lax.psum_scatter(partial, ("dp", "seq"), scatter_dimension=0, tiled=True)
                for partial in partials[layer]
            ]
        mine = lax.psum_scatter(shares, ("dp", "seq"), scatter_dimension=0, tiled=True)
        head_sums = lax.psum(head_sums, ("dp", "seq"))
    grad_norm, grad_conv, grad_gate = own_small(mine, norm_gain, conv_weight, gate_gain)
    grad_heads = head_sums[: 3 * LAYERS, :HEADS].reshape(LAYERS, 3, HEADS)
    return (
        result,
        grad_hidden,
        grad_norm,
        jnp.stack(grads_in)[..., :PROJ].astype(f32),
        grad_conv,
        grad_gate,
        jnp.stack(grads_out).astype(f32),
        grad_heads[:, 0],
        grad_heads[:, 1],
        grad_heads[:, 2],
    )


def solution(mesh):
    tokens = P("dp", "seq", None)
    every = ("dp", "seq")
    weights = (P(None, every), P(None, every, None), P(None, None, every), P(None, every), P(None, every, None))
    return jax.shard_map(
        body,
        mesh=mesh,
        in_specs=(tokens, tokens, P("dp")) + weights + (P(), P(), P()),
        out_specs=(tokens, tokens) + weights + (P(), P(), P()),
        check_vma=False,
    )
```

```python
import functools

import jax
import jax.numpy as jnp
from jax import lax
from jax.experimental import pallas as pl
from jax.experimental.pallas import tpu as pltpu
from jax.sharding import PartitionSpec as P

D = 1536
HEADS = 48
HEADDIM = 64
NSTATE = 128
CONV = 4
LAYERS = 2
INNER = 3072
CONVCH = 3328
PROJ = 6448
SLOTS = 2
SHORT = 256

LANES = 128
TAIL = 3584
BLK = 256
NB = INNER // BLK
COLS = 512
PER = BLK // HEADDIM
CHAIN = 512
PARTS = CHAIN // BLK

f32 = jnp.float32
bf16 = jnp.bfloat16
epsilon = 1e-05
VMEM_LIMIT = 58 << 20


def launch(
    kernel, name, grid, in_specs, out_specs, out_shape, args, scratch=(), cost=None, carry=None, identity=None,
    along=False, remote=False,
):
    options = {"compiler_params": params()}
    if cost is not None:
        options["cost_estimate"] = pl.CostEstimate(flops=cost[0], bytes_accessed=cost[1], transcendentals=cost[2])
    if carry is not None or remote:
        options["compiler_params"] = params(collective_id=identity, has_side_effects=True)
    if carry is None:
        return pl.pallas_call(
            kernel, name=name, grid=grid, in_specs=in_specs, out_specs=out_specs, out_shape=out_shape,
            scratch_shapes=list(scratch), **options,
        )(*args)
    sizes = [len(in_specs), len(carry.in_specs), len(out_specs), len(carry.out_specs), len(scratch)]
    if carry.aliases:
        options["input_output_aliases"] = {sizes[0] + i: sizes[2] + o for i, o in carry.aliases.items()}

    def wrapped(*refs):
        groups, at = [], 0
        for size in sizes:
            groups.append(refs[at : at + size])
            at += size
        step, total = 0, 1
        for axis, extent in enumerate(grid):
            step, total = step * extent + pl.program_id(axis), total * extent
        ticks = carry.ticks(groups[1], groups[3], refs[at:], along)
        plan = {}
        for number, tick in enumerate(ticks[:-1]):
            plan.setdefault(number * total // (len(ticks) - 1), []).append(tick)
        for moment, members in plan.items():
            @pl.when(step == moment)
            def _(members=members):
                for member in members:
                    member()

        kernel(*groups[0], *groups[2], *groups[4])

        @pl.when(step == total - 1)
        def _():
            ticks[-1]()

    found = pl.pallas_call(
        wrapped, name=name, grid=grid, in_specs=list(in_specs) + carry.in_specs,
        out_specs=list(out_specs) + carry.out_specs, out_shape=list(out_shape) + carry.out_shape,
        scratch_shapes=list(scratch) + carry.scratch, **options,
    )(*args, *carry.args)
    return list(found[: sizes[2]]) + [carry.results(found[sizes[2] :])]


def params(**more):
    return pltpu.CompilerParams(vmem_limit_bytes=VMEM_LIMIT, **more)


def for_rows(total, size, function):
    def step(index, carry):
        function(pl.ds(pl.multiple_of(index * size, size), size))
        return carry

    lax.fori_loop(0, total // size, step, 0)


def dot(left, right):
    return jnp.dot(left, right, preferred_element_type=f32)


def dot_nt(left, right):
    return lax.dot_general(left, right, (((1,), (1,)), ((), ())), preferred_element_type=f32)


def dot_tn(left, right):
    return lax.dot_general(left, right, (((0,), (0,)), ((), ())), preferred_element_type=f32)


def dot_exact(left, right):
    return jnp.dot(left, right, preferred_element_type=f32, precision=lax.Precision.HIGHEST)


def halves(array):
    high = array.astype(bf16)
    return high, (array - high.astype(f32)).astype(bf16)


def dot_halves(left, right, product=dot):
    left_high, left_low = left
    right_high, right_low = right
    return product(left_high, right_high) + product(left_high, right_low) + product(left_low, right_high)


def dot_member(array, member):
    high, low = halves(array)
    return dot(high, member) + dot(low, member)


def sigmoid(vector):
    return 0.5 + 0.5 * jnp.tanh(0.5 * vector)


def softplus(vector):
    return jnp.maximum(vector, 0.0) + jnp.log1p(jnp.exp(-jnp.abs(vector)))


def spread(columns):
    length = columns.shape[0]
    return jnp.concatenate(
        [jnp.broadcast_to(columns[:, j : j + 1], (length, HEADDIM)) for j in range(PER)], axis=1
    )


def heads_first(columns, block):
    return pltpu.roll(columns, lax.rem(LANES - PER * block, LANES), 1)


def load_extended(scratch, edge_ref, rows_ref):
    scratch[0:8, :] = edge_ref[0]
    scratch[8:, :] = rows_ref[0]


def convolve(scratch, taps, length):
    total = taps[0:1] * scratch[5 : 5 + length, :]
    for k in range(1, CONV):
        total = total + taps[k : k + 1] * scratch[5 + k : 5 + k + length, :]
    return total


def lower(length):
    first = lax.broadcasted_iota(jnp.int32, (length, length), 0)
    second = lax.broadcasted_iota(jnp.int32, (length, length), 1)
    return first >= second


def project_kernel(h_ref, gain_ref, w_ref, proj_ref, raw_ref, normed_ref):
    step = pl.program_id(0)
    total = h_ref.shape[0]

    @pl.when(step == 0)
    def _():
        def one(rows):
            h = h_ref[rows, :]
            inverse = lax.rsqrt(jnp.mean(h * h, axis=-1, keepdims=True) + epsilon)
            normed_ref[rows, :] = (h * inverse * gain_ref[...]).astype(bf16)

        for_rows(total, 32, one)

    product = dot(normed_ref[...], w_ref[...])
    proj_ref[...] = product

    @pl.when(step == pl.num_programs(0) - 1)
    def _():
        raw_ref[...] = product[:, COLS - 2 * LANES : COLS - LANES]


def project(h, gain_row, weight, carry=None, identity=None):
    total = h.shape[0]
    return launch(
        project_kernel,
        "project",
        (TAIL // COLS,),
        [
            pl.BlockSpec((total, D), lambda n: (0, 0)),
            pl.BlockSpec((1, D), lambda n: (0, 0)),
            pl.BlockSpec((D, COLS), lambda n: (0, n)),
        ],
        [
            pl.BlockSpec((total, COLS), lambda n: (0, n)),
            pl.BlockSpec((total, LANES), lambda n: (0, 0)),
            pl.BlockSpec((total, D), lambda n: (0, 0)),
        ],
        [
            jax.ShapeDtypeStruct((total, TAIL), f32),
            jax.ShapeDtypeStruct((total, LANES), f32),
            jax.ShapeDtypeStruct((total, D), bf16),
        ],
        (h, gain_row, weight),
        cost=(2 * total * D * TAIL, 2 * D * TAIL, 0),
        carry=carry,
        identity=identity,
    )


def project_gate_kernel(normed_ref, w_ref, gate_ref):
    gate_ref[...] = dot(normed_ref[...], w_ref[...])


def project_gate(normed, weight, carry=None, identity=None):
    total = normed.shape[0]
    return launch(
        project_gate_kernel,
        "project_gate",
        (INNER // COLS,),
        [pl.BlockSpec((total, D), lambda n: (0, 0)), pl.BlockSpec((D, COLS), lambda n: (0, n))],
        [pl.BlockSpec((total, COLS), lambda n: (0, n))],
        [jax.ShapeDtypeStruct((total, INNER), f32)],
        (normed, weight),
        cost=(2 * total * D * INNER, 2 * D * INNER, 0),
        carry=carry,
        identity=identity,
    )


def mix_kernel(
    rows_ref, edge_ref, taps_ref, maps_ref, maps_edge_ref, maps_taps_ref, raw_ref, heads_ref, skip_ref,
    y_ref, state_ref, cum_ref, step_ref, act_ref, decay_ref,
    extended, inner, cum_t, input_t,
):
    block = pl.program_id(1)
    length = rows_ref.shape[1]

    @pl.when(block == 0)
    def _():
        load_extended(extended, maps_edge_ref, maps_ref)
        convolved = convolve(extended, maps_taps_ref[...], length)
        maps = convolved * sigmoid(convolved)
        act_ref[0] = maps
        products = dot_halves(halves(maps[:, NSTATE:]), halves(maps[:, :NSTATE]), dot_nt)
        input_t[0], input_t[1] = halves(maps[:, :NSTATE].T)
        causal = lower(length)
        inner[...] = jnp.where(causal, products, 0.0)
        size = softplus(raw_ref[0] + heads_ref[0:1, :])
        decay = -size * jnp.exp(heads_ref[1:2, :])
        cum = dot_exact(causal.astype(f32), decay)
        cum_ref[0] = cum
        step_ref[0] = size
        cum_t[...] = cum.T

    load_extended(extended, edge_ref, rows_ref)
    convolved = convolve(extended, taps_ref[...], length)
    values = convolved * sigmoid(convolved)
    cum = heads_first(cum_ref[0], block)
    stepped = values * spread(heads_first(step_ref[0], block))
    low = stepped.astype(bf16)
    parts = []
    for j in range(PER):
        row = cum_t[pl.ds(block * PER + j, 1), :]
        column = cum[:, j : j + 1]
        pieces = []
        for first in range(0, length, LANES):
            end = first + LANES
            decays = jnp.exp(jnp.minimum(column[first:end] - row[:, :end], 0.0))
            weights = (inner[first:end, :end] * decays).astype(bf16)
            pieces.append(dot(weights, low[:end, j * HEADDIM : (j + 1) * HEADDIM]))
        parts.append(jnp.concatenate(pieces, axis=0))
    y_ref[0] = jnp.concatenate(parts, axis=1) + skip_ref[...] * values
    final = cum[length - 1 :, :]
    remaining = jnp.exp(final - cum)
    state_ref[0] = dot_halves((input_t[0], input_t[1]), halves(stepped * spread(remaining)))
    decay_ref[0] = jnp.broadcast_to(spread(jnp.exp(final)), (8, BLK))


def mix(proj, edge, taps, raw, heads, skip_row, carry=None, identity=None):
    length = proj.shape[1]
    return launch(
        mix_kernel,
        "mix",
        (SLOTS, NB),
        [
            pl.BlockSpec((1, length, BLK), lambda s, b: (s, 0, b)),
            pl.BlockSpec((1, 8, BLK), lambda s, b: (s, 0, b)),
            pl.BlockSpec((8, BLK), lambda s, b: (0, b)),
            pl.BlockSpec((1, length, BLK), lambda s, b: (s, 0, NB)),
            pl.BlockSpec((1, 8, BLK), lambda s, b: (s, 0, NB)),
            pl.BlockSpec((8, BLK), lambda s, b: (0, NB)),
            pl.BlockSpec((1, length, LANES), lambda s, b: (s, 0, 0)),
            pl.BlockSpec((8, LANES), lambda s, b: (0, 0)),
            pl.BlockSpec((1, BLK), lambda s, b: (0, b)),
        ],
        [
            pl.BlockSpec((1, length, BLK), lambda s, b: (s, 0, b)),
            pl.BlockSpec((1, NSTATE, BLK), lambda s, b: (s, 0, b)),
            pl.BlockSpec((1, length, LANES), lambda s, b: (s, 0, 0)),
            pl.BlockSpec((1, length, LANES), lambda s, b: (s, 0, 0)),
            pl.BlockSpec((1, length, BLK), lambda s, b: (s, 0, 0)),
            pl.BlockSpec((1, 8, BLK), lambda s, b: (s, 0, b)),
        ],
        [
            jax.ShapeDtypeStruct((SLOTS, length, INNER), f32),
            jax.ShapeDtypeStruct((SLOTS, NSTATE, INNER), f32),
            jax.ShapeDtypeStruct((SLOTS, length, LANES), f32),
            jax.ShapeDtypeStruct((SLOTS, length, LANES), f32),
            jax.ShapeDtypeStruct((SLOTS, length, BLK), f32),
            jax.ShapeDtypeStruct((SLOTS, 8, INNER), f32),
        ],
        (proj, edge, taps, proj, edge, taps, raw, heads, skip_row),
        scratch=[
            pltpu.VMEM((length + 8, BLK), f32),
            pltpu.VMEM((length, length), f32),
            pltpu.VMEM((LANES, length), f32),
            pltpu.VMEM((2, NSTATE, length), bf16),
        ],
        cost=(6 * 10**9, 10**7, 10**7),
        carry=carry,
        identity=identity,
    )


def branch_kernel(
    y_ref, gate_ref, act_ref, cum_ref, state_ref, gain_ref, w_ref, h_ref, valid_ref,
    out_ref, mixture_ref, inverse_ref,
    total, squares, gated_low,
):
    block = pl.program_id(0)
    count = state_ref.shape[0]
    rows = y_ref.shape[0]
    length = rows // SLOTS

    @pl.when(block == 0)
    def _():
        total[...] = jnp.zeros_like(total)
        squares[...] = jnp.zeros_like(squares)

    for slot in range(SLOTS):
        span = slice(slot * length, (slot + 1) * length)
        mixture = y_ref[span, :]
        if slot < count:
            cum = heads_first(cum_ref[span, :], block)
            carried = dot_member(act_ref[span, NSTATE:], state_ref[slot, 0])
            mixture = mixture + carried * spread(jnp.exp(cum))
        gate = gate_ref[span, :]
        gated = mixture * gate * sigmoid(gate)
        mixture_ref[span, :] = mixture
        square = gated * gated
        squares[span, :] += square[:, :LANES] + square[:, LANES:]
        gated_low[span, :] = (gated * gain_ref[...]).astype(bf16)
    total[...] += dot(gated_low[...], w_ref[...])

    @pl.when(block == NB - 1)
    def _():
        def one(span):
            mean = jnp.sum(squares[span, :], axis=-1, keepdims=True) / INNER
            inverse = lax.rsqrt(mean + epsilon)
            inverse_ref[span, :] = jnp.broadcast_to(inverse, (32, LANES))
            factor = inverse * valid_ref[span, 0:1]
            out_ref[span, :] = h_ref[span, :] + factor * total[span, :]

        for_rows(rows, 32, one)


def branch(y, gate, act, cum, state, gain_row, weight, h, valid, carry=None, identity=None):
    rows = h.shape[0]
    count = state.shape[0]
    return launch(
        branch_kernel,
        "branch",
        (NB,),
        [
            pl.BlockSpec((rows, BLK), lambda b: (0, b)),
            pl.BlockSpec((rows, BLK), lambda b: (0, b)),
            pl.BlockSpec((rows, BLK), lambda b: (0, 0)),
            pl.BlockSpec((rows, LANES), lambda b: (0, 0)),
            pl.BlockSpec((count, 1, NSTATE, BLK), lambda b: (0, b // PARTS, 0, b % PARTS)),
            pl.BlockSpec((1, BLK), lambda b: (0, b)),
            pl.BlockSpec((BLK, D), lambda b: (b, 0)),
            pl.BlockSpec((rows, D), lambda b: (0, 0)),
            pl.BlockSpec((rows, LANES), lambda b: (0, 0)),
        ],
        [
            pl.BlockSpec((rows, D), lambda b: (0, 0)),
            pl.BlockSpec((rows, BLK), lambda b: (0, b)),
            pl.BlockSpec((rows, LANES), lambda b: (0, 0)),
        ],
        [
            jax.ShapeDtypeStruct((rows, D), f32),
            jax.ShapeDtypeStruct((rows, INNER), f32),
            jax.ShapeDtypeStruct((rows, LANES), f32),
        ],
        (y, gate, act, cum, state, gain_row, weight, h, valid),
        scratch=[
            pltpu.VMEM((rows, D), f32),
            pltpu.VMEM((rows, LANES), f32),
            pltpu.VMEM((rows, BLK), bf16),
        ],
        cost=(2 * rows * D * INNER, 2 * D * INNER, 10**6),
        carry=carry,
        identity=identity,
    )


def unbranch_kernel(
    g_ref, valid_ref, mixture_ref, gate_ref, inverse_ref, gain_ref, w_ref,
    back_ref, mean_ref, gain_out_ref, w_out_ref,
    low, norm_low,
):
    block = pl.program_id(0)
    rows = g_ref.shape[0]

    @pl.when(block == 0)
    def _():
        def one(span):
            low[span, :] = (valid_ref[span, 0:1] * g_ref[span, :]).astype(bf16)

        for_rows(rows, 32, one)
        mean_ref[...] = jnp.zeros_like(mean_ref)

    back_ref[...] = dot_nt(low[...], w_ref[...])
    gain_out_ref[...] = jnp.zeros_like(gain_out_ref)

    def one(span):
        gate = gate_ref[span, :]
        gated = mixture_ref[span, :] * gate * sigmoid(gate)
        back = back_ref[span, :]
        unit = gated * inverse_ref[span, 0:1]
        norm_low[span, :] = (unit * gain_ref[...]).astype(bf16)
        gain_out_ref[0:1, :] += jnp.sum(back * unit, axis=0, keepdims=True)
        product = gated * back * gain_ref[...]
        mean_ref[span, :] += product[:, :LANES] + product[:, LANES:]

    for_rows(rows, 128, one)
    w_out_ref[...] = dot_tn(norm_low[...], low[...]).astype(bf16)

    @pl.when(block == NB - 1)
    def _():
        mean_ref[...] = jnp.broadcast_to(
            jnp.sum(mean_ref[...], axis=-1, keepdims=True) / INNER, mean_ref.shape
        )


def unbranch(g, valid, mixture, gate, inverse, gain_row, weight, carry=None, identity=None):
    rows = g.shape[0]
    return launch(
        unbranch_kernel,
        "unbranch",
        (NB,),
        [
            pl.BlockSpec((rows, D), lambda b: (0, 0)),
            pl.BlockSpec((rows, LANES), lambda b: (0, 0)),
            pl.BlockSpec((rows, BLK), lambda b: (0, b)),
            pl.BlockSpec((rows, BLK), lambda b: (0, b)),
            pl.BlockSpec((rows, LANES), lambda b: (0, 0)),
            pl.BlockSpec((1, BLK), lambda b: (0, b)),
            pl.BlockSpec((BLK, D), lambda b: (b, 0)),
        ],
        [
            pl.BlockSpec((rows, BLK), lambda b: (0, b)),
            pl.BlockSpec((rows, LANES), lambda b: (0, 0)),
            pl.BlockSpec((8, BLK), lambda b: (0, b)),
            pl.BlockSpec((BLK, D), lambda b: (b, 0)),
        ],
        [
            jax.ShapeDtypeStruct((rows, INNER), f32),
            jax.ShapeDtypeStruct((rows, LANES), f32),
            jax.ShapeDtypeStruct((8, INNER), f32),
            jax.ShapeDtypeStruct((INNER, D), bf16),
        ],
        (g, valid, mixture, gate, inverse, gain_row, weight),
        scratch=[pltpu.VMEM((rows, D), bf16), pltpu.VMEM((rows, BLK), bf16)],
        cost=(4 * rows * D * INNER, 4 * D * INNER, 10**6),
        carry=carry,
        identity=identity,
    )


def ungate_kernel(
    back_ref, mixture_ref, gate_ref, inverse_ref, mean_ref, gain_ref, act_ref, cum_ref,
    dy_ref, dgate_ref, state_ref,
    output_t,
):
    block = pl.program_id(0)
    rows = back_ref.shape[0]
    length = rows // SLOTS

    @pl.when(block == 0)
    def _():
        for slot in range(state_ref.shape[0]):
            span = slice(slot * length, (slot + 1) * length)
            output_t[slot, 0], output_t[slot, 1] = halves(act_ref[span, NSTATE:].T)

    for slot in range(SLOTS):
        span = slice(slot * length, (slot + 1) * length)
        gate = gate_ref[span, :]
        curve = sigmoid(gate)
        mixture = mixture_ref[span, :]
        swish = gate * curve
        inverse = inverse_ref[span, 0:1]
        back = back_ref[span, :] * gain_ref[...]
        pull = inverse * inverse * inverse * mean_ref[span, 0:1]
        grad = inverse * back - (mixture * swish) * pull
        dy = grad * swish
        dy_ref[span, :] = dy
        dgate_ref[span, :] = (grad * mixture * curve * (1.0 + gate * (1.0 - curve))).astype(bf16)
        if slot < state_ref.shape[0]:
            grown = spread(jnp.exp(heads_first(cum_ref[span, :], block)))
            state_ref[slot] = dot_halves((output_t[slot, 0], output_t[slot, 1]), halves(dy * grown))


def ungate(back, mixture, gate, inverse, mean, gain_row, act, cum, count, carry=None, identity=None):
    rows = back.shape[0]
    length = rows // SLOTS
    return launch(
        ungate_kernel,
        "ungate",
        (NB,),
        [
            pl.BlockSpec((rows, BLK), lambda b: (0, b)),
            pl.BlockSpec((rows, BLK), lambda b: (0, b)),
            pl.BlockSpec((rows, BLK), lambda b: (0, b)),
            pl.BlockSpec((rows, LANES), lambda b: (0, 0)),
            pl.BlockSpec((rows, LANES), lambda b: (0, 0)),
            pl.BlockSpec((1, BLK), lambda b: (0, b)),
            pl.BlockSpec((rows, BLK), lambda b: (0, 0)),
            pl.BlockSpec((rows, LANES), lambda b: (0, 0)),
        ],
        [
            pl.BlockSpec((rows, BLK), lambda b: (0, b)),
            pl.BlockSpec((rows, BLK), lambda b: (0, b)),
            pl.BlockSpec((count, NSTATE, BLK), lambda b: (0, 0, b)),
        ],
        [
            jax.ShapeDtypeStruct((rows, INNER), f32),
            jax.ShapeDtypeStruct((rows, INNER), bf16),
            jax.ShapeDtypeStruct((count, NSTATE, INNER), f32),
        ],
        (back, mixture, gate, inverse, mean, gain_row, act, cum),
        scratch=[pltpu.VMEM((count, 2, NSTATE, length), bf16)],
        cost=(10**9, 2 * 10**7, 10**7),
        carry=carry,
        identity=identity,
    )


def unmix_kernel(
    rows_ref, edge_ref, taps_ref, maps_ref, maps_edge_ref, maps_taps_ref, raw_ref, heads_ref, skip_ref,
    dy_ref, state_ref, later_ref, cum_ref, step_ref, act_ref,
    grads_ref, edge_out_ref, taps_out_ref, heads_out_ref,
    extended, inner, d_inner, cum_t, grad_ext, d_maps, d_cum, d_step, over_rows, sums,
):
    block = pl.program_id(1)
    length = rows_ref.shape[1]
    count = state_ref.shape[0]

    def conv_back(gradient, taps):
        grad_ext[8 : 8 + length, :] = gradient
        back = taps[0:1] * grad_ext[3 : 3 + length + 8, :]
        for k in range(1, CONV):
            back = back + taps[k : k + 1] * grad_ext[3 - k : 3 - k + length + 8, :]
        edge_out_ref[0] = back[:8]
        grads_ref[0] = back[8:].astype(bf16)
        lines = [
            jnp.sum(gradient * extended[5 + k : 5 + k + length, :], axis=0, keepdims=True)
            for k in range(CONV)
        ]
        lines.append(jnp.zeros((8 - CONV, BLK), f32))
        taps_out_ref[0] = jnp.concatenate(lines, axis=0)

    @pl.when(block == 0)
    def _():
        grad_ext[0:8, :] = jnp.zeros((8, BLK), f32)
        grad_ext[8 + length :, :] = jnp.zeros((8, BLK), f32)
        maps = act_ref[0]
        products = dot_halves(halves(maps[:, :NSTATE]), halves(maps[:, NSTATE:]), dot_nt)
        inner[...] = jnp.where(lower(length).T, products, 0.0)
        cum_t[...] = cum_ref[0].T
        d_inner[...] = jnp.zeros_like(d_inner)
        d_maps[...] = jnp.zeros_like(d_maps)
        d_cum[...] = jnp.zeros_like(d_cum)
        d_step[...] = jnp.zeros_like(d_step)
        over_rows[...] = jnp.zeros_like(over_rows)
        sums[...] = jnp.zeros_like(sums)

    @pl.when(block < NB)
    def _():
        load_extended(extended, edge_ref, rows_ref)
        convolved = convolve(extended, taps_ref[...], length)
        curve = sigmoid(convolved)
        values = convolved * curve
        cum = heads_first(cum_ref[0], block)
        size = spread(heads_first(step_ref[0], block))
        stepped = values * size
        low = stepped.astype(bf16)
        dy = dy_ref[0]
        dy_low = dy.astype(bf16)
        lane = lax.broadcasted_iota(jnp.int32, (1, LANES), 1)
        parts = []
        for j in range(PER):
            head = block * PER + j
            row = cum_t[pl.ds(head, 1), :]
            column = cum[:, j : j + 1]
            dy_head = dy_low[:, j * HEADDIM : (j + 1) * HEADDIM]
            low_head = low[:, j * HEADDIM : (j + 1) * HEADDIM]
            pieces = []
            row_sums = []
            column_sums = None
            for first in range(0, length, LANES):
                end = first + LANES
                decays = jnp.exp(jnp.minimum(row[:, first:] - column[first:end], 0.0))
                products = inner[first:end, first:]
                weights = (products * decays).astype(bf16)
                grads = dot_nt(low_head[first:end], dy_head[first:]) * decays
                d_inner[first:end, first:] += grads
                pieces.append(dot(weights, dy_head[first:]))
                moved = grads * products
                row_sums.append(jnp.sum(moved, axis=1, keepdims=True))
                found = jnp.sum(moved, axis=0, keepdims=True)
                if first:
                    found = jnp.concatenate([jnp.zeros((1, first), f32), found], axis=1)
                column_sums = found if column_sums is None else column_sums + found
            parts.append(jnp.concatenate(pieces, axis=0))
            over_rows[pl.ds(head, 1), :] = column_sums
            d_cum[...] -= jnp.where(lane == head, jnp.concatenate(row_sums, axis=0), 0.0)
        d_stepped = jnp.concatenate(parts, axis=1)
        which = lax.broadcasted_iota(jnp.int32, (BLK, LANES), 0) // HEADDIM + block * PER
        chosen = which == lax.broadcasted_iota(jnp.int32, (BLK, LANES), 1)
        member = chosen.astype(f32)
        member_low = chosen.astype(bf16)
        state = state_ref[0, 0]
        later = later_ref[0, 0]
        maps = act_ref[0]
        remaining = spread(jnp.exp(cum[length - 1 :, :] - cum))
        grown = spread(jnp.exp(cum))
        from_later = dot_member(maps[:, :NSTATE], later) * remaining
        d_stepped = d_stepped + from_later
        left = stepped * remaining
        grown_dy = dy * grown
        used = stepped * from_later
        d_cum[...] += dot_member(grown_dy * dot_member(maps[:, NSTATE:], state) - used, member_low)
        d_maps[:, :NSTATE] += dot_nt(left.astype(bf16), later)
        d_maps[:, NSTATE:] += dot_nt(grown_dy.astype(bf16), state)
        d_step[...] += dot_member(d_stepped * values, member_low)
        lines = jnp.concatenate(
            [
                jnp.sum(used, axis=0, keepdims=True),
                jnp.sum(dy * values, axis=0, keepdims=True),
                jnp.sum(later.astype(f32) * state.astype(f32), axis=0, keepdims=True),
                jnp.zeros((5, BLK), f32),
            ],
            axis=0,
        )
        sums[...] += dot_exact(lines, member)
        d_values = d_stepped * size + skip_ref[...] * dy
        conv_back(d_values * curve * (1.0 + convolved * (1.0 - curve)), taps_ref[...])

    @pl.when(block == NB)
    def _():
        load_extended(extended, maps_edge_ref, maps_ref)
        convolved = convolve(extended, maps_taps_ref[...], length)
        curve = sigmoid(convolved)
        maps = act_ref[0]
        d_both = jnp.where(lower(length).T, d_inner[...], 0.0)
        d_input = d_maps[:, :NSTATE] + dot_halves(halves(d_both), halves(maps[:, NSTATE:]))
        d_output = d_maps[:, NSTATE:] + dot_halves(halves(d_both.T), halves(maps[:, :NSTATE]))
        d_both = jnp.concatenate([d_input, d_output], axis=1)
        conv_back(d_both * curve * (1.0 + convolved * (1.0 - curve)), maps_taps_ref[...])

    @pl.when(block == NB + 1)
    def _():
        final = cum_ref[0][length - 1 :, :]
        at_end = sums[0:1, :] + jnp.exp(final) * sums[2:3, :]
        d_total = d_cum[...] + over_rows[...].T
        position = lax.broadcasted_iota(jnp.int32, (length, 1), 0)
        d_total = d_total + jnp.where(position == length - 1, at_end, 0.0)
        d_decay = dot_exact(lower(length).T.astype(f32), d_total)
        rate = jnp.exp(heads_ref[1:2, :])
        size = step_ref[0]
        d_raw = (d_step[...] - d_decay * rate) * sigmoid(raw_ref[0] + heads_ref[0:1, :])
        grads_ref[0] = jnp.concatenate([d_raw, jnp.zeros_like(d_raw)], axis=1).astype(bf16)
        heads_out_ref[0] = jnp.concatenate(
            [
                jnp.sum(d_raw, axis=0, keepdims=True),
                jnp.sum(d_decay * (-size * rate), axis=0, keepdims=True),
                sums[1:2, :],
                jnp.zeros((5, LANES), f32),
            ],
            axis=0,
        )


def unmix(proj, edge, taps, raw, heads, skip_row, dy, state, later, cum, size, act, carry=None, identity=None):
    length = proj.shape[1]
    inside = lambda b: jnp.minimum(b, NB - 1)
    upto = lambda b: jnp.minimum(b, NB)
    return launch(
        unmix_kernel,
        "unmix",
        (SLOTS, NB + 2),
        [
            pl.BlockSpec((1, length, BLK), lambda s, b: (s, 0, inside(b))),
            pl.BlockSpec((1, 8, BLK), lambda s, b: (s, 0, inside(b))),
            pl.BlockSpec((8, BLK), lambda s, b: (0, inside(b))),
            pl.BlockSpec((1, length, BLK), lambda s, b: (s, 0, NB)),
            pl.BlockSpec((1, 8, BLK), lambda s, b: (s, 0, NB)),
            pl.BlockSpec((8, BLK), lambda s, b: (0, NB)),
            pl.BlockSpec((1, length, LANES), lambda s, b: (s, 0, 0)),
            pl.BlockSpec((8, LANES), lambda s, b: (0, 0)),
            pl.BlockSpec((1, BLK), lambda s, b: (0, inside(b))),
            pl.BlockSpec((1, length, BLK), lambda s, b: (s, 0, inside(b))),
            pl.BlockSpec((1, 1, NSTATE, BLK), lambda s, b: (s, inside(b) // PARTS, 0, inside(b) % PARTS)),
            pl.BlockSpec((1, 1, NSTATE, BLK), lambda s, b: (s, inside(b) // PARTS, 0, inside(b) % PARTS)),
            pl.BlockSpec((1, length, LANES), lambda s, b: (s, 0, 0)),
            pl.BlockSpec((1, length, LANES), lambda s, b: (s, 0, 0)),
            pl.BlockSpec((1, length, BLK), lambda s, b: (s, 0, 0)),
        ],
        [
            pl.BlockSpec((1, length, BLK), lambda s, b: (s, 0, b)),
            pl.BlockSpec((1, 8, BLK), lambda s, b: (s, 0, upto(b))),
            pl.BlockSpec((1, 8, BLK), lambda s, b: (s, 0, upto(b))),
            pl.BlockSpec((1, 8, LANES), lambda s, b: (s, 0, 0)),
        ],
        [
            jax.ShapeDtypeStruct((SLOTS, length, TAIL), bf16),
            jax.ShapeDtypeStruct((SLOTS, 8, CONVCH), f32),
            jax.ShapeDtypeStruct((SLOTS, 8, CONVCH), f32),
            jax.ShapeDtypeStruct((SLOTS, 8, LANES), f32),
        ],
        (proj, edge, taps, proj, edge, taps, raw, heads, skip_row, dy, state, later, cum, size, act),
        scratch=[
            pltpu.VMEM((length + 8, BLK), f32),
            pltpu.VMEM((length, length), f32),
            pltpu.VMEM((length, length), f32),
            pltpu.VMEM((LANES, length), f32),
            pltpu.VMEM((length + 16, BLK), f32),
            pltpu.VMEM((length, 2 * NSTATE), f32),
            pltpu.VMEM((length, LANES), f32),
            pltpu.VMEM((length, LANES), f32),
            pltpu.VMEM((LANES, length), f32),
            pltpu.VMEM((8, LANES), f32),
        ],
        cost=(2 * 10**10, 2 * 10**7, 10**7),
        carry=carry,
        identity=identity,
    )


def unproject_gate_kernel(grads_ref, w_ref, normed_ref, back_ref, w_out_ref, turned):
    step = pl.program_id(0)

    @pl.when(step == 0)
    def _():
        turned[...] = normed_ref[...].T

    w_out_ref[...] = dot(turned[...], grads_ref[...]).astype(bf16)
    product = dot_nt(grads_ref[...], w_ref[...])

    @pl.when(step == 0)
    def _():
        back_ref[...] = product

    @pl.when(step > 0)
    def _():
        back_ref[...] += product


def unproject_gate(grads, weight, normed, carry=None, identity=None):
    rows = normed.shape[0]
    return launch(
        unproject_gate_kernel,
        "unproject_gate",
        (INNER // COLS,),
        [
            pl.BlockSpec((rows, COLS), lambda n: (0, n)),
            pl.BlockSpec((D, COLS), lambda n: (0, n)),
            pl.BlockSpec((rows, D), lambda n: (0, 0)),
        ],
        [pl.BlockSpec((rows, D), lambda n: (0, 0)), pl.BlockSpec((D, COLS), lambda n: (0, n))],
        [jax.ShapeDtypeStruct((rows, D), f32), jax.ShapeDtypeStruct((D, INNER), bf16)],
        (grads, weight, normed),
        scratch=[pltpu.VMEM((D, rows), bf16)],
        cost=(4 * rows * D * INNER, 4 * D * INNER, 0),
        carry=carry,
        identity=identity,
    )


def unproject_kernel(
    grads_ref, late_ref, w_ref, normed_ref, h_ref, g_ref, gain_ref, back_ref,
    out_ref, gain_out_ref, w_out_ref,
    total, turned, mended,
):
    step = pl.program_id(0)
    rows = h_ref.shape[0]
    length = rows // SLOTS

    @pl.when(step == 0)
    def _():
        total[...] = back_ref[...]
        turned[...] = normed_ref[...].T

    mended[...] = grads_ref[...]
    for slot in range(SLOTS):
        span = slice((slot + 1) * length - 16, (slot + 1) * length)
        extra = jnp.concatenate([jnp.zeros((8, COLS), f32), late_ref[slot]], axis=0)
        mended[span, :] = (grads_ref[span, :].astype(f32) + extra).astype(bf16)
    w_out_ref[...] = dot(turned[...], mended[...]).astype(bf16)
    total[...] += dot_nt(mended[...], w_ref[...])

    @pl.when(step == pl.num_programs(0) - 1)
    def _():
        gain_out_ref[...] = jnp.zeros_like(gain_out_ref)

        def one(span):
            h = h_ref[span, :]
            inverse = lax.rsqrt(jnp.mean(h * h, axis=-1, keepdims=True) + epsilon)
            back = total[span, :]
            unit = h * inverse
            gain_out_ref[0:1, :] += jnp.sum(back * unit, axis=0, keepdims=True)
            wanted = back * gain_ref[...]
            mean = jnp.mean(unit * wanted, axis=-1, keepdims=True)
            out_ref[span, :] = g_ref[span, :] + inverse * (wanted - unit * mean)

        for_rows(rows, 32, one)


def unproject(grads, late, weight, normed, h, g, gain_row, back, carry=None, identity=None):
    rows = h.shape[0]
    return launch(
        unproject_kernel,
        "unproject",
        (TAIL // COLS,),
        [
            pl.BlockSpec((rows, COLS), lambda n: (0, n)),
            pl.BlockSpec((SLOTS, 8, COLS), lambda n: (0, 0, n)),
            pl.BlockSpec((D, COLS), lambda n: (0, n)),
            pl.BlockSpec((rows, D), lambda n: (0, 0)),
            pl.BlockSpec((rows, D), lambda n: (0, 0)),
            pl.BlockSpec((rows, D), lambda n: (0, 0)),
            pl.BlockSpec((1, D), lambda n: (0, 0)),
            pl.BlockSpec((rows, D), lambda n: (0, 0)),
        ],
        [
            pl.BlockSpec((rows, D), lambda n: (0, 0)),
            pl.BlockSpec((8, D), lambda n: (0, 0)),
            pl.BlockSpec((D, COLS), lambda n: (0, n)),
        ],
        [
            jax.ShapeDtypeStruct((rows, D), f32),
            jax.ShapeDtypeStruct((8, D), f32),
            jax.ShapeDtypeStruct((D, TAIL), bf16),
        ],
        (grads, late, weight, normed, h, g, gain_row, back),
        scratch=[
            pltpu.VMEM((rows, D), f32),
            pltpu.VMEM((D, rows), bf16),
            pltpu.VMEM((rows, COLS), bf16),
        ],
        cost=(4 * rows * D * TAIL, 4 * D * TAIL, 0),
        carry=carry,
        identity=identity,
    )


MESH = pl.DeviceIdType.MESH
ANY = pl.BlockSpec(memory_space=pl.ANY)
DP_BITS = {"core": 1, "x": 2, "y": 4}
STEPS = ("z1", "z2", "x", "y", "core")


def place():
    dp, z = lax.axis_index("dp"), lax.axis_index("seq")
    return {"y": dp // 4, "x": lax.rem(dp // 2, 2), "core": lax.rem(dp, 2), "z": z, "dp": dp}


def partner(here, step):
    if step == "z1":
        return (here["dp"], here["z"] + 1 - 2 * lax.rem(here["z"], 2))
    if step == "z2":
        return (here["dp"], here["z"] + 2 - 4 * (here["z"] // 2))
    if step == "middle":
        return (here["dp"], 3 - here["z"])
    return (here["dp"] + DP_BITS[step] * (1 - 2 * here[step]), here["z"])


def greet(here, along=False):
    peers = STEPS + ("middle",) if along else STEPS
    barrier = pltpu.get_barrier_semaphore()
    for step in peers:
        pl.semaphore_signal(barrier, inc=1, device_id=partner(here, step), device_id_type=MESH)
    pl.semaphore_wait(barrier, len(peers))


class Exchange:
    def __init__(self, shapes, split, pace):
        self.shapes, self.pace = shapes, pace
        self.jobs, self.waves = [], []
        for index, (rows, columns) in enumerate(shapes):
            parts, pieces = split[index]
            height, width = rows // parts, columns // pieces
            for part in range(parts):
                for piece in range(pieces):
                    if piece % 2 == 0:
                        self.waves.append([])
                    job = (index, piece % 2, part * height, height, piece * width, width)
                    self.jobs.append(job)
                    self.waves[-1].append(job)

    def plan(self):
        last = len(self.waves) - 1 + self.pace * len(STEPS)
        ticks = [[] for _ in range(last + 1)]
        for stage in reversed(range(len(STEPS) + 1)):
            for wave, jobs in enumerate(self.waves):
                ticks[wave + self.pace * stage] += [(stage, job) for job in jobs]
        return ticks


class Gather(Exchange):
    def __init__(self, shards, split, pace):
        super().__init__(tuple(shard.shape for shard in shards), split, pace)
        self.shards, self.wholes = list(shards), {}
        self.entries = self.plan()

    def done(self, index):
        return max(t for t, entries in enumerate(self.entries) for _, job in entries if job[0] == index)

    def whole(self, index):
        found = self.wholes[index]
        return found.reshape(-1, found.shape[-1])

    def until(self, last):
        first = getattr(self, "reached", 0)
        self.reached = last + 1
        return Run(self, first, last)


class Run:
    def __init__(self, gather, first, last):
        self.gather = gather
        self.entries = gather.entries[first : last + 1]
        live = sorted({job[0] for entries in self.entries for stage, job in entries if stage < len(STEPS)})
        self.live = live
        self.fresh = [index for index in live if index not in gather.wholes]
        self.old = [index for index in live if index in gather.wholes]
        needed = {job[0] for entries in self.entries for stage, job in entries if stage == 0}
        self.sources = sorted(needed | set(self.fresh))
        self.args = [gather.shards[i] for i in self.sources] + [gather.wholes[i] for i in self.old]
        self.in_specs = [ANY] * len(self.args)
        self.out_specs = [ANY] * len(live)
        self.out_shape = [
            jax.ShapeDtypeStruct((2, 2, 2, 4) + gather.shapes[i], gather.shards[i].dtype) for i in live
        ]
        self.aliases = {len(self.sources) + k: live.index(i) for k, i in enumerate(self.old)}
        self.started = [
            (stage, job) for entries in self.entries for stage, job in entries if stage < len(STEPS)
        ]
        self.scratch = [
            pltpu.SemaphoreType.DMA((max(1, len(self.fresh)),)),
            pltpu.SemaphoreType.DMA((len(self.started),)),
            pltpu.SemaphoreType.DMA((len(self.started),)),
        ]

    def results(self, wholes):
        for index, whole in zip(self.live, wholes):
            self.gather.wholes[index] = whole
        return None

    def ticks(self, ins, outs, scratch, along=False):
        local_sems, send_sems, recv_sems = scratch
        here = place()
        shards = dict(zip(self.sources, ins))
        wholes = dict(zip(self.live, outs))
        own = [
            pltpu.make_async_copy(
                shards[i], wholes[i].at[here["y"], here["x"], here["core"], here["z"]], local_sems.at[k]
            )
            for k, i in enumerate(self.fresh)
        ]

        def make(stage, job):
            index, colour, top, height, left, width = job
            order = ("z1", "z2", "x", "y", "core") if colour == 0 else ("z1", "z2", "y", "x", "core")
            done = order[:stage]
            axis = lambda name: slice(None) if name in done else here[name]
            depth = here["z"]
            if "z2" in done:
                depth = slice(None)
            elif "z1" in done:
                depth = pl.ds(here["z"] // 2 * 2, 2)
            rows, columns = pl.ds(top, height), pl.ds(left, width)
            target = wholes[index].at[axis("y"), axis("x"), axis("core"), depth, rows, columns]
            source = shards[index].at[rows, columns] if stage == 0 else target
            number = self.started.index((stage, job))
            return pltpu.make_async_remote_copy(
                src_ref=source,
                dst_ref=target,
                send_sem=send_sems.at[number],
                recv_sem=recv_sems.at[number],
                device_id=partner(here, order[stage]),
                device_id_type=MESH,
            )

        ended = set()

        def steps(number, entries):
            actions = []
            if number == 0:
                actions.append(lambda: greet(here, along))
                actions += [copy.start for copy in own]
            if number == 1:
                actions += [copy.wait for copy in own]
            for stage, job in entries:
                before = (stage - 1, job)
                if before in self.started:
                    actions.append(lambda before=before: make(*before).wait())
                    ended.add(before)
                if stage < len(STEPS):
                    actions.append(lambda stage=stage, job=job: make(stage, job).start())
            return actions

        lists = [steps(number, entries) for number, entries in enumerate(self.entries)]
        last = [lambda key=key: make(*key).wait() for key in self.started if key not in ended]
        if len(lists) == 1:
            last = [copy.wait for copy in own] + last
        lists.append(last)

        def run(actions):
            for action in actions:
                action()

        return [functools.partial(run, actions) for actions in lists]


class Reduce(Exchange):
    def __init__(self, partials, split, pace=2, heads=None):
        super().__init__(tuple(partial.shape[1:] for partial in partials), split, pace)
        self.heads = heads is not None
        self.aliases = {}
        self.args = [partial.reshape((2, 2, 2, 4) + partial.shape[1:]) for partial in partials]
        count, number = len(partials), len(self.jobs)
        self.in_specs = [ANY] * count
        outs = list(self.shapes)
        if self.heads:
            self.args.append(heads)
            self.in_specs.append(pl.BlockSpec(heads.shape, lambda *_: (0, 0)))
            outs.append(heads.shape)
        self.out_specs = [pl.BlockSpec(shape, lambda *_: (0, 0)) for shape in outs]
        self.out_shape = [jax.ShapeDtypeStruct(shape, f32) for shape in outs]
        kept, landed = [], [[] for _ in STEPS]
        for index, _, _, height, _, width in self.jobs:
            kind = partials[index].dtype
            kept.append(pltpu.VMEM((2, 2, 4, height, width), kind))
            for stage, lead in enumerate(((2, 2, 4), (2, 4), (4,), (2,), ())):
                landed[stage].append(pltpu.VMEM(lead + (height, width), kind))
        tile = pltpu.SemaphoreType.DMA((number, len(STEPS)))
        self.scratch = kept + sum(landed, []) + [pltpu.SemaphoreType.DMA((number,)), tile, tile]
        if self.heads:
            line = pltpu.SemaphoreType.DMA((len(STEPS),))
            self.scratch += [pltpu.VMEM((len(STEPS),) + heads.shape, f32), line, line]

    def results(self, totals):
        return list(totals)

    def ticks(self, partials, totals, scratch, along=False):
        jobs, number, stages = self.jobs, len(self.jobs), len(STEPS)
        kept, landed = scratch[:number], scratch[number : 6 * number]
        local_sems, send_sems, recv_sems = scratch[6 * number : 6 * number + 3]
        here = place()
        y, x, core, z = here["y"], here["x"], here["core"], here["z"]
        half, odd = z // 2, lax.rem(z, 2)

        def order(job):
            return ("core", "y", "x", "z2", "z1") if job[1] == 0 else ("core", "x", "y", "z2", "z1")

        def leaving(job, stage):
            if stage == 1:
                return (1 - y, slice(None), slice(None)) if job[1] == 0 else (slice(None), 1 - x, slice(None))
            if stage == 2:
                return (y, 1 - x, slice(None)) if job[1] == 0 else (1 - y, x, slice(None))
            if stage == 3:
                return (y, x, pl.ds((1 - half) * 2, 2))
            return (y, x, half * 2 + 1 - odd)

        def cut(job, side):
            index, _, top, height, left, width = job
            return partials[index].at[:, :, side, :, pl.ds(top, height), pl.ds(left, width)]

        def load(job):
            k = jobs.index(job)
            return pltpu.make_async_copy(cut(job, core), kept[k], local_sems.at[k])

        def make(job, stage):
            k = jobs.index(job)
            return pltpu.make_async_remote_copy(
                src_ref=cut(job, 1 - core) if stage == 0 else kept[k].at[leaving(job, stage)],
                dst_ref=landed[stage * number + k],
                send_sem=send_sems.at[k, stage],
                recv_sem=recv_sems.at[k, stage],
                device_id=partner(here, order(job)[stage]),
                device_id_type=MESH,
            )

        def add(job, stage, mine):
            k = jobs.index(job)
            into, came = kept[k], landed[(stage - 1) * number + k]
            pick = lambda value: value if mine else 1 - value
            first = job[1] == 0

            def accumulate(target, source):
                into[target] = (into[target].astype(f32) + came[source].astype(f32)).astype(into.dtype)

            if stage == 1:
                def one(i, carry):
                    a, b = i // 4, lax.rem(i, 4)
                    where = (pick(y), a, b) if first else (a, pick(x), b)
                    accumulate(where, where)
                    return carry

                lax.fori_loop(0, 8, one, 0)
            elif stage == 2:
                def one(b, carry):
                    if first:
                        accumulate((y, pick(x), b), (pick(x), b))
                    else:
                        accumulate((pick(y), x, b), (pick(y), b))
                    return carry

                lax.fori_loop(0, 4, one, 0)
            elif stage == 3:
                for b in range(2):
                    accumulate((y, x, pick(half) * 2 + b), (pick(half) * 2 + b,))
            else:
                accumulate((y, x, half * 2 + pick(odd)), (pick(odd),))

        def finish(job):
            index, _, top, height, left, width = job
            k = jobs.index(job)
            summed = kept[k][y, x, z].astype(f32) + landed[4 * number + k][...].astype(f32)
            totals[index][top : top + height, left : left + width] = summed

        def heads_copy(stage):
            heads_landed, head_send, head_recv = scratch[6 * number + 3 :]
            return pltpu.make_async_remote_copy(
                src_ref=totals[-1],
                dst_ref=heads_landed.at[stage],
                send_sem=head_send.at[stage],
                recv_sem=head_recv.at[stage],
                device_id=partner(here, STEPS[stage]),
                device_id_type=MESH,
            )

        def tick(moment, entries):
            if moment == 0:
                greet(here, along)
                if self.heads:
                    totals[-1][...] = partials[-1][...]
            if self.heads and 0 < moment <= stages:
                heads_copy(moment - 1).wait()
                totals[-1][...] = totals[-1][...] + scratch[6 * number + 3][moment - 1]
            if self.heads and moment < stages:
                heads_copy(moment).start()
            for stage, job in entries:
                if stage == 0:
                    make(job, 0).start()
                    load(job).start()
                    continue
                if stage == 1:
                    load(job).wait()
                make(job, stage - 1).wait()
                if stage == stages:
                    finish(job)
                else:
                    add(job, stage, False)
                    make(job, stage).start()
                    add(job, stage, True)

        return [functools.partial(tick, moment, entries) for moment, entries in enumerate(self.plan())]


def alone(exchange, name, identity):
    ins, outs = len(exchange.in_specs), len(exchange.out_specs)

    def kernel(*refs):
        for tick in exchange.ticks(refs[:ins], refs[ins : ins + outs], refs[ins + outs :]):
            tick()

    found = pl.pallas_call(
        kernel,
        name=name,
        grid=(1,),
        in_specs=exchange.in_specs,
        out_specs=exchange.out_specs,
        out_shape=exchange.out_shape,
        scratch_shapes=exchange.scratch,
        input_output_aliases=exchange.aliases,
        compiler_params=params(collective_id=identity, has_side_effects=True),
    )(*exchange.args)
    return exchange.results(found)


def chain_kernel(steps, last, alone, local_ref, decay_ref, state_ref, landed, send_ref, send_sems, recv_sems):
    dp, me = lax.axis_index("dp"), lax.axis_index("seq")
    number = pl.program_id(0)
    total = landed.shape[0]
    receives = me > 0 if steps > 0 else me < last
    sends = me < last if steps > 0 else me > 0

    def make(part):
        return pltpu.make_async_remote_copy(
            src_ref=send_ref.at[part],
            dst_ref=landed.at[part],
            send_sem=send_sems.at[part],
            recv_sem=recv_sems.at[part],
            device_id=(dp, me + steps),
            device_id_type=MESH,
        )

    if alone:
        @pl.when(number == 0)
        def _():
            chain_greet(steps, last, pltpu.get_barrier_semaphore())

    @pl.when(jnp.logical_and(number < total, receives))
    def _():
        make(number).wait_recv()
        state_ref[0] = landed[number]

    @pl.when(jnp.logical_and(number < total, jnp.logical_not(receives)))
    def _():
        state_ref[0] = jnp.zeros(state_ref.shape[1:], bf16)

    @pl.when(jnp.logical_and(number < total, sends))
    def _():
        decay = decay_ref[0, 0:1, :]
        send_ref[number] = (decay * state_ref[0].astype(f32) + local_ref[0]).astype(bf16)
        make(number).start()

    @pl.when(jnp.logical_and(number == total, sends))
    def _():
        for part in range(total):
            make(part).wait_send()


def chain_greet(steps, last, barrier):
    dp, me = lax.axis_index("dp"), lax.axis_index("seq")
    receives = me > 0 if steps > 0 else me < last
    sends = me < last if steps > 0 else me > 0

    @pl.when(receives)
    def _():
        pl.semaphore_signal(barrier, inc=1, device_id=(dp, me - steps), device_id_type=MESH)

    @pl.when(sends)
    def _():
        pl.semaphore_wait(barrier, 1)


def chained(local, decay, slots, steps, identity, carry=None):
    pieces = INNER // CHAIN
    total = slots * pieces
    last = lax.axis_size("seq") - 1
    piece = lambda n: jnp.minimum(n, total - 1)
    return launch(
        functools.partial(chain_kernel, steps, last, carry is None),
        "chain",
        (total + 1,),
        [
            pl.BlockSpec((1, NSTATE, CHAIN), lambda n: (piece(n) // pieces, 0, piece(n) % pieces)),
            pl.BlockSpec((1, 8, CHAIN), lambda n: (piece(n) // pieces, 0, piece(n) % pieces)),
        ],
        [pl.BlockSpec((1, NSTATE, CHAIN), lambda n: (piece(n), 0, 0))],
        [jax.ShapeDtypeStruct((total, NSTATE, CHAIN), bf16)],
        (local, decay),
        scratch=[
            pltpu.VMEM((total, NSTATE, CHAIN), bf16),
            pltpu.VMEM((total, NSTATE, CHAIN), bf16),
            pltpu.SemaphoreType.DMA((total,)),
            pltpu.SemaphoreType.DMA((total,)),
        ],
        carry=carry,
        identity=identity,
        along=True,
        remote=True,
    )


def passed_along(value, steps):
    count = lax.axis_size("seq")
    initial, last = (max(0, -steps), min(count, count - steps))
    return lax.ppermute(value, "seq", [(source, source + steps) for source in range(initial, last)])


def all_slots(state):
    missing = SLOTS - state.shape[0]
    if missing:
        state = jnp.concatenate([state, jnp.zeros((missing,) + state.shape[1:], state.dtype)], axis=0)
    return state


def spaced(first, last, weights):
    marks, sum_so_far = [], 0
    for weight in weights:
        sum_so_far += weight
        marks.append(first + (last - first) * sum_so_far // sum(weights))
    return marks


def padded_rows(array, rows):
    return jnp.pad(array, ((0, rows - array.shape[0]), (0, 0)))


def pack_small(norm_gain, conv_weight, gate_gain):
    pieces = [norm_gain, conv_weight.reshape(LAYERS, -1), gate_gain]
    flat = jnp.concatenate(pieces, axis=1).reshape(-1)
    size = flat.shape[0]
    tiles = -(-size // (16 * LANES)) * 16
    return jnp.pad(flat, (0, tiles * LANES - size)).reshape(tiles, LANES)


def unpack_small(everything, norm_gain, conv_weight, gate_gain):
    count = everything.shape[0]
    size = LAYERS * (norm_gain.shape[1] + conv_weight.shape[1] * conv_weight.shape[2] + gate_gain.shape[1])
    everything = everything.reshape(count, -1)[:, :size].reshape(count, LAYERS, -1)
    everything = jnp.swapaxes(everything, 0, 1).astype(f32)
    first = norm_gain.shape[1]
    second = first + conv_weight.shape[1] * conv_weight.shape[2]
    norm = everything[..., :first].reshape(LAYERS, -1)
    conv = everything[..., first:second].reshape(LAYERS, count, CONV, -1)
    conv = jnp.swapaxes(conv, 1, 2).reshape(LAYERS, CONV, -1)
    gate = everything[..., second:].reshape(LAYERS, -1)
    return norm, conv, gate


def share_small(norm, conv, gate):
    count = lax.axis_size("dp") * lax.axis_size("seq")
    conv = jnp.swapaxes(conv.reshape(LAYERS, CONV, count, -1), 1, 2).reshape(LAYERS, count, -1)
    pieces = [norm.reshape(LAYERS, count, -1), conv, gate.reshape(LAYERS, count, -1)]
    flat = jnp.swapaxes(jnp.concatenate(pieces, axis=-1), 0, 1).reshape(count, -1)
    size = flat.shape[1]
    tiles = -(-size // (16 * LANES)) * 16
    return jnp.pad(flat, ((0, 0), (0, tiles * LANES - size))).reshape(count, tiles, LANES)


def own_small(mine, norm_gain, conv_weight, gate_gain):
    first = norm_gain.shape[1]
    second = first + conv_weight.shape[1] * conv_weight.shape[2]
    width = second + gate_gain.shape[1]
    mine = mine.reshape(-1)[: LAYERS * width].reshape(LAYERS, width)
    return mine[:, :first], mine[:, first:second].reshape(LAYERS, CONV, -1), mine[:, second:]


def body(
    hidden,
    out_grad,
    lengths,
    norm_gain,
    in_proj,
    conv_weight,
    gate_gain,
    out_proj,
    dt_bias,
    a_log,
    d_skip,
):
    length = hidden.shape[1]
    rows = SLOTS * length
    count = 1 if length >= SHORT else SLOTS
    swap = lengths[0] < lengths[1]

    def ordered(array):
        return jnp.where(swap, array[::-1], array)

    positions = lax.axis_index("seq") * length + jnp.arange(length, dtype=jnp.int32)
    valid = (positions[None, :] < ordered(lengths)[:, None]).astype(f32).reshape(rows, 1)
    valid = jnp.broadcast_to(valid, (rows, LANES))
    gates = in_proj[..., :INNER]
    tails = jnp.pad(in_proj[..., INNER:], ((0, 0), (0, 0), (0, TAIL - (PROJ - INNER))))
    ours = lax.axis_size("dp") == 8 and lax.axis_size("seq") == 4
    packed = pack_small(norm_gain, conv_weight, gate_gain)
    shards = [packed]
    for layer in range(LAYERS):
        shards += [tails[layer], gates[layer], out_proj[layer]]
    ids = iter(range(100))
    if ours:
        moving = Gather(shards, [(1, 1)] + [(3, 2)] * (3 * LAYERS), 1)
        tail_done, gate_done, out_done = [[moving.done(1 + 3 * layer + k) for layer in range(LAYERS)] for k in range(3)]
        end = len(moving.entries) - 1
        run = lambda last: moving.until(min(last, end)) if min(last, end) >= moving.reached else None
        alone(moving.until(tail_done[0]), "gather", next(ids))
        everything = moving.wholes[0].reshape((-1,) + packed.shape)
        whole = moving.whole
    else:
        gathered = [lax.all_gather(shard, ("dp", "seq"), axis=0, tiled=True) for shard in shards]
        everything = gathered[0].reshape((-1,) + packed.shape)
        whole = lambda index: gathered[index]
        run = lambda last: None
        tail_done = gate_done = out_done = [0] * LAYERS
    norm_all, conv_all, gate_all = unpack_small(everything, norm_gain, conv_weight, gate_gain)
    h = ordered(hidden).reshape(rows, D)
    kept = []
    for layer in range(LAYERS):
        gain_row = norm_all[layer].reshape(1, D)
        gate_row = gate_all[layer].reshape(1, INNER)
        taps = padded_rows(conv_all[layer], 8)
        heads = padded_rows(
            jnp.pad(
                jnp.stack([dt_bias[layer], a_log[layer]]), ((0, 0), (0, LANES - HEADS))
            ),
            8,
        )
        skip_row = jnp.repeat(d_skip[layer], HEADDIM).reshape(1, INNER)
        base = 1 + 3 * layer
        more = tail_done[layer + 1] if layer + 1 < LAYERS else out_done[layer]
        marks = spaced(tail_done[layer], out_done[layer], (1, 3, 2)) + spaced(out_done[layer], more, (1, 2))
        proj, raw, normed, *_ = project(h, gain_row, whole(base), run(marks[0]), next(ids))
        cube = proj.reshape(SLOTS, length, TAIL)
        raw = raw.reshape(SLOTS, length, LANES)
        edge = passed_along(cube[:, length - (CONV - 1) :, :CONVCH], 1)
        edge = jnp.pad(edge, ((0, 0), (8 - (CONV - 1), 0), (0, 0)))
        y, local, cum, size, act, decay, *_ = mix(cube, edge, taps, raw, heads, skip_row, run(marks[1]), next(ids))
        state, *_ = chained(local, decay, count, 1, next(ids), run(marks[2]))
        state = state.reshape(count, -1, NSTATE, CHAIN)
        gate, *_ = project_gate(normed, whole(base + 1), run(marks[3]), next(ids))
        flat = lambda array: array.reshape(rows, -1)
        h_next, mixture, inverse, *_ = branch(
            flat(y), gate, flat(act), flat(cum), state, gate_row, whole(base + 2), h, valid, run(marks[4]), next(ids)
        )
        kept.append(
            (h, gain_row, gate_row, taps, heads, skip_row, proj, gate, raw, normed, edge, cum, size, act,
             decay, state, mixture, inverse, whole(base), whole(base + 1), whole(base + 2))
        )
        h = h_next
    result = ordered(h.reshape(SLOTS, length, D))

    g = ordered(out_grad).reshape(rows, D)
    small = [None] * LAYERS
    partials = [None] * LAYERS
    totals = [[None] * 3 for _ in range(LAYERS)]
    waiting = None
    cut = lambda partial: partial.reshape(lax.axis_size("dp") * lax.axis_size("seq"), -1, partial.shape[-1])

    def summing(arrays):
        if not ours or arrays[0] is None:
            return None
        return Reduce([cut(array) for array in arrays], [(3, 2)] * len(arrays))

    for layer in reversed(range(LAYERS)):
        (h, gain_row, gate_row, taps, heads, skip_row, proj, gate, raw, normed, edge, cum, size, act,
         decay, state, mixture, inverse, weight_tail, weight_gate, weight_out) = kept[layer]
        cube = proj.reshape(SLOTS, length, TAIL)
        flat = lambda array: array.reshape(rows, -1)
        shaped = lambda array: array.reshape(SLOTS, length, -1)
        back, mean, grad_gate, partial_out, *sums = unbranch(
            g, valid, mixture, gate, inverse, gate_row, weight_out, summing([waiting]), next(ids)
        )
        if waiting is not None and ours:
            totals[layer + 1][0] = sums[0][0]
        dy, grads, local = ungate(back, mixture, gate, inverse, mean, gate_row, flat(act), flat(cum), count)
        back, partial_gate = unproject_gate(grads, weight_gate, normed)
        later, *_ = chained(local, decay, count, -1, next(ids))
        later = later.reshape(count, -1, NSTATE, CHAIN)
        grads, edge_grad, grad_taps, grad_heads, *sums = unmix(
            cube, edge, taps, raw, heads, skip_row, shaped(dy), all_slots(state), all_slots(later),
            cum, size, act, summing([partial_gate, partial_out]), next(ids),
        )
        if ours:
            totals[layer][1], totals[layer][2] = sums[0]
        late = passed_along(edge_grad[:, 8 - (CONV - 1) :].astype(bf16), -1).astype(f32)
        late = jnp.pad(late, ((0, 0), (8 - (CONV - 1), 0), (0, TAIL - CONVCH)))
        g, grad_norm, waiting = unproject(flat(grads), late, weight_tail, normed, h, g, gain_row, back)
        partials[layer] = (waiting, partial_gate, partial_out)
        small[layer] = (
            grad_norm[0], jnp.sum(grad_taps, axis=0)[:CONV], grad_gate[0],
            jnp.sum(grad_heads, axis=0)[:3, :HEADS],
        )
    grad_hidden = ordered(g.reshape(SLOTS, length, D))
    stacked = [jnp.stack([small[layer][member] for layer in range(LAYERS)]) for member in range(4)]
    shares = share_small(*stacked[:3])
    head_sums = jnp.pad(stacked[3].reshape(-1, HEADS), ((0, 8 - 3 * LAYERS), (0, LANES - HEADS)))
    if ours:
        totals[0][0], mine, head_sums = alone(
            Reduce([cut(waiting), shares], [(3, 2), (1, 1)], heads=head_sums), "reduce", next(ids)
        )
    else:
        totals = [
            [
                lax.optimization_barrier(
                    lax.psum_scatter(partial, ("dp", "seq"), scatter_dimension=0, tiled=True)
                ).astype(f32)
                for partial in members
            ]
            for members in partials
        ]
        mine = lax.psum_scatter(shares, ("dp", "seq"), scatter_dimension=0, tiled=True)
        head_sums = lax.psum(head_sums, ("dp", "seq"))
    grad_norm, grad_conv, grad_gate = own_small(mine, norm_gain, conv_weight, gate_gain)
    grad_heads = head_sums[: 3 * LAYERS, :HEADS].reshape(LAYERS, 3, HEADS)
    return (
        result,
        grad_hidden,
        grad_norm,
        jnp.stack([jnp.concatenate([gate, tail[:, : PROJ - INNER]], axis=1) for tail, gate, _ in totals]),
        grad_conv,
        grad_gate,
        jnp.stack([members[2] for members in totals]),
        grad_heads[:, 0],
        grad_heads[:, 1],
        grad_heads[:, 2],
    )


def solution(mesh):
    tokens = P("dp", "seq", None)
    every = ("dp", "seq")
    weights = (P(None, every), P(None, every, None), P(None, None, every), P(None, every), P(None, every, None))
    return jax.shard_map(
        body,
        mesh=mesh,
        in_specs=(tokens, tokens, P("dp")) + weights + (P(), P(), P()),
        out_specs=(tokens, tokens) + weights + (P(), P(), P()),
        check_vma=False,
    )
```

```python
import functools

import jax
import jax.numpy as jnp
from jax import lax
from jax.experimental import pallas as pl
from jax.experimental.pallas import tpu as pltpu
from jax.sharding import PartitionSpec as P

D = 1536
HEADS = 48
HEADDIM = 64
NSTATE = 128
CONV = 4
LAYERS = 2
INNER = 3072
CONVCH = 3328
PROJ = 6448
SLOTS = 2
SHORT = 256

LANES = 128
TAIL = 3584
BLK = 512
MAPS = 2 * NSTATE
NB = INNER // BLK
COLS = 512
PER = BLK // HEADDIM

f32 = jnp.float32
bf16 = jnp.bfloat16
epsilon = 1e-05
VMEM_LIMIT = 58 << 20


def launch(
    kernel, name, grid, in_specs, out_specs, out_shape, args, scratch=(), cost=None, carry=None, identity=None,
    relay=False,
):
    options = {"compiler_params": params()}
    if cost is not None:
        options["cost_estimate"] = pl.CostEstimate(flops=cost[0], bytes_accessed=cost[1], transcendentals=cost[2])
    if carry is not None or relay:
        options["compiler_params"] = params(collective_id=identity, has_side_effects=True)
    if carry is None:
        return pl.pallas_call(
            kernel, name=name, grid=grid, in_specs=in_specs, out_specs=out_specs, out_shape=out_shape,
            scratch_shapes=list(scratch), **options,
        )(*args)
    sizes = [len(in_specs), len(carry.in_specs), len(out_specs), len(carry.out_specs), len(scratch)]
    if carry.aliases:
        options["input_output_aliases"] = {sizes[0] + i: sizes[2] + o for i, o in carry.aliases.items()}

    def wrapped(*refs):
        groups, at = [], 0
        for size in sizes:
            groups.append(refs[at : at + size])
            at += size
        step, total = 0, 1
        for axis, extent in enumerate(grid):
            step, total = step * extent + pl.program_id(axis), total * extent
        ticks = carry.ticks(groups[1], groups[3], refs[at:], relay)
        plan = {}
        for number, tick in enumerate(ticks[:-1]):
            plan.setdefault(number * total // (len(ticks) - 1), []).append(tick)
        for moment, members in plan.items():
            @pl.when(step == moment)
            def _(members=members):
                for member in members:
                    member()

        kernel(*groups[0], *groups[2], *groups[4])

        @pl.when(step == total - 1)
        def _():
            ticks[-1]()

    found = pl.pallas_call(
        wrapped, name=name, grid=grid, in_specs=list(in_specs) + carry.in_specs,
        out_specs=list(out_specs) + carry.out_specs, out_shape=list(out_shape) + carry.out_shape,
        scratch_shapes=list(scratch) + carry.scratch, **options,
    )(*args, *carry.args)
    return list(found[: sizes[2]]) + [carry.results(found[sizes[2] :])]


def params(**more):
    return pltpu.CompilerParams(vmem_limit_bytes=VMEM_LIMIT, **more)


def for_rows(total, size, function):
    def step(index, carry):
        function(pl.ds(pl.multiple_of(index * size, size), size))
        return carry

    lax.fori_loop(0, total // size, step, 0)


def dot(left, right):
    return jnp.dot(left, right, preferred_element_type=f32)


def dot_nt(left, right):
    return lax.dot_general(left, right, (((1,), (1,)), ((), ())), preferred_element_type=f32)


def dot_tn(left, right):
    return lax.dot_general(left, right, (((0,), (0,)), ((), ())), preferred_element_type=f32)


def dot_exact(left, right):
    return jnp.dot(left, right, preferred_element_type=f32, precision=lax.Precision.HIGHEST)


def halves(array):
    high = array.astype(bf16)
    return high, (array - high.astype(f32)).astype(bf16)


def dot_halves(left, right, product=dot):
    left_high, left_low = left
    right_high, right_low = right
    return product(left_high, right_high) + product(left_high, right_low) + product(left_low, right_high)


def dot_member(array, member):
    high, low = halves(array)
    return dot(high, member) + dot(low, member)


def sigmoid(vector):
    return 0.5 + 0.5 * jnp.tanh(0.5 * vector)


def softplus(vector):
    return jnp.maximum(vector, 0.0) + jnp.log1p(jnp.exp(-jnp.abs(vector)))


def spread(columns):
    length = columns.shape[0]
    return jnp.concatenate(
        [jnp.broadcast_to(columns[:, j : j + 1], (length, HEADDIM)) for j in range(PER)], axis=1
    )


def heads_first(columns, block):
    return pltpu.roll(columns, lax.rem(LANES - PER * block, LANES), 1)


def fold(array):
    return functools.reduce(jnp.add, [array[:, at : at + LANES] for at in range(0, array.shape[1], LANES)])


def expander(block):
    head = lax.broadcasted_iota(jnp.int32, (LANES, BLK), 0)
    mine = lax.broadcasted_iota(jnp.int32, (LANES, BLK), 1) // HEADDIM + block * PER
    return (head == mine).astype(bf16)


def stack_halves(scratch, arrays):
    length = arrays[0].shape[0]
    for number, array in enumerate(arrays):
        high, low = halves(array)
        scratch[2 * number * length : (2 * number + 1) * length, :] = high
        scratch[(2 * number + 1) * length : (2 * number + 2) * length, :] = low


def spread_all(scratch, block, length):
    wide = dot(scratch[...], expander(block))
    return [
        wide[at : at + length] + wide[at + length : at + 2 * length] for at in range(0, wide.shape[0], 2 * length)
    ]


def split_rows(cum_t, minus, plus):
    rows, length = HEADS, cum_t.shape[1]
    first = cum_t[:rows].astype(bf16).astype(f32)
    rest = cum_t[:rows] - first
    second = rest.astype(bf16).astype(f32)
    third = rest - second
    index = lax.broadcasted_iota(jnp.int32, (rows, 16, length), 1)
    wide = lambda array: jnp.broadcast_to(array[:, None, :], (rows, 16, length))

    def pick(offset, sign, ones):
        found = jnp.where(jnp.logical_and(index >= ones, index < ones + 3), 1.0, 0.0)
        for number, part in enumerate((first, second, third)):
            found = jnp.where(index == offset + number, wide(sign * part), found)
        return found.astype(bf16).reshape(rows * 16, length)

    minus[...] = pick(0, -1.0, 3)
    plus[...] = pick(3, 1.0, 0)


def head_pairs(array, pair):
    columns = array[:, pair * LANES : (pair + 1) * LANES]
    lane = lax.broadcasted_iota(jnp.int32, columns.shape, 1)
    zero = jnp.zeros_like(columns)
    return jnp.where(lane < HEADDIM, columns, zero), jnp.where(lane < HEADDIM, zero, columns)


def load_extended(scratch, edge_ref, rows_ref):
    scratch[0:8, :] = edge_ref[0]
    scratch[8:, :] = rows_ref[0]


def convolve(scratch, taps, length):
    total = taps[0:1] * scratch[5 : 5 + length, :]
    for k in range(1, CONV):
        total = total + taps[k : k + 1] * scratch[5 + k : 5 + k + length, :]
    return total


def lower(length):
    first = lax.broadcasted_iota(jnp.int32, (length, length), 0)
    second = lax.broadcasted_iota(jnp.int32, (length, length), 1)
    return first >= second


class Along:
    def __init__(self, steps, pieces, shape, kind):
        self.steps, self.pieces, self.shape, self.kind = steps, pieces, shape, kind
        self.scratch = [
            pltpu.VMEM((pieces + 1,) + shape, kind),
            pltpu.VMEM((pieces,) + shape, kind),
            pltpu.SemaphoreType.DMA((pieces,)),
            pltpu.SemaphoreType.DMA((pieces,)),
        ]

    def bind(self, landed, sent, send_sems, recv_sems):
        self.landed, self.sent, self.send_sems, self.recv_sems = landed, sent, send_sems, recv_sems
        self.me, last = lax.axis_index("seq"), lax.axis_size("seq") - 1
        ahead, behind = self.me < last, self.me > 0
        self.sends, self.receives = (ahead, behind) if self.steps > 0 else (behind, ahead)

    def peer(self, steps):
        return (lax.axis_index("dp"), self.me + steps)

    def greet(self):
        barrier = pltpu.get_barrier_semaphore()

        @pl.when(self.receives)
        def _():
            pl.semaphore_signal(barrier, inc=1, device_id=self.peer(-self.steps), device_id_type=pl.DeviceIdType.MESH)

        @pl.when(self.sends)
        def _():
            pl.semaphore_wait(barrier, 1)

    def open(self):
        self.landed[self.pieces] = jnp.zeros(self.shape, self.kind)

        @pl.when(jnp.logical_not(self.receives))
        def _():
            for piece in range(self.pieces):
                self.landed[piece] = jnp.zeros(self.shape, self.kind)

    def copy(self, piece):
        return pltpu.make_async_remote_copy(
            src_ref=self.sent.at[piece],
            dst_ref=self.landed.at[piece],
            send_sem=self.send_sems.at[piece],
            recv_sem=self.recv_sems.at[piece],
            device_id=self.peer(self.steps),
            device_id_type=pl.DeviceIdType.MESH,
        )

    def take(self, piece):
        @pl.when(self.receives)
        def _():
            self.copy(piece).wait_recv()

    def give(self, piece, value):
        @pl.when(self.sends)
        def _():
            self.sent[piece] = value()
            self.copy(piece).start()

    def grow(self, piece, local, decay):
        self.take(piece)
        self.give(piece, lambda: (decay * self.landed[piece].astype(f32) + local).astype(bf16))

    def close(self):
        @pl.when(self.sends)
        def _():
            for piece in range(self.pieces):
                self.copy(piece).wait_send()


def project_kernel(edge, alone, h_ref, gain_ref, w_ref, proj_ref, raw_ref, normed_ref, edge_ref, *flow):
    step = pl.program_id(0)
    total = h_ref.shape[0]
    length = total // SLOTS
    edge.bind(*flow)

    @pl.when(step == 0)
    def _():
        if alone:
            edge.greet()
        edge.open()

        def one(rows):
            h = h_ref[rows, :]
            inverse = lax.rsqrt(jnp.mean(h * h, axis=-1, keepdims=True) + epsilon)
            normed_ref[rows, :] = (h * inverse * gain_ref[...]).astype(bf16)

        for_rows(total, 32, one)

    product = dot(normed_ref[...], w_ref[...])
    proj_ref[...] = product
    for slot in range(SLOTS):
        edge.give(step * SLOTS + slot, lambda slot=slot: product[(slot + 1) * length - 8 : (slot + 1) * length])

    @pl.when(step == pl.num_programs(0) - 1)
    def _():
        raw_ref[...] = product[:, COLS - 2 * LANES : COLS - LANES]
        for piece in range(edge.pieces):
            edge.take(piece)
            number, slot = divmod(piece, SLOTS)
            edge_ref[slot, :, number * COLS : (number + 1) * COLS] = edge.landed[piece]
        edge.close()


def project(h, gain_row, weight, carry=None, identity=None):
    total = h.shape[0]
    edge = Along(1, SLOTS * (TAIL // COLS), (8, COLS), f32)
    return launch(
        functools.partial(project_kernel, edge, carry is None),
        "project",
        (TAIL // COLS,),
        [
            pl.BlockSpec((total, D), lambda n: (0, 0)),
            pl.BlockSpec((1, D), lambda n: (0, 0)),
            pl.BlockSpec((D, COLS), lambda n: (0, n)),
        ],
        [
            pl.BlockSpec((total, COLS), lambda n: (0, n)),
            pl.BlockSpec((total, LANES), lambda n: (0, 0)),
            pl.BlockSpec((total, D), lambda n: (0, 0)),
            pl.BlockSpec((SLOTS, 8, TAIL), lambda n: (0, 0, 0)),
        ],
        [
            jax.ShapeDtypeStruct((total, TAIL), f32),
            jax.ShapeDtypeStruct((total, LANES), f32),
            jax.ShapeDtypeStruct((total, D), bf16),
            jax.ShapeDtypeStruct((SLOTS, 8, TAIL), f32),
        ],
        (h, gain_row, weight),
        scratch=edge.scratch,
        cost=(2 * total * D * TAIL, 2 * D * TAIL, 0),
        carry=carry,
        identity=identity,
        relay=True,
    )


def mix_kernel(
    relay, alone, count, rows_ref, edge_ref, taps_ref, maps_ref, maps_edge_ref, maps_taps_ref, raw_ref, heads_ref, skip_ref,
    y_ref, state_ref, cum_ref, step_ref, act_ref, decay_ref,
    extended, maps_extended, inner, minus, plus, input_t, scales, local, decay, *flow,
):
    slot, block = pl.program_id(0), pl.program_id(1)
    number = slot * NB + block
    length = rows_ref.shape[1]
    relay.bind(*flow)

    @pl.when(number == 0)
    def _():
        if alone:
            relay.greet()
        relay.open()

    def grow(piece):
        relay.grow(piece, local[piece], decay[piece, 0:1, :])

    due = number - 1 - 2 * relay.me

    @pl.when(jnp.logical_and(due >= 0, due < NB))
    def _():
        grow(due)

    @pl.when(block == 0)
    def _():
        load_extended(maps_extended, maps_edge_ref, maps_ref)
        convolved = convolve(maps_extended, maps_taps_ref[...], length)
        maps = convolved * sigmoid(convolved)
        act_ref[0] = maps
        products = dot_halves(halves(maps[:, NSTATE:]), halves(maps[:, :NSTATE]), dot_nt)
        input_t[0], input_t[1] = halves(maps[:, :NSTATE].T)
        causal = lower(length)
        inner[...] = jnp.where(causal, products, 0.0)
        size = softplus(raw_ref[0] + heads_ref[0:1, :])
        decay = -size * jnp.exp(heads_ref[1:2, :])
        cum = dot_exact(causal.astype(f32), decay)
        cum_ref[0] = cum
        step_ref[0] = size
        split_rows(cum.T, minus, plus)
        stack_halves(scales, [size, jnp.exp(cum[length - 1 :, :] - cum)])

    load_extended(extended, edge_ref, rows_ref)
    convolved = convolve(extended, taps_ref[...], length)
    values = convolved * sigmoid(convolved)
    wide_step, remaining = spread_all(scales, block, length)
    stepped = values * wide_step
    low = stepped.astype(bf16)
    parts = []
    for pair in range(PER // 2):
        members = head_pairs(low, pair)
        pieces = []
        for first in range(0, length, LANES):
            end = first + LANES
            weights = []
            for j in range(2):
                rows = pl.ds(pl.multiple_of((block * PER + 2 * pair + j) * 16, 16), 16)
                change = dot_tn(plus[rows, first:end], minus[rows, :end])
                weights.append((inner[first:end, :end] * jnp.exp(jnp.minimum(change, 0.0))).astype(bf16))
            pieces.append(
                dot(jnp.concatenate(weights, axis=1), jnp.concatenate([member[:end] for member in members], axis=0))
            )
        parts.append(jnp.concatenate(pieces, axis=0))
    y_ref[0] = jnp.concatenate(parts, axis=1) + skip_ref[...] * values
    final = heads_first(cum_ref[0][length - 8 :, :], block)
    rate = jnp.broadcast_to(spread(jnp.exp(final))[7:], (8, BLK))
    decay_ref[0, 0] = rate

    @pl.when(slot < count)
    def _():
        local[number] = dot_halves((input_t[0], input_t[1]), halves(stepped * remaining))
        decay[number] = rate

    @pl.when(number == SLOTS * NB - 1)
    def _():
        for piece in range(relay.pieces):
            @pl.when(jnp.logical_or(piece >= NB, piece > due))
            def _():
                grow(piece)

            state_ref[piece] = relay.landed[piece]
        relay.close()


def mix(proj, edge, taps, raw, heads, skip_row, count, carry=None, identity=None):
    length = proj.shape[1]
    relay = Along(1, count * NB, (NSTATE, BLK), bf16)
    return launch(
        functools.partial(mix_kernel, relay, carry is None, count),
        "mix",
        (SLOTS, NB),
        [
            pl.BlockSpec((1, length, BLK), lambda s, b: (s, 0, b)),
            pl.BlockSpec((1, 8, BLK), lambda s, b: (s, 0, b)),
            pl.BlockSpec((8, BLK), lambda s, b: (0, b)),
            pl.BlockSpec((1, length, MAPS), lambda s, b: (s, 0, INNER // MAPS)),
            pl.BlockSpec((1, 8, MAPS), lambda s, b: (s, 0, INNER // MAPS)),
            pl.BlockSpec((8, MAPS), lambda s, b: (0, INNER // MAPS)),
            pl.BlockSpec((1, length, LANES), lambda s, b: (s, 0, 0)),
            pl.BlockSpec((8, LANES), lambda s, b: (0, 0)),
            pl.BlockSpec((1, BLK), lambda s, b: (0, b)),
        ],
        [
            pl.BlockSpec((1, length, BLK), lambda s, b: (s, 0, b)),
            pl.BlockSpec((count * NB, NSTATE, BLK), lambda s, b: (0, 0, 0)),
            pl.BlockSpec((1, length, LANES), lambda s, b: (s, 0, 0)),
            pl.BlockSpec((1, length, LANES), lambda s, b: (s, 0, 0)),
            pl.BlockSpec((1, length, MAPS), lambda s, b: (s, 0, 0)),
            pl.BlockSpec((1, 1, 8, BLK), lambda s, b: (s, b, 0, 0)),
        ],
        [
            jax.ShapeDtypeStruct((SLOTS, length, INNER), f32),
            jax.ShapeDtypeStruct((count * NB, NSTATE, BLK), bf16),
            jax.ShapeDtypeStruct((SLOTS, length, LANES), f32),
            jax.ShapeDtypeStruct((SLOTS, length, LANES), f32),
            jax.ShapeDtypeStruct((SLOTS, length, MAPS), f32),
            jax.ShapeDtypeStruct((SLOTS, NB, 8, BLK), f32),
        ],
        (proj, edge, taps, proj, edge, taps, raw, heads, skip_row),
        scratch=[
            pltpu.VMEM((length + 8, BLK), f32),
            pltpu.VMEM((length + 8, MAPS), f32),
            pltpu.VMEM((length, length), f32),
            pltpu.VMEM((16 * HEADS, length), bf16),
            pltpu.VMEM((16 * HEADS, length), bf16),
            pltpu.VMEM((2, NSTATE, length), bf16),
            pltpu.VMEM((4 * length, LANES), bf16),
            pltpu.VMEM((count * NB, NSTATE, BLK), f32),
            pltpu.VMEM((count * NB, 8, BLK), f32),
        ]
        + relay.scratch,
        cost=(6 * 10**9, 10**7, 10**7),
        carry=carry,
        identity=identity,
        relay=True,
    )


def project_gate_kernel(normed_ref, w_ref, gate_ref):
    gate_ref[...] = dot(normed_ref[...], w_ref[...])


def project_gate(normed, weight, carry=None, identity=None):
    total = normed.shape[0]
    return launch(
        project_gate_kernel,
        "project_gate",
        (INNER // COLS,),
        [pl.BlockSpec((total, D), lambda n: (0, 0)), pl.BlockSpec((D, COLS), lambda n: (0, n))],
        [pl.BlockSpec((total, COLS), lambda n: (0, n))],
        [jax.ShapeDtypeStruct((total, INNER), f32)],
        (normed, weight),
        cost=(2 * total * D * INNER, 2 * D * INNER, 0),
        carry=carry,
        identity=identity,
    )


def branch_kernel(
    y_ref, gate_ref, act_ref, cum_ref, state_ref, gain_ref, w_ref, h_ref, valid_ref,
    out_ref, mixture_ref, inverse_ref,
    total, squares, gated_low,
):
    block = pl.program_id(0)
    count = state_ref.shape[0]
    rows = y_ref.shape[0]
    length = rows // SLOTS

    @pl.when(block == 0)
    def _():
        total[...] = jnp.zeros_like(total)
        squares[...] = jnp.zeros_like(squares)

    for slot in range(SLOTS):
        span = slice(slot * length, (slot + 1) * length)
        mixture = y_ref[span, :]
        if slot < count:
            cum = heads_first(cum_ref[span, :], block)
            carried = dot_member(act_ref[span, NSTATE:], state_ref[slot, 0])
            mixture = mixture + carried * spread(jnp.exp(cum))
        gate = gate_ref[span, :]
        gated = mixture * gate * sigmoid(gate)
        mixture_ref[span, :] = mixture
        square = gated * gated
        squares[span, :] += fold(square)
        gated_low[span, :] = (gated * gain_ref[...]).astype(bf16)
    total[...] += dot(gated_low[...], w_ref[...])

    @pl.when(block == NB - 1)
    def _():
        def one(span):
            mean = jnp.sum(squares[span, :], axis=-1, keepdims=True) / INNER
            inverse = lax.rsqrt(mean + epsilon)
            inverse_ref[span, :] = jnp.broadcast_to(inverse, (32, LANES))
            factor = inverse * valid_ref[span, 0:1]
            out_ref[span, :] = h_ref[span, :] + factor * total[span, :]

        for_rows(rows, 32, one)


def branch(y, gate, act, cum, state, gain_row, weight, h, valid, carry=None, identity=None):
    rows = h.shape[0]
    count = state.shape[0]
    return launch(
        branch_kernel,
        "branch",
        (NB,),
        [
            pl.BlockSpec((rows, BLK), lambda b: (0, b)),
            pl.BlockSpec((rows, BLK), lambda b: (0, b)),
            pl.BlockSpec((rows, MAPS), lambda b: (0, 0)),
            pl.BlockSpec((rows, LANES), lambda b: (0, 0)),
            pl.BlockSpec((count, 1, NSTATE, BLK), lambda b: (0, b, 0, 0)),
            pl.BlockSpec((1, BLK), lambda b: (0, b)),
            pl.BlockSpec((BLK, D), lambda b: (b, 0)),
            pl.BlockSpec((rows, D), lambda b: (0, 0)),
            pl.BlockSpec((rows, LANES), lambda b: (0, 0)),
        ],
        [
            pl.BlockSpec((rows, D), lambda b: (0, 0)),
            pl.BlockSpec((rows, BLK), lambda b: (0, b)),
            pl.BlockSpec((rows, LANES), lambda b: (0, 0)),
        ],
        [
            jax.ShapeDtypeStruct((rows, D), f32),
            jax.ShapeDtypeStruct((rows, INNER), f32),
            jax.ShapeDtypeStruct((rows, LANES), f32),
        ],
        (y, gate, act, cum, state, gain_row, weight, h, valid),
        scratch=[
            pltpu.VMEM((rows, D), f32),
            pltpu.VMEM((rows, LANES), f32),
            pltpu.VMEM((rows, BLK), bf16),
        ],
        cost=(2 * rows * D * INNER, 2 * D * INNER, 10**6),
        carry=carry,
        identity=identity,
    )


def unbranch_kernel(
    g_ref, valid_ref, mixture_ref, gate_ref, inverse_ref, gain_ref, w_ref,
    back_ref, mean_ref, gain_out_ref, w_out_ref,
    low, norm_low,
):
    block = pl.program_id(0)
    rows = g_ref.shape[0]

    @pl.when(block == 0)
    def _():
        def one(span):
            low[span, :] = (valid_ref[span, 0:1] * g_ref[span, :]).astype(bf16)

        for_rows(rows, 32, one)
        mean_ref[...] = jnp.zeros_like(mean_ref)

    back_ref[...] = dot_nt(low[...], w_ref[...])
    gain_out_ref[...] = jnp.zeros_like(gain_out_ref)

    def one(span):
        gate = gate_ref[span, :]
        gated = mixture_ref[span, :] * gate * sigmoid(gate)
        back = back_ref[span, :]
        unit = gated * inverse_ref[span, 0:1]
        norm_low[span, :] = (unit * gain_ref[...]).astype(bf16)
        gain_out_ref[0:1, :] += jnp.sum(back * unit, axis=0, keepdims=True)
        product = gated * back * gain_ref[...]
        mean_ref[span, :] += fold(product)

    for_rows(rows, 128, one)
    w_out_ref[...] = dot_tn(norm_low[...], low[...]).astype(bf16)

    @pl.when(block == NB - 1)
    def _():
        mean_ref[...] = jnp.broadcast_to(
            jnp.sum(mean_ref[...], axis=-1, keepdims=True) / INNER, mean_ref.shape
        )


def unbranch(g, valid, mixture, gate, inverse, gain_row, weight, carry=None, identity=None):
    rows = g.shape[0]
    return launch(
        unbranch_kernel,
        "unbranch",
        (NB,),
        [
            pl.BlockSpec((rows, D), lambda b: (0, 0)),
            pl.BlockSpec((rows, LANES), lambda b: (0, 0)),
            pl.BlockSpec((rows, BLK), lambda b: (0, b)),
            pl.BlockSpec((rows, BLK), lambda b: (0, b)),
            pl.BlockSpec((rows, LANES), lambda b: (0, 0)),
            pl.BlockSpec((1, BLK), lambda b: (0, b)),
            pl.BlockSpec((BLK, D), lambda b: (b, 0)),
        ],
        [
            pl.BlockSpec((rows, BLK), lambda b: (0, b)),
            pl.BlockSpec((rows, LANES), lambda b: (0, 0)),
            pl.BlockSpec((8, BLK), lambda b: (0, b)),
            pl.BlockSpec((BLK, D), lambda b: (b, 0)),
        ],
        [
            jax.ShapeDtypeStruct((rows, INNER), f32),
            jax.ShapeDtypeStruct((rows, LANES), f32),
            jax.ShapeDtypeStruct((8, INNER), f32),
            jax.ShapeDtypeStruct((INNER, D), bf16),
        ],
        (g, valid, mixture, gate, inverse, gain_row, weight),
        scratch=[pltpu.VMEM((rows, D), bf16), pltpu.VMEM((rows, BLK), bf16)],
        cost=(4 * rows * D * INNER, 4 * D * INNER, 10**6),
        carry=carry,
        identity=identity,
    )


def ungate_kernel(
    back_ref, mixture_ref, gate_ref, inverse_ref, mean_ref, gain_ref, act_ref, cum_ref,
    dy_ref, dgate_ref, state_ref,
    output_t,
):
    block = pl.program_id(0)
    rows = back_ref.shape[0]
    length = rows // SLOTS

    @pl.when(block == 0)
    def _():
        for slot in range(state_ref.shape[0]):
            span = slice(slot * length, (slot + 1) * length)
            output_t[slot, 0], output_t[slot, 1] = halves(act_ref[span, NSTATE:].T)

    for slot in range(SLOTS):
        span = slice(slot * length, (slot + 1) * length)
        gate = gate_ref[span, :]
        curve = sigmoid(gate)
        mixture = mixture_ref[span, :]
        swish = gate * curve
        inverse = inverse_ref[span, 0:1]
        back = back_ref[span, :] * gain_ref[...]
        pull = inverse * inverse * inverse * mean_ref[span, 0:1]
        grad = inverse * back - (mixture * swish) * pull
        dy = grad * swish
        dy_ref[span, :] = dy
        dgate_ref[span, :] = (grad * mixture * curve * (1.0 + gate * (1.0 - curve))).astype(bf16)
        if slot < state_ref.shape[0]:
            grown = spread(jnp.exp(heads_first(cum_ref[span, :], block)))
            state_ref[slot, 0] = dot_halves((output_t[slot, 0], output_t[slot, 1]), halves(dy * grown))


def ungate(back, mixture, gate, inverse, mean, gain_row, act, cum, count, carry=None, identity=None):
    rows = back.shape[0]
    length = rows // SLOTS
    return launch(
        ungate_kernel,
        "ungate",
        (NB,),
        [
            pl.BlockSpec((rows, BLK), lambda b: (0, b)),
            pl.BlockSpec((rows, BLK), lambda b: (0, b)),
            pl.BlockSpec((rows, BLK), lambda b: (0, b)),
            pl.BlockSpec((rows, LANES), lambda b: (0, 0)),
            pl.BlockSpec((rows, LANES), lambda b: (0, 0)),
            pl.BlockSpec((1, BLK), lambda b: (0, b)),
            pl.BlockSpec((rows, MAPS), lambda b: (0, 0)),
            pl.BlockSpec((rows, LANES), lambda b: (0, 0)),
        ],
        [
            pl.BlockSpec((rows, BLK), lambda b: (0, b)),
            pl.BlockSpec((rows, BLK), lambda b: (0, b)),
            pl.BlockSpec((count, 1, NSTATE, BLK), lambda b: (0, b, 0, 0)),
        ],
        [
            jax.ShapeDtypeStruct((rows, INNER), f32),
            jax.ShapeDtypeStruct((rows, INNER), bf16),
            jax.ShapeDtypeStruct((count, NB, NSTATE, BLK), f32),
        ],
        (back, mixture, gate, inverse, mean, gain_row, act, cum),
        scratch=[pltpu.VMEM((count, 2, NSTATE, length), bf16)],
        cost=(10**9, 2 * 10**7, 10**7),
        carry=carry,
        identity=identity,
    )


def unmix_kernel(
    relay, edge, alone, count, rows_ref, edge_ref, taps_ref, maps_ref, maps_edge_ref, maps_taps_ref, raw_ref, heads_ref, skip_ref,
    dy_ref, state_ref, local_ref, decay_ref, cum_ref, step_ref, act_ref,
    grads_ref, late_ref, taps_out_ref, heads_out_ref,
    extended, maps_extended, inner, d_inner, minus, plus, scales, grad_ext, maps_grad_ext, d_maps, d_cum, d_step, over_rows, sums, *flow,
):
    turn, block = pl.program_id(0), pl.program_id(1)
    slot = SLOTS - 1 - turn
    length = rows_ref.shape[1]
    relay.bind(*flow[:4])
    edge.bind(*flow[4:])
    reached = slot < count
    piece = jnp.where(reached, slot * NB + block, relay.pieces)
    number = turn * (NB + 1) + block

    @pl.when(number == 0)
    def _():
        if alone:
            relay.greet()
        relay.open()
        edge.open()

    def grow(member):
        its_slot, its_block = member // NB, lax.rem(member, NB)
        relay.grow(member, local_ref[its_slot, its_block], decay_ref[its_slot, its_block, 0:1, :])

    due = number - jnp.minimum(2 * (lax.axis_size("seq") - 1 - relay.me), NB)

    @pl.when(jnp.logical_and(due >= 0, due < NB))
    def _():
        grow(due)

    if count == SLOTS:
        @pl.when(jnp.logical_and(turn == 0, block < NB))
        def _():
            grow(NB + block)

    def conv_back(gradient, taps, given, padded):
        padded[8 : 8 + length, :] = gradient
        back = taps[0:1] * padded[3 : 3 + length + 8, :]
        for k in range(1, CONV):
            back = back + taps[k : k + 1] * padded[3 - k : 3 - k + length + 8, :]
        lines = [
            jnp.sum(gradient * given[5 + k : 5 + k + length, :], axis=0, keepdims=True) for k in range(CONV)
        ]
        lines.append(jnp.zeros((8 - CONV, gradient.shape[1]), f32))
        return back[:8], back[8:].astype(bf16), jnp.concatenate(lines, axis=0)

    @pl.when(block == 0)
    def _():
        for padded in (grad_ext, maps_grad_ext):
            padded[0:8, :] = jnp.zeros((8, padded.shape[1]), f32)
            padded[8 + length :, :] = jnp.zeros((8, padded.shape[1]), f32)
        maps = act_ref[0]
        products = dot_halves(halves(maps[:, :NSTATE]), halves(maps[:, NSTATE:]), dot_nt)
        inner[...] = jnp.where(lower(length).T, products, 0.0)
        cum = cum_ref[0]
        split_rows(cum.T, minus, plus)
        stack_halves(scales, [step_ref[0], jnp.exp(cum[length - 1 :, :] - cum), jnp.exp(cum)])
        d_inner[...] = jnp.zeros_like(d_inner)
        d_maps[...] = jnp.zeros_like(d_maps)
        d_cum[...] = jnp.zeros_like(d_cum)
        d_step[...] = jnp.zeros_like(d_step)
        over_rows[...] = jnp.zeros_like(over_rows)
        sums[...] = jnp.zeros_like(sums)

    @pl.when(block < NB)
    def _():
        load_extended(extended, edge_ref, rows_ref)
        convolved = convolve(extended, taps_ref[...], length)
        curve = sigmoid(convolved)
        values = convolved * curve
        size, remaining, grown = spread_all(scales, block, length)
        stepped = values * size
        low = stepped.astype(bf16)
        dy = dy_ref[0]
        dy_low = dy.astype(bf16)
        dy_t = dy.T.astype(bf16)
        parts = []
        moved_all = {first: [] for first in range(0, length, LANES)}
        for pair in range(PER // 2):
            low_pair = head_pairs(low, pair)
            dy_pair = head_pairs(dy_low, pair)
            dy_pair_t = dy_t[pair * LANES : (pair + 1) * LANES, :]
            pieces = []
            column_sums = [None, None]
            for first in range(0, length, LANES):
                end = first + LANES
                weights = []
                products = inner[first:end, first:]
                grads_sum = None
                for j in range(2):
                    rows = pl.ds(pl.multiple_of((block * PER + 2 * pair + j) * 16, 16), 16)
                    change = dot_tn(minus[rows, first:end], plus[rows, first:])
                    decays = jnp.exp(jnp.minimum(change, 0.0))
                    weights.append((products * decays).astype(bf16))
                    grads = dot(low_pair[j][first:end], dy_pair_t[:, first:]) * decays
                    grads_sum = grads if grads_sum is None else grads_sum + grads
                    moved = (grads * products).astype(bf16)
                    moved_all[first].append(moved)
                    found = jnp.sum(moved.astype(f32), axis=0, keepdims=True)
                    if first:
                        found = jnp.concatenate([jnp.zeros((1, first), f32), found], axis=1)
                    column_sums[j] = found if column_sums[j] is None else column_sums[j] + found
                d_inner[first:end, first:] += grads_sum
                pieces.append(
                    dot(jnp.concatenate(weights, axis=1), jnp.concatenate([part[first:] for part in dy_pair], axis=0))
                )
            parts.append(jnp.concatenate(pieces, axis=0))
            for j in range(2):
                over_rows[pl.ds(block * PER + 2 * pair + j, 1), :] = column_sums[j]
        intra = jnp.concatenate(parts, axis=1)
        for first, moved in moved_all.items():
            span = length - first
            head = lax.broadcasted_iota(jnp.int32, (PER * span, LANES), 0) // span + block * PER
            chosen = (lax.broadcasted_iota(jnp.int32, (PER * span, LANES), 1) == head).astype(bf16)
            d_cum[first : first + LANES, :] -= dot(jnp.concatenate(moved, axis=1), chosen)
        which = lax.broadcasted_iota(jnp.int32, (BLK, LANES), 0) // HEADDIM + block * PER
        chosen = which == lax.broadcasted_iota(jnp.int32, (BLK, LANES), 1)
        member = chosen.astype(f32)
        member_low = chosen.astype(bf16)
        state = jnp.where(reached, state_ref[0, 0].astype(f32), 0.0).astype(bf16)
        later = relay.landed[piece]
        maps = act_ref[0]
        from_later = dot_member(maps[:, :NSTATE], later) * remaining
        d_stepped = intra + from_later
        left = stepped * remaining
        grown_dy = dy * grown
        used = stepped * from_later
        d_cum[...] += dot_member(
            grown_dy * dot_member(maps[:, NSTATE:], state) - used, member_low
        )
        d_maps[:, :NSTATE] += dot_nt(left.astype(bf16), later)
        d_maps[:, NSTATE:] += dot_nt(grown_dy.astype(bf16), state)
        d_step[...] += dot_member(d_stepped * values, member_low)
        lines = jnp.concatenate(
            [
                jnp.sum(used, axis=0, keepdims=True),
                jnp.sum(dy * values, axis=0, keepdims=True),
                jnp.sum(later.astype(f32) * state.astype(f32), axis=0, keepdims=True),
                jnp.zeros((5, BLK), f32),
            ],
            axis=0,
        )
        sums[...] += dot_exact(lines, member)
        d_values = d_stepped * size + skip_ref[...] * dy
        before, grads_ref[0], taps_out_ref[0] = conv_back(
            d_values * curve * (1.0 + convolved * (1.0 - curve)), taps_ref[...], extended, grad_ext
        )
        edge.give(number, lambda: before)

    @pl.when(block == NB)
    def _():
        load_extended(maps_extended, maps_edge_ref, maps_ref)
        convolved = convolve(maps_extended, maps_taps_ref[...], length)
        curve = sigmoid(convolved)
        maps = act_ref[0]
        masked = jnp.where(lower(length).T, d_inner[...], 0.0)
        d_input = d_maps[:, :NSTATE] + dot_halves(halves(masked), halves(maps[:, NSTATE:]))
        d_output = d_maps[:, NSTATE:] + dot_halves(halves(masked.T), halves(maps[:, :NSTATE]))
        d_both = jnp.concatenate([d_input, d_output], axis=1)
        before, inside, lines = conv_back(
            d_both * curve * (1.0 + convolved * (1.0 - curve)), maps_taps_ref[...], maps_extended, maps_grad_ext
        )
        rest = jnp.zeros((8, BLK - MAPS), f32)
        edge.give(number, lambda: jnp.concatenate([before, rest], axis=1))
        taps_out_ref[0] = jnp.concatenate([lines, rest], axis=1)
        final = cum_ref[0][length - 1 :, :]
        at_end = sums[0:1, :] + jnp.exp(final) * sums[2:3, :]
        d_total = d_cum[...] + over_rows[...].T
        position = lax.broadcasted_iota(jnp.int32, (length, 1), 0)
        d_total = d_total + jnp.where(position == length - 1, at_end, 0.0)
        d_decay = dot_exact(lower(length).T.astype(f32), d_total)
        rate = jnp.exp(heads_ref[1:2, :])
        size = step_ref[0]
        d_raw = (d_step[...] - d_decay * rate) * sigmoid(raw_ref[0] + heads_ref[0:1, :])
        d_raw_low = d_raw.astype(bf16)
        grads_ref[0] = jnp.concatenate([inside, d_raw_low, jnp.zeros_like(d_raw_low)], axis=1)
        heads_out_ref[0] = jnp.concatenate(
            [
                jnp.sum(d_raw, axis=0, keepdims=True),
                jnp.sum(d_decay * (-size * rate), axis=0, keepdims=True),
                sums[1:2, :],
                jnp.zeros((5, LANES), f32),
            ],
            axis=0,
        )

    @pl.when(number == SLOTS * (NB + 1) - 1)
    def _():
        relay.close()
        for given in range(edge.pieces):
            edge.take(given)
            its_turn, its_block = divmod(given, NB + 1)
            late_ref[SLOTS - 1 - its_turn, :, its_block * BLK : (its_block + 1) * BLK] = edge.landed[given]
        edge.close()


def unmix(proj, edge, taps, raw, heads, skip_row, dy, state, local, decay, cum, size, act, count, carry=None, identity=None):
    length = proj.shape[1]
    relay = Along(-1, count * NB, (NSTATE, BLK), bf16)
    border = Along(-1, SLOTS * (NB + 1), (8, BLK), f32)
    of = lambda s: SLOTS - 1 - s
    known = lambda s: jnp.minimum(of(s), count - 1)
    inside = lambda b: jnp.minimum(b, NB - 1)
    return launch(
        functools.partial(unmix_kernel, relay, border, carry is None, count),
        "unmix",
        (SLOTS, NB + 1),
        [
            pl.BlockSpec((1, length, BLK), lambda s, b: (of(s), 0, inside(b))),
            pl.BlockSpec((1, 8, BLK), lambda s, b: (of(s), 0, inside(b))),
            pl.BlockSpec((8, BLK), lambda s, b: (0, inside(b))),
            pl.BlockSpec((1, length, MAPS), lambda s, b: (of(s), 0, INNER // MAPS)),
            pl.BlockSpec((1, 8, MAPS), lambda s, b: (of(s), 0, INNER // MAPS)),
            pl.BlockSpec((8, MAPS), lambda s, b: (0, INNER // MAPS)),
            pl.BlockSpec((1, length, LANES), lambda s, b: (of(s), 0, 0)),
            pl.BlockSpec((8, LANES), lambda s, b: (0, 0)),
            pl.BlockSpec((1, BLK), lambda s, b: (0, inside(b))),
            pl.BlockSpec((1, length, BLK), lambda s, b: (of(s), 0, inside(b))),
            pl.BlockSpec((1, 1, NSTATE, BLK), lambda s, b: (known(s), inside(b), 0, 0)),
            pl.BlockSpec((count, NB, NSTATE, BLK), lambda s, b: (0, 0, 0, 0)),
            pl.BlockSpec((SLOTS, NB, 8, BLK), lambda s, b: (0, 0, 0, 0)),
            pl.BlockSpec((1, length, LANES), lambda s, b: (of(s), 0, 0)),
            pl.BlockSpec((1, length, LANES), lambda s, b: (of(s), 0, 0)),
            pl.BlockSpec((1, length, MAPS), lambda s, b: (of(s), 0, 0)),
        ],
        [
            pl.BlockSpec((1, length, BLK), lambda s, b: (of(s), 0, b)),
            pl.BlockSpec((SLOTS, 8, TAIL), lambda s, b: (0, 0, 0)),
            pl.BlockSpec((1, 8, BLK), lambda s, b: (of(s), 0, b)),
            pl.BlockSpec((1, 8, LANES), lambda s, b: (of(s), 0, 0)),
        ],
        [
            jax.ShapeDtypeStruct((SLOTS, length, TAIL), bf16),
            jax.ShapeDtypeStruct((SLOTS, 8, TAIL), f32),
            jax.ShapeDtypeStruct((SLOTS, 8, TAIL), f32),
            jax.ShapeDtypeStruct((SLOTS, 8, LANES), f32),
        ],
        (proj, edge, taps, proj, edge, taps, raw, heads, skip_row, dy, state, local, decay, cum, size, act),
        scratch=[
            pltpu.VMEM((length + 8, BLK), f32),
            pltpu.VMEM((length + 8, MAPS), f32),
            pltpu.VMEM((length, length), f32),
            pltpu.VMEM((length, length), f32),
            pltpu.VMEM((16 * HEADS, length), bf16),
            pltpu.VMEM((16 * HEADS, length), bf16),
            pltpu.VMEM((6 * length, LANES), bf16),
            pltpu.VMEM((length + 16, BLK), f32),
            pltpu.VMEM((length + 16, MAPS), f32),
            pltpu.VMEM((length, 2 * NSTATE), f32),
            pltpu.VMEM((length, LANES), f32),
            pltpu.VMEM((length, LANES), f32),
            pltpu.VMEM((LANES, length), f32),
            pltpu.VMEM((8, LANES), f32),
        ]
        + relay.scratch
        + border.scratch,
        cost=(2 * 10**10, 2 * 10**7, 10**7),
        carry=carry,
        identity=identity,
        relay=True,
    )


def unproject_gate_kernel(grads_ref, w_ref, normed_ref, back_ref, w_out_ref, turned):
    step = pl.program_id(0)

    @pl.when(step == 0)
    def _():
        turned[...] = normed_ref[...].T

    w_out_ref[...] = dot(turned[...], grads_ref[...]).astype(bf16)
    product = dot_nt(grads_ref[...], w_ref[...])

    @pl.when(step == 0)
    def _():
        back_ref[...] = product

    @pl.when(step > 0)
    def _():
        back_ref[...] += product


def unproject_gate(grads, weight, normed, carry=None, identity=None):
    rows = normed.shape[0]
    return launch(
        unproject_gate_kernel,
        "unproject_gate",
        (INNER // COLS,),
        [
            pl.BlockSpec((rows, COLS), lambda n: (0, n)),
            pl.BlockSpec((D, COLS), lambda n: (0, n)),
            pl.BlockSpec((rows, D), lambda n: (0, 0)),
        ],
        [pl.BlockSpec((rows, D), lambda n: (0, 0)), pl.BlockSpec((D, COLS), lambda n: (0, n))],
        [jax.ShapeDtypeStruct((rows, D), f32), jax.ShapeDtypeStruct((D, INNER), bf16)],
        (grads, weight, normed),
        scratch=[pltpu.VMEM((D, rows), bf16)],
        cost=(4 * rows * D * INNER, 4 * D * INNER, 0),
        carry=carry,
        identity=identity,
    )


def unproject_kernel(
    grads_ref, late_ref, w_ref, normed_ref, h_ref, g_ref, gain_ref, back_ref,
    out_ref, gain_out_ref, w_out_ref,
    total, turned, mended,
):
    step = pl.program_id(0)
    rows = h_ref.shape[0]
    length = rows // SLOTS

    @pl.when(step == 0)
    def _():
        total[...] = back_ref[...]
        turned[...] = normed_ref[...].T

    mended[...] = grads_ref[...]
    for slot in range(SLOTS):
        span = slice((slot + 1) * length - 16, (slot + 1) * length)
        extra = jnp.concatenate([jnp.zeros((8, COLS), f32), late_ref[slot]], axis=0)
        mended[span, :] = (grads_ref[span, :].astype(f32) + extra).astype(bf16)
    w_out_ref[...] = dot(turned[...], mended[...]).astype(bf16)
    total[...] += dot_nt(mended[...], w_ref[...])

    @pl.when(step == pl.num_programs(0) - 1)
    def _():
        gain_out_ref[...] = jnp.zeros_like(gain_out_ref)

        def one(span):
            h = h_ref[span, :]
            inverse = lax.rsqrt(jnp.mean(h * h, axis=-1, keepdims=True) + epsilon)
            back = total[span, :]
            unit = h * inverse
            gain_out_ref[0:1, :] += jnp.sum(back * unit, axis=0, keepdims=True)
            wanted = back * gain_ref[...]
            mean = jnp.mean(unit * wanted, axis=-1, keepdims=True)
            out_ref[span, :] = g_ref[span, :] + inverse * (wanted - unit * mean)

        for_rows(rows, 32, one)


def unproject(grads, late, weight, normed, h, g, gain_row, back, carry=None, identity=None):
    rows = h.shape[0]
    return launch(
        unproject_kernel,
        "unproject",
        (TAIL // COLS,),
        [
            pl.BlockSpec((rows, COLS), lambda n: (0, n)),
            pl.BlockSpec((SLOTS, 8, COLS), lambda n: (0, 0, n)),
            pl.BlockSpec((D, COLS), lambda n: (0, n)),
            pl.BlockSpec((rows, D), lambda n: (0, 0)),
            pl.BlockSpec((rows, D), lambda n: (0, 0)),
            pl.BlockSpec((rows, D), lambda n: (0, 0)),
            pl.BlockSpec((1, D), lambda n: (0, 0)),
            pl.BlockSpec((rows, D), lambda n: (0, 0)),
        ],
        [
            pl.BlockSpec((rows, D), lambda n: (0, 0)),
            pl.BlockSpec((8, D), lambda n: (0, 0)),
            pl.BlockSpec((D, COLS), lambda n: (0, n)),
        ],
        [
            jax.ShapeDtypeStruct((rows, D), f32),
            jax.ShapeDtypeStruct((8, D), f32),
            jax.ShapeDtypeStruct((D, TAIL), bf16),
        ],
        (grads, late, weight, normed, h, g, gain_row, back),
        scratch=[
            pltpu.VMEM((rows, D), f32),
            pltpu.VMEM((D, rows), bf16),
            pltpu.VMEM((rows, COLS), bf16),
        ],
        cost=(4 * rows * D * TAIL, 4 * D * TAIL, 0),
        carry=carry,
        identity=identity,
    )


MESH = pl.DeviceIdType.MESH
ANY = pl.BlockSpec(memory_space=pl.ANY)
DP_BITS = {"core": 1, "x": 2, "y": 4}
STEPS = ("z1", "z2", "x", "y", "core")


def place():
    dp, z = lax.axis_index("dp"), lax.axis_index("seq")
    return {"y": dp // 4, "x": lax.rem(dp // 2, 2), "core": lax.rem(dp, 2), "z": z, "dp": dp}


def partner(here, step):
    if step == "z1":
        return (here["dp"], here["z"] + 1 - 2 * lax.rem(here["z"], 2))
    if step == "z2":
        return (here["dp"], here["z"] + 2 - 4 * (here["z"] // 2))
    if step == "middle":
        return (here["dp"], 3 - here["z"])
    return (here["dp"] + DP_BITS[step] * (1 - 2 * here[step]), here["z"])


def greet(here, along=False):
    peers = STEPS + ("middle",) if along else STEPS
    barrier = pltpu.get_barrier_semaphore()
    for step in peers:
        pl.semaphore_signal(barrier, inc=1, device_id=partner(here, step), device_id_type=MESH)
    pl.semaphore_wait(barrier, len(peers))


class Exchange:
    def __init__(self, shapes, split, pace):
        self.shapes, self.pace = shapes, pace
        self.jobs, self.waves = [], []
        for index, (rows, columns) in enumerate(shapes):
            parts, pieces = split[index]
            height, width = rows // parts, columns // pieces
            for part in range(parts):
                for piece in range(pieces):
                    if piece % 2 == 0:
                        self.waves.append([])
                    job = (index, piece % 2, part * height, height, piece * width, width)
                    self.jobs.append(job)
                    self.waves[-1].append(job)

    def plan(self):
        last = len(self.waves) - 1 + self.pace * len(STEPS)
        ticks = [[] for _ in range(last + 1)]
        for stage in reversed(range(len(STEPS) + 1)):
            for wave, jobs in enumerate(self.waves):
                ticks[wave + self.pace * stage] += [(stage, job) for job in jobs]
        return ticks


class Gather(Exchange):
    def __init__(self, shards, split, pace):
        super().__init__(tuple(shard.shape for shard in shards), split, pace)
        self.shards, self.wholes = list(shards), {}
        self.entries = self.plan()

    def done(self, index):
        return max(t for t, entries in enumerate(self.entries) for _, job in entries if job[0] == index)

    def whole(self, index):
        found = self.wholes[index]
        return found.reshape(-1, found.shape[-1])

    def until(self, last):
        first = getattr(self, "reached", 0)
        self.reached = last + 1
        return Run(self, first, last)


class Run:
    def __init__(self, gather, first, last):
        self.gather = gather
        self.entries = gather.entries[first : last + 1]
        live = sorted({job[0] for entries in self.entries for stage, job in entries if stage < len(STEPS)})
        self.live = live
        self.fresh = [index for index in live if index not in gather.wholes]
        self.old = [index for index in live if index in gather.wholes]
        needed = {job[0] for entries in self.entries for stage, job in entries if stage == 0}
        self.sources = sorted(needed | set(self.fresh))
        self.args = [gather.shards[i] for i in self.sources] + [gather.wholes[i] for i in self.old]
        self.in_specs = [ANY] * len(self.args)
        self.out_specs = [ANY] * len(live)
        self.out_shape = [
            jax.ShapeDtypeStruct((2, 2, 2, 4) + gather.shapes[i], gather.shards[i].dtype) for i in live
        ]
        self.aliases = {len(self.sources) + k: live.index(i) for k, i in enumerate(self.old)}
        self.started = [
            (stage, job) for entries in self.entries for stage, job in entries if stage < len(STEPS)
        ]
        self.scratch = [
            pltpu.SemaphoreType.DMA((max(1, len(self.fresh)),)),
            pltpu.SemaphoreType.DMA((len(self.started),)),
            pltpu.SemaphoreType.DMA((len(self.started),)),
        ]

    def results(self, wholes):
        for index, whole in zip(self.live, wholes):
            self.gather.wholes[index] = whole
        return None

    def ticks(self, ins, outs, scratch, along=False):
        local_sems, send_sems, recv_sems = scratch
        here = place()
        shards = dict(zip(self.sources, ins))
        wholes = dict(zip(self.live, outs))
        own = [
            pltpu.make_async_copy(
                shards[i], wholes[i].at[here["y"], here["x"], here["core"], here["z"]], local_sems.at[k]
            )
            for k, i in enumerate(self.fresh)
        ]

        def make(stage, job):
            index, colour, top, height, left, width = job
            order = ("z1", "z2", "x", "y", "core") if colour == 0 else ("z1", "z2", "y", "x", "core")
            done = order[:stage]
            axis = lambda name: slice(None) if name in done else here[name]
            depth = here["z"]
            if "z2" in done:
                depth = slice(None)
            elif "z1" in done:
                depth = pl.ds(here["z"] // 2 * 2, 2)
            rows, columns = pl.ds(top, height), pl.ds(left, width)
            target = wholes[index].at[axis("y"), axis("x"), axis("core"), depth, rows, columns]
            source = shards[index].at[rows, columns] if stage == 0 else target
            number = self.started.index((stage, job))
            return pltpu.make_async_remote_copy(
                src_ref=source,
                dst_ref=target,
                send_sem=send_sems.at[number],
                recv_sem=recv_sems.at[number],
                device_id=partner(here, order[stage]),
                device_id_type=MESH,
            )

        ended = set()

        def steps(number, entries):
            actions = []
            if number == 0:
                actions.append(lambda: greet(here, along))
                actions += [copy.start for copy in own]
            if number == 1:
                actions += [copy.wait for copy in own]
            for stage, job in entries:
                before = (stage - 1, job)
                if before in self.started:
                    actions.append(lambda before=before: make(*before).wait())
                    ended.add(before)
                if stage < len(STEPS):
                    actions.append(lambda stage=stage, job=job: make(stage, job).start())
            return actions

        lists = [steps(number, entries) for number, entries in enumerate(self.entries)]
        last = [lambda key=key: make(*key).wait() for key in self.started if key not in ended]
        if len(lists) == 1:
            last = [copy.wait for copy in own] + last
        lists.append(last)

        def run(actions):
            for action in actions:
                action()

        return [functools.partial(run, actions) for actions in lists]


class Reduce(Exchange):
    def __init__(self, partials, split, pace=2, heads=None):
        super().__init__(tuple(partial.shape[1:] for partial in partials), split, pace)
        self.heads = heads is not None
        self.aliases = {}
        self.args = [partial.reshape((2, 2, 2, 4) + partial.shape[1:]) for partial in partials]
        count, number = len(partials), len(self.jobs)
        self.in_specs = [ANY] * count
        outs = list(self.shapes)
        if self.heads:
            self.args.append(heads)
            self.in_specs.append(pl.BlockSpec(heads.shape, lambda *_: (0, 0)))
            outs.append(heads.shape)
        self.out_specs = [pl.BlockSpec(shape, lambda *_: (0, 0)) for shape in outs]
        self.out_shape = [jax.ShapeDtypeStruct(shape, f32) for shape in outs]
        kept, landed = [], [[] for _ in STEPS]
        for index, _, _, height, _, width in self.jobs:
            kind = partials[index].dtype
            kept.append(pltpu.VMEM((2, 2, 4, height, width), kind))
            for stage, lead in enumerate(((2, 2, 4), (2, 4), (4,), (2,), ())):
                landed[stage].append(pltpu.VMEM(lead + (height, width), kind))
        tile = pltpu.SemaphoreType.DMA((number, len(STEPS)))
        self.scratch = kept + sum(landed, []) + [pltpu.SemaphoreType.DMA((number,)), tile, tile]
        if self.heads:
            line = pltpu.SemaphoreType.DMA((len(STEPS),))
            self.scratch += [pltpu.VMEM((len(STEPS),) + heads.shape, f32), line, line]

    def results(self, totals):
        return list(totals)

    def ticks(self, partials, totals, scratch, along=False):
        jobs, number, stages = self.jobs, len(self.jobs), len(STEPS)
        kept, landed = scratch[:number], scratch[number : 6 * number]
        local_sems, send_sems, recv_sems = scratch[6 * number : 6 * number + 3]
        here = place()
        y, x, core, z = here["y"], here["x"], here["core"], here["z"]
        half, odd = z // 2, lax.rem(z, 2)

        def order(job):
            return ("core", "y", "x", "z2", "z1") if job[1] == 0 else ("core", "x", "y", "z2", "z1")

        def leaving(job, stage):
            if stage == 1:
                return (1 - y, slice(None), slice(None)) if job[1] == 0 else (slice(None), 1 - x, slice(None))
            if stage == 2:
                return (y, 1 - x, slice(None)) if job[1] == 0 else (1 - y, x, slice(None))
            if stage == 3:
                return (y, x, pl.ds((1 - half) * 2, 2))
            return (y, x, half * 2 + 1 - odd)

        def cut(job, side):
            index, _, top, height, left, width = job
            return partials[index].at[:, :, side, :, pl.ds(top, height), pl.ds(left, width)]

        def load(job):
            k = jobs.index(job)
            return pltpu.make_async_copy(cut(job, core), kept[k], local_sems.at[k])

        def make(job, stage):
            k = jobs.index(job)
            return pltpu.make_async_remote_copy(
                src_ref=cut(job, 1 - core) if stage == 0 else kept[k].at[leaving(job, stage)],
                dst_ref=landed[stage * number + k],
                send_sem=send_sems.at[k, stage],
                recv_sem=recv_sems.at[k, stage],
                device_id=partner(here, order(job)[stage]),
                device_id_type=MESH,
            )

        def add(job, stage, mine):
            k = jobs.index(job)
            into, came = kept[k], landed[(stage - 1) * number + k]
            pick = lambda value: value if mine else 1 - value
            first = job[1] == 0

            def accumulate(target, source):
                into[target] = (into[target].astype(f32) + came[source].astype(f32)).astype(into.dtype)

            if stage == 1:
                def one(i, carry):
                    a, b = i // 4, lax.rem(i, 4)
                    where = (pick(y), a, b) if first else (a, pick(x), b)
                    accumulate(where, where)
                    return carry

                lax.fori_loop(0, 8, one, 0)
            elif stage == 2:
                def one(b, carry):
                    if first:
                        accumulate((y, pick(x), b), (pick(x), b))
                    else:
                        accumulate((pick(y), x, b), (pick(y), b))
                    return carry

                lax.fori_loop(0, 4, one, 0)
            elif stage == 3:
                for b in range(2):
                    accumulate((y, x, pick(half) * 2 + b), (pick(half) * 2 + b,))
            else:
                accumulate((y, x, half * 2 + pick(odd)), (pick(odd),))

        def finish(job):
            index, _, top, height, left, width = job
            k = jobs.index(job)
            summed = kept[k][y, x, z].astype(f32) + landed[4 * number + k][...].astype(f32)
            totals[index][top : top + height, left : left + width] = summed

        def heads_copy(stage):
            heads_landed, head_send, head_recv = scratch[6 * number + 3 :]
            return pltpu.make_async_remote_copy(
                src_ref=totals[-1],
                dst_ref=heads_landed.at[stage],
                send_sem=head_send.at[stage],
                recv_sem=head_recv.at[stage],
                device_id=partner(here, STEPS[stage]),
                device_id_type=MESH,
            )

        def tick(moment, entries):
            if moment == 0:
                greet(here, along)
                if self.heads:
                    totals[-1][...] = partials[-1][...]
            if self.heads and 0 < moment <= stages:
                heads_copy(moment - 1).wait()
                totals[-1][...] = totals[-1][...] + scratch[6 * number + 3][moment - 1]
            if self.heads and moment < stages:
                heads_copy(moment).start()
            for stage, job in entries:
                if stage == 0:
                    make(job, 0).start()
                    load(job).start()
                    continue
                if stage == 1:
                    load(job).wait()
                make(job, stage - 1).wait()
                if stage == stages:
                    finish(job)
                else:
                    add(job, stage, False)
                    make(job, stage).start()
                    add(job, stage, True)

        return [functools.partial(tick, moment, entries) for moment, entries in enumerate(self.plan())]


def alone(exchange, name, identity):
    ins, outs = len(exchange.in_specs), len(exchange.out_specs)

    def kernel(*refs):
        for tick in exchange.ticks(refs[:ins], refs[ins : ins + outs], refs[ins + outs :]):
            tick()

    found = pl.pallas_call(
        kernel,
        name=name,
        grid=(1,),
        in_specs=exchange.in_specs,
        out_specs=exchange.out_specs,
        out_shape=exchange.out_shape,
        scratch_shapes=exchange.scratch,
        input_output_aliases=exchange.aliases,
        compiler_params=params(collective_id=identity, has_side_effects=True),
    )(*exchange.args)
    return exchange.results(found)


def spaced(first, last, weights):
    marks, sum_so_far = [], 0
    for weight in weights:
        sum_so_far += weight
        marks.append(first + (last - first) * sum_so_far // sum(weights))
    return marks


def padded_rows(array, rows):
    return jnp.pad(array, ((0, rows - array.shape[0]), (0, 0)))


def pack_small(norm_gain, conv_weight, gate_gain):
    pieces = [norm_gain, conv_weight.reshape(LAYERS, -1), gate_gain]
    flat = jnp.concatenate(pieces, axis=1).reshape(-1)
    size = flat.shape[0]
    tiles = -(-size // (16 * LANES)) * 16
    return jnp.pad(flat, (0, tiles * LANES - size)).reshape(tiles, LANES)


def unpack_small(everything, norm_gain, conv_weight, gate_gain):
    count = everything.shape[0]
    size = LAYERS * (norm_gain.shape[1] + conv_weight.shape[1] * conv_weight.shape[2] + gate_gain.shape[1])
    everything = everything.reshape(count, -1)[:, :size].reshape(count, LAYERS, -1)
    everything = jnp.swapaxes(everything, 0, 1).astype(f32)
    first = norm_gain.shape[1]
    second = first + conv_weight.shape[1] * conv_weight.shape[2]
    norm = everything[..., :first].reshape(LAYERS, -1)
    conv = everything[..., first:second].reshape(LAYERS, count, CONV, -1)
    conv = jnp.swapaxes(conv, 1, 2).reshape(LAYERS, CONV, -1)
    gate = everything[..., second:].reshape(LAYERS, -1)
    return norm, conv, gate


def share_small(norm, conv, gate):
    count = lax.axis_size("dp") * lax.axis_size("seq")
    conv = jnp.swapaxes(conv.reshape(LAYERS, CONV, count, -1), 1, 2).reshape(LAYERS, count, -1)
    pieces = [norm.reshape(LAYERS, count, -1), conv, gate.reshape(LAYERS, count, -1)]
    flat = jnp.swapaxes(jnp.concatenate(pieces, axis=-1), 0, 1).reshape(count, -1)
    size = flat.shape[1]
    tiles = -(-size // (16 * LANES)) * 16
    return jnp.pad(flat, ((0, 0), (0, tiles * LANES - size))).reshape(count, tiles, LANES)


def own_small(mine, norm_gain, conv_weight, gate_gain):
    first = norm_gain.shape[1]
    second = first + conv_weight.shape[1] * conv_weight.shape[2]
    width = second + gate_gain.shape[1]
    mine = mine.reshape(-1)[: LAYERS * width].reshape(LAYERS, width)
    return mine[:, :first], mine[:, first:second].reshape(LAYERS, CONV, -1), mine[:, second:]


def body(
    hidden,
    out_grad,
    lengths,
    norm_gain,
    in_proj,
    conv_weight,
    gate_gain,
    out_proj,
    dt_bias,
    a_log,
    d_skip,
):
    length = hidden.shape[1]
    rows = SLOTS * length
    count = 1 if length >= SHORT else SLOTS
    swap = lengths[0] < lengths[1]

    def ordered(array):
        return jnp.where(swap, array[::-1], array)

    positions = lax.axis_index("seq") * length + jnp.arange(length, dtype=jnp.int32)
    valid = (positions[None, :] < ordered(lengths)[:, None]).astype(f32).reshape(rows, 1)
    valid = jnp.broadcast_to(valid, (rows, LANES))
    gates = in_proj[..., :INNER]
    tails = jnp.pad(in_proj[..., INNER:], ((0, 0), (0, 0), (0, TAIL - (PROJ - INNER))))
    ours = lax.axis_size("dp") == 8 and lax.axis_size("seq") == 4
    packed = pack_small(norm_gain, conv_weight, gate_gain)
    shards = [packed]
    for layer in range(LAYERS):
        shards += [tails[layer], gates[layer], out_proj[layer]]
    ids = iter(range(100))
    if ours:
        moving = Gather(shards, [(1, 1)] + [(3, 2)] * (3 * LAYERS), 1)
        tail_done, gate_done, out_done = [[moving.done(1 + 3 * layer + k) for layer in range(LAYERS)] for k in range(3)]
        end = len(moving.entries) - 1
        run = lambda last: moving.until(min(last, end)) if min(last, end) >= moving.reached else None
        alone(moving.until(tail_done[0]), "gather", next(ids))
        everything = moving.wholes[0].reshape((-1,) + packed.shape)
        whole = moving.whole
    else:
        gathered = [lax.all_gather(shard, ("dp", "seq"), axis=0, tiled=True) for shard in shards]
        everything = gathered[0].reshape((-1,) + packed.shape)
        whole = lambda index: gathered[index]
        run = lambda last: None
        tail_done = gate_done = out_done = [0] * LAYERS
    norm_all, conv_all, gate_all = unpack_small(everything, norm_gain, conv_weight, gate_gain)
    h = ordered(hidden).reshape(rows, D)
    kept = []
    for layer in range(LAYERS):
        gain_row = norm_all[layer].reshape(1, D)
        gate_row = gate_all[layer].reshape(1, INNER)
        taps = jnp.pad(conv_all[layer], ((0, 8 - CONV), (0, TAIL - CONVCH)))
        heads = padded_rows(
            jnp.pad(
                jnp.stack([dt_bias[layer], a_log[layer]]), ((0, 0), (0, LANES - HEADS))
            ),
            8,
        )
        skip_row = jnp.repeat(d_skip[layer], HEADDIM).reshape(1, INNER)
        base = 1 + 3 * layer
        more = tail_done[layer + 1] if layer + 1 < LAYERS else out_done[layer]
        marks = spaced(tail_done[layer], more, (16, 30, 11, 30) if layer + 1 < LAYERS else (18, 30, 11, 0))
        marks[1] = max(marks[1], gate_done[layer])
        marks[2] = max(marks[2], out_done[layer])
        proj, raw, normed, edge, *_ = project(h, gain_row, whole(base), run(marks[0]), next(ids))
        cube = proj.reshape(SLOTS, length, TAIL)
        raw = raw.reshape(SLOTS, length, LANES)
        y, state, cum, size, act, decay, *_ = mix(
            cube, edge, taps, raw, heads, skip_row, count, run(marks[1]), next(ids)
        )
        state = state.reshape(count, NB, NSTATE, BLK)
        gate, *_ = project_gate(normed, whole(base + 1), run(marks[2]), next(ids))
        flat = lambda array: array.reshape(rows, -1)
        h_next, mixture, inverse, *_ = branch(
            flat(y), gate, flat(act), flat(cum), state, gate_row, whole(base + 2), h, valid, run(marks[3]), next(ids)
        )
        kept.append(
            (h, gain_row, gate_row, taps, heads, skip_row, proj, gate, raw, normed, edge, cum, size, act,
             decay, state, mixture, inverse, whole(base), whole(base + 1), whole(base + 2))
        )
        h = h_next
    result = ordered(h.reshape(SLOTS, length, D))

    g = ordered(out_grad).reshape(rows, D)
    small = [None] * LAYERS
    partials = [None] * LAYERS
    totals = [[None] * 3 for _ in range(LAYERS)]
    waiting = None
    cut = lambda partial: partial.reshape(lax.axis_size("dp") * lax.axis_size("seq"), -1, partial.shape[-1])

    def summing(arrays):
        if not ours or arrays[0] is None:
            return None
        return Reduce([cut(array) for array in arrays], [(3, 4)] * len(arrays), 2)

    for layer in reversed(range(LAYERS)):
        (h, gain_row, gate_row, taps, heads, skip_row, proj, gate, raw, normed, edge, cum, size, act,
         decay, state, mixture, inverse, weight_tail, weight_gate, weight_out) = kept[layer]
        cube = proj.reshape(SLOTS, length, TAIL)
        flat = lambda array: array.reshape(rows, -1)
        shaped = lambda array: array.reshape(SLOTS, length, -1)
        back, mean, grad_gate, partial_out, *sums = unbranch(
            g, valid, mixture, gate, inverse, gate_row, weight_out, summing([waiting]), next(ids)
        )
        if waiting is not None and ours:
            totals[layer + 1][0] = sums[0][0]
        dy, grads, local = ungate(back, mixture, gate, inverse, mean, gate_row, flat(act), flat(cum), count)
        back, partial_gate = unproject_gate(grads, weight_gate, normed)
        grads, late, grad_taps, grad_heads, *sums = unmix(
            cube, edge, taps, raw, heads, skip_row, shaped(dy), state, local, decay, cum, size, act, count,
            summing([partial_gate, partial_out]), next(ids),
        )
        if ours:
            totals[layer][1], totals[layer][2] = sums[0]
        g, grad_norm, waiting = unproject(flat(grads), late, weight_tail, normed, h, g, gain_row, back)
        partials[layer] = (waiting, partial_gate, partial_out)
        small[layer] = (
            grad_norm[0], jnp.sum(grad_taps, axis=0)[:CONV, :CONVCH], grad_gate[0],
            jnp.sum(grad_heads, axis=0)[:3, :HEADS],
        )
    grad_hidden = ordered(g.reshape(SLOTS, length, D))
    stacked = [jnp.stack([small[layer][member] for layer in range(LAYERS)]) for member in range(4)]
    shares = share_small(*stacked[:3])
    head_sums = jnp.pad(stacked[3].reshape(-1, HEADS), ((0, 8 - 3 * LAYERS), (0, LANES - HEADS)))
    if ours:
        totals[0][0], mine, head_sums = alone(
            Reduce([cut(waiting), shares], [(3, 2), (1, 1)], heads=head_sums), "reduce", next(ids)
        )
    else:
        totals = [
            [
                lax.optimization_barrier(
                    lax.psum_scatter(partial, ("dp", "seq"), scatter_dimension=0, tiled=True)
                ).astype(f32)
                for partial in members
            ]
            for members in partials
        ]
        mine = lax.psum_scatter(shares, ("dp", "seq"), scatter_dimension=0, tiled=True)
        head_sums = lax.psum(head_sums, ("dp", "seq"))
    grad_norm, grad_conv, grad_gate = own_small(mine, norm_gain, conv_weight, gate_gain)
    grad_heads = head_sums[: 3 * LAYERS, :HEADS].reshape(LAYERS, 3, HEADS)
    return (
        result,
        grad_hidden,
        grad_norm,
        jnp.stack([jnp.concatenate([gate, tail[:, : PROJ - INNER]], axis=1) for tail, gate, _ in totals]),
        grad_conv,
        grad_gate,
        jnp.stack([members[2] for members in totals]),
        grad_heads[:, 0],
        grad_heads[:, 1],
        grad_heads[:, 2],
    )


def solution(mesh):
    tokens = P("dp", "seq", None)
    every = ("dp", "seq")
    weights = (P(None, every), P(None, every, None), P(None, None, every), P(None, every), P(None, every, None))
    return jax.shard_map(
        body,
        mesh=mesh,
        in_specs=(tokens, tokens, P("dp")) + weights + (P(), P(), P()),
        out_specs=(tokens, tokens) + weights + (P(), P(), P()),
        check_vma=False,
    )
```

```python
import functools

import jax
import jax.numpy as jnp
from jax import lax
from jax.experimental import pallas as pl
from jax.experimental.pallas import tpu as pltpu
from jax.sharding import PartitionSpec as P

D = 1536
HEADS = 48
HEADDIM = 64
NSTATE = 128
CONV = 4
LAYERS = 2
INNER = 3072
CONVCH = 3328
PROJ = 6448
SLOTS = 2
SHORT = 256

LANES = 128
TAIL = 3584
BLK = 512
MAPS = 2 * NSTATE
NB = INNER // BLK
COLS = 512
PER = BLK // HEADDIM

f32 = jnp.float32
bf16 = jnp.bfloat16
epsilon = 1e-05
VMEM_LIMIT = 60 << 20


def launch(
    kernel, name, grid, in_specs, out_specs, out_shape, args, scratch=(), cost=None, carry=None, identity=None,
    relay=False,
):
    options = {"compiler_params": params()}
    if cost is not None:
        options["cost_estimate"] = pl.CostEstimate(flops=cost[0], bytes_accessed=cost[1], transcendentals=cost[2])
    if carry is not None or relay:
        options["compiler_params"] = params(collective_id=identity, has_side_effects=True)
    if carry is None:
        return pl.pallas_call(
            kernel, name=name, grid=grid, in_specs=in_specs, out_specs=out_specs, out_shape=out_shape,
            scratch_shapes=list(scratch), **options,
        )(*args)
    sizes = [len(in_specs), len(carry.in_specs), len(out_specs), len(carry.out_specs), len(scratch)]
    if carry.aliases:
        options["input_output_aliases"] = {sizes[0] + i: sizes[2] + o for i, o in carry.aliases.items()}

    def wrapped(*refs):
        groups, at = [], 0
        for size in sizes:
            groups.append(refs[at : at + size])
            at += size
        step, total = 0, 1
        for axis, extent in enumerate(grid):
            step, total = step * extent + pl.program_id(axis), total * extent
        ticks = carry.ticks(groups[1], groups[3], refs[at:], relay)
        plan = {}
        for number, tick in enumerate(ticks[:-1]):
            plan.setdefault(number * total // (len(ticks) - 1), []).append(tick)
        for moment, members in plan.items():
            @pl.when(step == moment)
            def _(members=members):
                for member in members:
                    member()

        kernel(*groups[0], *groups[2], *groups[4])

        @pl.when(step == total - 1)
        def _():
            ticks[-1]()

    found = pl.pallas_call(
        wrapped, name=name, grid=grid, in_specs=list(in_specs) + carry.in_specs,
        out_specs=list(out_specs) + carry.out_specs, out_shape=list(out_shape) + carry.out_shape,
        scratch_shapes=list(scratch) + carry.scratch, **options,
    )(*args, *carry.args)
    return list(found[: sizes[2]]) + [carry.results(found[sizes[2] :])]


def params(**more):
    return pltpu.CompilerParams(vmem_limit_bytes=VMEM_LIMIT, **more)


def for_rows(total, size, function):
    def step(index, carry):
        function(pl.ds(pl.multiple_of(index * size, size), size))
        return carry

    lax.fori_loop(0, total // size, step, 0)


def dot(left, right):
    return jnp.dot(left, right, preferred_element_type=f32)


def dot_nt(left, right):
    return lax.dot_general(left, right, (((1,), (1,)), ((), ())), preferred_element_type=f32)


def dot_tn(left, right):
    return lax.dot_general(left, right, (((0,), (0,)), ((), ())), preferred_element_type=f32)


def dot_exact(left, right):
    return jnp.dot(left, right, preferred_element_type=f32, precision=lax.Precision.HIGHEST)


def halves(array):
    high = array.astype(bf16)
    return high, (array - high.astype(f32)).astype(bf16)


def dot_halves(left, right, product=dot):
    left_high, left_low = left
    right_high, right_low = right
    return product(left_high, right_high) + product(left_high, right_low) + product(left_low, right_high)


def dot_member(array, member):
    high, low = halves(array)
    return dot(high, member) + dot(low, member)


def sigmoid(vector):
    return 0.5 + 0.5 * jnp.tanh(0.5 * vector)


def softplus(vector):
    return jnp.maximum(vector, 0.0) + jnp.log1p(jnp.exp(-jnp.abs(vector)))


def spread(columns):
    length = columns.shape[0]
    return jnp.concatenate(
        [jnp.broadcast_to(columns[:, j : j + 1], (length, HEADDIM)) for j in range(PER)], axis=1
    )


def heads_first(columns, block):
    return pltpu.roll(columns, lax.rem(LANES - PER * block, LANES), 1)


def fold(array):
    return functools.reduce(jnp.add, [array[:, at : at + LANES] for at in range(0, array.shape[1], LANES)])


def expander(block):
    head = lax.broadcasted_iota(jnp.int32, (LANES, BLK), 0)
    mine = lax.broadcasted_iota(jnp.int32, (LANES, BLK), 1) // HEADDIM + block * PER
    return (head == mine).astype(bf16)


def stack_halves(scratch, arrays):
    length = arrays[0].shape[0]
    for number, array in enumerate(arrays):
        high, low = halves(array)
        scratch[2 * number * length : (2 * number + 1) * length, :] = high
        scratch[(2 * number + 1) * length : (2 * number + 2) * length, :] = low


def spread_all(scratch, block, length):
    wide = dot(scratch[...], expander(block))
    return [
        wide[at : at + length] + wide[at + length : at + 2 * length] for at in range(0, wide.shape[0], 2 * length)
    ]


def split_rows(cum_t, minus, plus):
    rows, length = HEADS, cum_t.shape[1]
    first = cum_t[:rows].astype(bf16).astype(f32)
    rest = cum_t[:rows] - first
    second = rest.astype(bf16).astype(f32)
    third = rest - second
    index = lax.broadcasted_iota(jnp.int32, (rows, 16, length), 1)
    wide = lambda array: jnp.broadcast_to(array[:, None, :], (rows, 16, length))

    def pick(offset, sign, ones):
        found = jnp.where(jnp.logical_and(index >= ones, index < ones + 3), 1.0, 0.0)
        for number, part in enumerate((first, second, third)):
            found = jnp.where(index == offset + number, wide(sign * part), found)
        return found.astype(bf16).reshape(rows * 16, length)

    minus[...] = pick(0, -1.0, 3)
    plus[...] = pick(3, 1.0, 0)


def head_pairs(array, pair):
    columns = array[:, pair * LANES : (pair + 1) * LANES]
    lane = lax.broadcasted_iota(jnp.int32, columns.shape, 1)
    zero = jnp.zeros_like(columns)
    return jnp.where(lane < HEADDIM, columns, zero), jnp.where(lane < HEADDIM, zero, columns)


def load_extended(scratch, edge_ref, rows_ref):
    scratch[0:8, :] = edge_ref[0]
    scratch[8:, :] = rows_ref[0]


def convolve(scratch, taps, length):
    total = taps[0:1] * scratch[5 : 5 + length, :]
    for k in range(1, CONV):
        total = total + taps[k : k + 1] * scratch[5 + k : 5 + k + length, :]
    return total


def lower(length):
    first = lax.broadcasted_iota(jnp.int32, (length, length), 0)
    second = lax.broadcasted_iota(jnp.int32, (length, length), 1)
    return first >= second


class Along:
    def __init__(self, steps, pieces, shape, kind):
        self.steps, self.pieces, self.shape, self.kind = steps, pieces, shape, kind
        self.scratch = [
            pltpu.VMEM((pieces + 1,) + shape, kind),
            pltpu.VMEM((pieces,) + shape, kind),
            pltpu.SemaphoreType.DMA((pieces,)),
            pltpu.SemaphoreType.DMA((pieces,)),
        ]

    def bind(self, landed, sent, send_sems, recv_sems):
        self.landed, self.sent, self.send_sems, self.recv_sems = landed, sent, send_sems, recv_sems
        self.me, last = lax.axis_index("seq"), lax.axis_size("seq") - 1
        ahead, behind = self.me < last, self.me > 0
        self.sends, self.receives = (ahead, behind) if self.steps > 0 else (behind, ahead)

    def peer(self, steps):
        return (lax.axis_index("dp"), self.me + steps)

    def greet(self):
        barrier = pltpu.get_barrier_semaphore()

        @pl.when(self.receives)
        def _():
            pl.semaphore_signal(barrier, inc=1, device_id=self.peer(-self.steps), device_id_type=pl.DeviceIdType.MESH)

        @pl.when(self.sends)
        def _():
            pl.semaphore_wait(barrier, 1)

    def open(self):
        self.landed[self.pieces] = jnp.zeros(self.shape, self.kind)

        @pl.when(jnp.logical_not(self.receives))
        def _():
            for piece in range(self.pieces):
                self.landed[piece] = jnp.zeros(self.shape, self.kind)

    def copy(self, piece):
        return pltpu.make_async_remote_copy(
            src_ref=self.sent.at[piece],
            dst_ref=self.landed.at[piece],
            send_sem=self.send_sems.at[piece],
            recv_sem=self.recv_sems.at[piece],
            device_id=self.peer(self.steps),
            device_id_type=pl.DeviceIdType.MESH,
        )

    def take(self, piece):
        @pl.when(self.receives)
        def _():
            self.copy(piece).wait_recv()

    def give(self, piece, value):
        @pl.when(self.sends)
        def _():
            self.sent[piece] = value()
            self.copy(piece).start()

    def grow(self, piece, local, decay):
        self.take(piece)
        self.give(piece, lambda: (decay * self.landed[piece].astype(f32) + local).astype(bf16))

    def close(self):
        @pl.when(self.sends)
        def _():
            for piece in range(self.pieces):
                self.copy(piece).wait_send()


def project_kernel(edge, alone, h_ref, gain_ref, w_ref, proj_ref, raw_ref, normed_ref, edge_ref, *flow):
    step = pl.program_id(0)
    total = h_ref.shape[0]
    length = total // SLOTS
    edge.bind(*flow)

    @pl.when(step == 0)
    def _():
        if alone:
            edge.greet()
        edge.open()

        def one(rows):
            h = h_ref[rows, :]
            inverse = lax.rsqrt(jnp.mean(h * h, axis=-1, keepdims=True) + epsilon)
            normed_ref[rows, :] = (h * inverse * gain_ref[...]).astype(bf16)

        for_rows(total, 32, one)

    product = dot(normed_ref[...], w_ref[...])
    proj_ref[...] = product
    for slot in range(SLOTS):
        edge.give(step * SLOTS + slot, lambda slot=slot: product[(slot + 1) * length - 8 : (slot + 1) * length])

    @pl.when(step == pl.num_programs(0) - 1)
    def _():
        raw_ref[...] = product[:, COLS - 2 * LANES : COLS - LANES]
        for piece in range(edge.pieces):
            edge.take(piece)
            number, slot = divmod(piece, SLOTS)
            edge_ref[slot, :, number * COLS : (number + 1) * COLS] = edge.landed[piece]
        edge.close()


def project(h, gain_row, weight, carry=None, identity=None):
    total = h.shape[0]
    edge = Along(1, SLOTS * (TAIL // COLS), (8, COLS), f32)
    return launch(
        functools.partial(project_kernel, edge, carry is None),
        "project",
        (TAIL // COLS,),
        [
            pl.BlockSpec((total, D), lambda n: (0, 0)),
            pl.BlockSpec((1, D), lambda n: (0, 0)),
            pl.BlockSpec((D, COLS), lambda n: (0, n)),
        ],
        [
            pl.BlockSpec((total, COLS), lambda n: (0, n)),
            pl.BlockSpec((total, LANES), lambda n: (0, 0)),
            pl.BlockSpec((total, D), lambda n: (0, 0)),
            pl.BlockSpec((SLOTS, 8, TAIL), lambda n: (0, 0, 0)),
        ],
        [
            jax.ShapeDtypeStruct((total, TAIL), f32),
            jax.ShapeDtypeStruct((total, LANES), f32),
            jax.ShapeDtypeStruct((total, D), bf16),
            jax.ShapeDtypeStruct((SLOTS, 8, TAIL), f32),
        ],
        (h, gain_row, weight),
        scratch=edge.scratch,
        cost=(2 * total * D * TAIL, 2 * D * TAIL, 0),
        carry=carry,
        identity=identity,
        relay=True,
    )


def mix_kernel(
    relay, alone, count, rows_ref, edge_ref, taps_ref, maps_ref, maps_edge_ref, maps_taps_ref, raw_ref, heads_ref, skip_ref,
    y_ref, state_ref, cum_ref, step_ref, act_ref, decay_ref,
    extended, maps_extended, inner, minus, plus, input_t, scales, local, decay, *flow,
):
    slot, block = pl.program_id(0), pl.program_id(1)
    number = slot * NB + block
    length = rows_ref.shape[1]
    relay.bind(*flow)

    @pl.when(number == 0)
    def _():
        if alone:
            relay.greet()
        relay.open()

    def grow(piece):
        relay.grow(piece, local[piece], decay[piece, 0:1, :])

    due = number - 1 - 2 * relay.me

    @pl.when(jnp.logical_and(due >= 0, due < NB))
    def _():
        grow(due)

    @pl.when(block == 0)
    def _():
        load_extended(maps_extended, maps_edge_ref, maps_ref)
        convolved = convolve(maps_extended, maps_taps_ref[...], length)
        maps = convolved * sigmoid(convolved)
        act_ref[0] = maps
        products = dot_halves(halves(maps[:, NSTATE:]), halves(maps[:, :NSTATE]), dot_nt)
        input_t[0], input_t[1] = halves(maps[:, :NSTATE].T)
        causal = lower(length)
        inner[...] = jnp.where(causal, products, 0.0)
        size = softplus(raw_ref[0] + heads_ref[0:1, :])
        decay = -size * jnp.exp(heads_ref[1:2, :])
        cum = dot_exact(causal.astype(f32), decay)
        cum_ref[0] = cum
        step_ref[0] = size
        split_rows(cum.T, minus, plus)
        stack_halves(scales, [size, jnp.exp(cum[length - 1 :, :] - cum)])

    load_extended(extended, edge_ref, rows_ref)
    convolved = convolve(extended, taps_ref[...], length)
    values = convolved * sigmoid(convolved)
    wide_step, remaining = spread_all(scales, block, length)
    stepped = values * wide_step
    low = stepped.astype(bf16)
    parts = []
    for pair in range(PER // 2):
        members = head_pairs(low, pair)
        pieces = []
        for first in range(0, length, LANES):
            end = first + LANES
            weights = []
            for j in range(2):
                rows = pl.ds(pl.multiple_of((block * PER + 2 * pair + j) * 16, 16), 16)
                change = dot_tn(plus[rows, first:end], minus[rows, :end])
                weights.append((inner[first:end, :end] * jnp.exp(jnp.minimum(change, 0.0))).astype(bf16))
            pieces.append(
                dot(jnp.concatenate(weights, axis=1), jnp.concatenate([member[:end] for member in members], axis=0))
            )
        parts.append(jnp.concatenate(pieces, axis=0))
    y_ref[0] = jnp.concatenate(parts, axis=1) + skip_ref[...] * values
    final = heads_first(cum_ref[0][length - 8 :, :], block)
    rate = jnp.broadcast_to(spread(jnp.exp(final))[7:], (8, BLK))
    decay_ref[0, 0] = rate

    @pl.when(slot < count)
    def _():
        local[number] = dot_halves((input_t[0], input_t[1]), halves(stepped * remaining))
        decay[number] = rate

    @pl.when(number == SLOTS * NB - 1)
    def _():
        for piece in range(relay.pieces):
            @pl.when(jnp.logical_or(piece >= NB, piece > due))
            def _():
                grow(piece)

            state_ref[piece] = relay.landed[piece]
        relay.close()


def mix(proj, edge, taps, raw, heads, skip_row, count, carry=None, identity=None):
    length = proj.shape[1]
    relay = Along(1, count * NB, (NSTATE, BLK), bf16)
    return launch(
        functools.partial(mix_kernel, relay, carry is None, count),
        "mix",
        (SLOTS, NB),
        [
            pl.BlockSpec((1, length, BLK), lambda s, b: (s, 0, b)),
            pl.BlockSpec((1, 8, BLK), lambda s, b: (s, 0, b)),
            pl.BlockSpec((8, BLK), lambda s, b: (0, b)),
            pl.BlockSpec((1, length, MAPS), lambda s, b: (s, 0, INNER // MAPS)),
            pl.BlockSpec((1, 8, MAPS), lambda s, b: (s, 0, INNER // MAPS)),
            pl.BlockSpec((8, MAPS), lambda s, b: (0, INNER // MAPS)),
            pl.BlockSpec((1, length, LANES), lambda s, b: (s, 0, 0)),
            pl.BlockSpec((8, LANES), lambda s, b: (0, 0)),
            pl.BlockSpec((1, BLK), lambda s, b: (0, b)),
        ],
        [
            pl.BlockSpec((1, length, BLK), lambda s, b: (s, 0, b)),
            pl.BlockSpec((count * NB, NSTATE, BLK), lambda s, b: (0, 0, 0)),
            pl.BlockSpec((1, length, LANES), lambda s, b: (s, 0, 0)),
            pl.BlockSpec((1, length, LANES), lambda s, b: (s, 0, 0)),
            pl.BlockSpec((1, length, MAPS), lambda s, b: (s, 0, 0)),
            pl.BlockSpec((1, 1, 8, BLK), lambda s, b: (s, b, 0, 0)),
        ],
        [
            jax.ShapeDtypeStruct((SLOTS, length, INNER), f32),
            jax.ShapeDtypeStruct((count * NB, NSTATE, BLK), bf16),
            jax.ShapeDtypeStruct((SLOTS, length, LANES), f32),
            jax.ShapeDtypeStruct((SLOTS, length, LANES), f32),
            jax.ShapeDtypeStruct((SLOTS, length, MAPS), f32),
            jax.ShapeDtypeStruct((SLOTS, NB, 8, BLK), f32),
        ],
        (proj, edge, taps, proj, edge, taps, raw, heads, skip_row),
        scratch=[
            pltpu.VMEM((length + 8, BLK), f32),
            pltpu.VMEM((length + 8, MAPS), f32),
            pltpu.VMEM((length, length), f32),
            pltpu.VMEM((16 * HEADS, length), bf16),
            pltpu.VMEM((16 * HEADS, length), bf16),
            pltpu.VMEM((2, NSTATE, length), bf16),
            pltpu.VMEM((4 * length, LANES), bf16),
            pltpu.VMEM((count * NB, NSTATE, BLK), f32),
            pltpu.VMEM((count * NB, 8, BLK), f32),
        ]
        + relay.scratch,
        cost=(6 * 10**9, 10**7, 10**7),
        carry=carry,
        identity=identity,
        relay=True,
    )


def project_gate_kernel(normed_ref, w_ref, gate_ref):
    gate_ref[...] = dot(normed_ref[...], w_ref[...])


def project_gate(normed, weight, carry=None, identity=None):
    total = normed.shape[0]
    return launch(
        project_gate_kernel,
        "project_gate",
        (INNER // COLS,),
        [pl.BlockSpec((total, D), lambda n: (0, 0)), pl.BlockSpec((D, COLS), lambda n: (0, n))],
        [pl.BlockSpec((total, COLS), lambda n: (0, n))],
        [jax.ShapeDtypeStruct((total, INNER), f32)],
        (normed, weight),
        cost=(2 * total * D * INNER, 2 * D * INNER, 0),
        carry=carry,
        identity=identity,
    )


def branch_kernel(
    y_ref, gate_ref, act_ref, cum_ref, state_ref, gain_ref, w_ref, h_ref, valid_ref,
    out_ref, mixture_ref, inverse_ref,
    total, squares, gated_low,
):
    block = pl.program_id(0)
    count = state_ref.shape[0]
    rows = y_ref.shape[0]
    length = rows // SLOTS

    @pl.when(block == 0)
    def _():
        total[...] = jnp.zeros_like(total)
        squares[...] = jnp.zeros_like(squares)

    for slot in range(SLOTS):
        span = slice(slot * length, (slot + 1) * length)
        mixture = y_ref[span, :]
        if slot < count:
            cum = heads_first(cum_ref[span, :], block)
            carried = dot_member(act_ref[span, NSTATE:], state_ref[slot, 0])
            mixture = mixture + carried * spread(jnp.exp(cum))
        gate = gate_ref[span, :]
        gated = mixture * gate * sigmoid(gate)
        mixture_ref[span, :] = mixture
        square = gated * gated
        squares[span, :] += fold(square)
        gated_low[span, :] = (gated * gain_ref[...]).astype(bf16)
    total[...] += dot(gated_low[...], w_ref[...])

    @pl.when(block == NB - 1)
    def _():
        def one(span):
            mean = jnp.sum(squares[span, :], axis=-1, keepdims=True) / INNER
            inverse = lax.rsqrt(mean + epsilon)
            inverse_ref[span, :] = jnp.broadcast_to(inverse, (32, LANES))
            factor = inverse * valid_ref[span, 0:1]
            out_ref[span, :] = h_ref[span, :] + factor * total[span, :]

        for_rows(rows, 32, one)


def branch(y, gate, act, cum, state, gain_row, weight, h, valid, carry=None, identity=None):
    rows = h.shape[0]
    count = state.shape[0]
    return launch(
        branch_kernel,
        "branch",
        (NB,),
        [
            pl.BlockSpec((rows, BLK), lambda b: (0, b)),
            pl.BlockSpec((rows, BLK), lambda b: (0, b)),
            pl.BlockSpec((rows, MAPS), lambda b: (0, 0)),
            pl.BlockSpec((rows, LANES), lambda b: (0, 0)),
            pl.BlockSpec((count, 1, NSTATE, BLK), lambda b: (0, b, 0, 0)),
            pl.BlockSpec((1, BLK), lambda b: (0, b)),
            pl.BlockSpec((BLK, D), lambda b: (b, 0)),
            pl.BlockSpec((rows, D), lambda b: (0, 0)),
            pl.BlockSpec((rows, LANES), lambda b: (0, 0)),
        ],
        [
            pl.BlockSpec((rows, D), lambda b: (0, 0)),
            pl.BlockSpec((rows, BLK), lambda b: (0, b)),
            pl.BlockSpec((rows, LANES), lambda b: (0, 0)),
        ],
        [
            jax.ShapeDtypeStruct((rows, D), f32),
            jax.ShapeDtypeStruct((rows, INNER), f32),
            jax.ShapeDtypeStruct((rows, LANES), f32),
        ],
        (y, gate, act, cum, state, gain_row, weight, h, valid),
        scratch=[
            pltpu.VMEM((rows, D), f32),
            pltpu.VMEM((rows, LANES), f32),
            pltpu.VMEM((rows, BLK), bf16),
        ],
        cost=(2 * rows * D * INNER, 2 * D * INNER, 10**6),
        carry=carry,
        identity=identity,
    )


def turn_kernel(
    g_ref, valid_ref, mixture_ref, gate_ref, inverse_ref, gain_ref, w_ref, act_ref, cum_ref, normed_ref, w_gate_ref,
    gain_out_ref, w_out_ref, dy_ref, state_ref, back_ref, w_gate_out_ref,
    low, norm_low, held, mean, output_t, turned,
):
    step = pl.program_id(0)
    rows = g_ref.shape[0]
    length = rows // SLOTS
    count = state_ref.shape[0]

    @pl.when(step == 0)
    def _():
        def one(span):
            low[span, :] = (valid_ref[span, 0:1] * g_ref[span, :]).astype(bf16)

        for_rows(rows, 32, one)
        mean[...] = jnp.zeros_like(mean)
        turned[...] = normed_ref[...].T
        for slot in range(count):
            span = slice(slot * length, (slot + 1) * length)
            output_t[slot, 0], output_t[slot, 1] = halves(act_ref[span, NSTATE:].T)

    @pl.when(step < NB)
    def _():
        held[step] = dot_nt(low[...], w_ref[...])
        gain_out_ref[...] = jnp.zeros_like(gain_out_ref)

        def one(span):
            gate = gate_ref[span, :]
            gated = mixture_ref[span, :] * gate * sigmoid(gate)
            back = held[step, span, :]
            unit = gated * inverse_ref[span, 0:1]
            norm_low[span, :] = (unit * gain_ref[...]).astype(bf16)
            gain_out_ref[0:1, :] += jnp.sum(back * unit, axis=0, keepdims=True)
            mean[span, :] += fold(gated * back * gain_ref[...])

        for_rows(rows, 128, one)
        w_out_ref[...] = dot_tn(norm_low[...], low[...]).astype(bf16)

    @pl.when(step == NB - 1)
    def _():
        mean[...] = jnp.broadcast_to(jnp.sum(mean[...], axis=-1, keepdims=True) / INNER, mean.shape)

    @pl.when(jnp.logical_and(step >= NB, step < 2 * NB))
    def _():
        block = step - NB
        for slot in range(SLOTS):
            span = slice(slot * length, (slot + 1) * length)
            gate = gate_ref[span, :]
            curve = sigmoid(gate)
            mixture = mixture_ref[span, :]
            swish = gate * curve
            inverse = inverse_ref[span, 0:1]
            back = held[block, span, :] * gain_ref[...]
            pull = inverse * inverse * inverse * mean[span, 0:1]
            grad = inverse * back - (mixture * swish) * pull
            dy = grad * swish
            dy_ref[span, :] = dy
            held[block, span, :] = grad * mixture * curve * (1.0 + gate * (1.0 - curve))
            if slot < count:
                grown = spread(jnp.exp(heads_first(cum_ref[span, :], block)))
                state_ref[slot, 0] = dot_halves((output_t[slot, 0], output_t[slot, 1]), halves(dy * grown))

    @pl.when(step >= 2 * NB)
    def _():
        grads = held[step - 2 * NB].astype(bf16)
        w_gate_out_ref[...] = dot(turned[...], grads).astype(bf16)
        product = dot_nt(grads, w_gate_ref[...])

        @pl.when(step == 2 * NB)
        def _():
            back_ref[...] = product

        @pl.when(step > 2 * NB)
        def _():
            back_ref[...] += product


def turn(
    g, valid, mixture, gate, inverse, gain_row, weight, act, cum, normed, weight_gate, count, carry=None, identity=None
):
    rows = g.shape[0]
    length = rows // SLOTS
    first = lambda n: jnp.minimum(n, NB - 1)
    second = lambda n: jnp.clip(n - NB, 0, NB - 1)
    third = lambda n: jnp.maximum(n - 2 * NB, 0)
    both = lambda n: jnp.where(n < NB, n, second(n))
    once = dict(pipeline_mode=pl.Buffered(1))
    return launch(
        turn_kernel,
        "turn",
        (3 * NB,),
        [
            pl.BlockSpec((rows, D), lambda n: (0, 0), **once),
            pl.BlockSpec((rows, LANES), lambda n: (0, 0), **once),
            pl.BlockSpec((rows, BLK), lambda n: (0, both(n))),
            pl.BlockSpec((rows, BLK), lambda n: (0, both(n))),
            pl.BlockSpec((rows, LANES), lambda n: (0, 0), **once),
            pl.BlockSpec((1, BLK), lambda n: (0, both(n))),
            pl.BlockSpec((BLK, D), lambda n: (first(n), 0)),
            pl.BlockSpec((rows, MAPS), lambda n: (0, 0), **once),
            pl.BlockSpec((rows, LANES), lambda n: (0, 0), **once),
            pl.BlockSpec((rows, D), lambda n: (0, 0), **once),
            pl.BlockSpec((D, BLK), lambda n: (0, third(n))),
        ],
        [
            pl.BlockSpec((8, BLK), lambda n: (0, first(n))),
            pl.BlockSpec((BLK, D), lambda n: (first(n), 0)),
            pl.BlockSpec((rows, BLK), lambda n: (0, second(n))),
            pl.BlockSpec((count, 1, NSTATE, BLK), lambda n: (0, second(n), 0, 0)),
            pl.BlockSpec((rows, D), lambda n: (0, 0)),
            pl.BlockSpec((D, BLK), lambda n: (0, third(n))),
        ],
        [
            jax.ShapeDtypeStruct((8, INNER), f32),
            jax.ShapeDtypeStruct((INNER, D), bf16),
            jax.ShapeDtypeStruct((rows, INNER), f32),
            jax.ShapeDtypeStruct((count, NB, NSTATE, BLK), f32),
            jax.ShapeDtypeStruct((rows, D), f32),
            jax.ShapeDtypeStruct((D, INNER), bf16),
        ],
        (g, valid, mixture, gate, inverse, gain_row, weight, act, cum, normed, weight_gate),
        scratch=[
            pltpu.VMEM((rows, D), bf16),
            pltpu.VMEM((rows, BLK), bf16),
            pltpu.VMEM((NB, rows, BLK), f32),
            pltpu.VMEM((rows, LANES), f32),
            pltpu.VMEM((count, 2, NSTATE, length), bf16),
            pltpu.VMEM((D, rows), bf16),
        ],
        cost=(8 * rows * D * INNER, 8 * D * INNER, 10**7),
        carry=carry,
        identity=identity,
    )


def unmix_kernel(
    relay, edge, alone, count, rows_ref, edge_ref, taps_ref, maps_ref, maps_edge_ref, maps_taps_ref, raw_ref, heads_ref, skip_ref,
    dy_ref, state_ref, local_ref, decay_ref, cum_ref, step_ref, act_ref,
    grads_ref, late_ref, taps_out_ref, heads_out_ref,
    extended, maps_extended, inner, d_inner, minus, plus, scales, grad_ext, maps_grad_ext, d_maps, d_cum, d_step, over_rows, sums, *flow,
):
    turn, block = pl.program_id(0), pl.program_id(1)
    slot = SLOTS - 1 - turn
    length = rows_ref.shape[1]
    relay.bind(*flow[:4])
    edge.bind(*flow[4:])
    reached = slot < count
    piece = jnp.where(reached, slot * NB + block, relay.pieces)
    number = turn * (NB + 1) + block

    @pl.when(number == 0)
    def _():
        if alone:
            relay.greet()
        relay.open()
        edge.open()

    def grow(member):
        its_slot, its_block = member // NB, lax.rem(member, NB)
        relay.grow(member, local_ref[its_slot, its_block], decay_ref[its_slot, its_block, 0:1, :])

    due = number - jnp.minimum(2 * (lax.axis_size("seq") - 1 - relay.me), NB)

    @pl.when(jnp.logical_and(due >= 0, due < NB))
    def _():
        grow(due)

    if count == SLOTS:
        @pl.when(jnp.logical_and(turn == 0, block < NB))
        def _():
            grow(NB + block)

    def conv_back(gradient, taps, given, padded):
        padded[8 : 8 + length, :] = gradient
        back = taps[0:1] * padded[3 : 3 + length + 8, :]
        for k in range(1, CONV):
            back = back + taps[k : k + 1] * padded[3 - k : 3 - k + length + 8, :]
        lines = [
            jnp.sum(gradient * given[5 + k : 5 + k + length, :], axis=0, keepdims=True) for k in range(CONV)
        ]
        lines.append(jnp.zeros((8 - CONV, gradient.shape[1]), f32))
        return back[:8], back[8:].astype(bf16), jnp.concatenate(lines, axis=0)

    @pl.when(block == 0)
    def _():
        for padded in (grad_ext, maps_grad_ext):
            padded[0:8, :] = jnp.zeros((8, padded.shape[1]), f32)
            padded[8 + length :, :] = jnp.zeros((8, padded.shape[1]), f32)
        maps = act_ref[0]
        products = dot_halves(halves(maps[:, :NSTATE]), halves(maps[:, NSTATE:]), dot_nt)
        inner[...] = jnp.where(lower(length).T, products, 0.0)
        cum = cum_ref[0]
        split_rows(cum.T, minus, plus)
        stack_halves(scales, [step_ref[0], jnp.exp(cum[length - 1 :, :] - cum), jnp.exp(cum)])
        d_inner[...] = jnp.zeros_like(d_inner)
        d_maps[...] = jnp.zeros_like(d_maps)
        d_cum[...] = jnp.zeros_like(d_cum)
        d_step[...] = jnp.zeros_like(d_step)
        over_rows[...] = jnp.zeros_like(over_rows)
        sums[...] = jnp.zeros_like(sums)

    @pl.when(block < NB)
    def _():
        load_extended(extended, edge_ref, rows_ref)
        convolved = convolve(extended, taps_ref[...], length)
        curve = sigmoid(convolved)
        values = convolved * curve
        size, remaining, grown = spread_all(scales, block, length)
        stepped = values * size
        low = stepped.astype(bf16)
        dy = dy_ref[0]
        dy_low = dy.astype(bf16)
        dy_t = dy.T.astype(bf16)
        parts = []
        moved_all = {first: [] for first in range(0, length, LANES)}
        for pair in range(PER // 2):
            low_pair = head_pairs(low, pair)
            dy_pair = head_pairs(dy_low, pair)
            dy_pair_t = dy_t[pair * LANES : (pair + 1) * LANES, :]
            pieces = []
            column_sums = [None, None]
            for first in range(0, length, LANES):
                end = first + LANES
                weights = []
                products = inner[first:end, first:]
                grads_sum = None
                for j in range(2):
                    rows = pl.ds(pl.multiple_of((block * PER + 2 * pair + j) * 16, 16), 16)
                    change = dot_tn(minus[rows, first:end], plus[rows, first:])
                    decays = jnp.exp(jnp.minimum(change, 0.0))
                    weights.append((products * decays).astype(bf16))
                    grads = dot(low_pair[j][first:end], dy_pair_t[:, first:]) * decays
                    grads_sum = grads if grads_sum is None else grads_sum + grads
                    moved = (grads * products).astype(bf16)
                    moved_all[first].append(moved)
                    found = jnp.sum(moved.astype(f32), axis=0, keepdims=True)
                    if first:
                        found = jnp.concatenate([jnp.zeros((1, first), f32), found], axis=1)
                    column_sums[j] = found if column_sums[j] is None else column_sums[j] + found
                d_inner[first:end, first:] += grads_sum
                pieces.append(
                    dot(jnp.concatenate(weights, axis=1), jnp.concatenate([part[first:] for part in dy_pair], axis=0))
                )
            parts.append(jnp.concatenate(pieces, axis=0))
            for j in range(2):
                over_rows[pl.ds(block * PER + 2 * pair + j, 1), :] = column_sums[j]
        intra = jnp.concatenate(parts, axis=1)
        for first, moved in moved_all.items():
            span = length - first
            head = lax.broadcasted_iota(jnp.int32, (PER * span, LANES), 0) // span + block * PER
            chosen = (lax.broadcasted_iota(jnp.int32, (PER * span, LANES), 1) == head).astype(bf16)
            d_cum[first : first + LANES, :] -= dot(jnp.concatenate(moved, axis=1), chosen)
        which = lax.broadcasted_iota(jnp.int32, (BLK, LANES), 0) // HEADDIM + block * PER
        chosen = which == lax.broadcasted_iota(jnp.int32, (BLK, LANES), 1)
        member = chosen.astype(f32)
        member_low = chosen.astype(bf16)
        state = jnp.where(reached, state_ref[0, 0].astype(f32), 0.0).astype(bf16)
        later = relay.landed[piece]
        maps = act_ref[0]
        from_later = dot_member(maps[:, :NSTATE], later) * remaining
        d_stepped = intra + from_later
        left = stepped * remaining
        grown_dy = dy * grown
        used = stepped * from_later
        d_cum[...] += dot_member(
            grown_dy * dot_member(maps[:, NSTATE:], state) - used, member_low
        )
        d_maps[:, :NSTATE] += dot_nt(left.astype(bf16), later)
        d_maps[:, NSTATE:] += dot_nt(grown_dy.astype(bf16), state)
        d_step[...] += dot_member(d_stepped * values, member_low)
        lines = jnp.concatenate(
            [
                jnp.sum(used, axis=0, keepdims=True),
                jnp.sum(dy * values, axis=0, keepdims=True),
                jnp.sum(later.astype(f32) * state.astype(f32), axis=0, keepdims=True),
                jnp.zeros((5, BLK), f32),
            ],
            axis=0,
        )
        sums[...] += dot_exact(lines, member)
        d_values = d_stepped * size + skip_ref[...] * dy
        before, grads_ref[0], taps_out_ref[0] = conv_back(
            d_values * curve * (1.0 + convolved * (1.0 - curve)), taps_ref[...], extended, grad_ext
        )
        edge.give(number, lambda: before)

    @pl.when(block == NB)
    def _():
        load_extended(maps_extended, maps_edge_ref, maps_ref)
        convolved = convolve(maps_extended, maps_taps_ref[...], length)
        curve = sigmoid(convolved)
        maps = act_ref[0]
        masked = jnp.where(lower(length).T, d_inner[...], 0.0)
        d_input = d_maps[:, :NSTATE] + dot_halves(halves(masked), halves(maps[:, NSTATE:]))
        d_output = d_maps[:, NSTATE:] + dot_halves(halves(masked.T), halves(maps[:, :NSTATE]))
        d_both = jnp.concatenate([d_input, d_output], axis=1)
        before, inside, lines = conv_back(
            d_both * curve * (1.0 + convolved * (1.0 - curve)), maps_taps_ref[...], maps_extended, maps_grad_ext
        )
        rest = jnp.zeros((8, BLK - MAPS), f32)
        edge.give(number, lambda: jnp.concatenate([before, rest], axis=1))
        taps_out_ref[0] = jnp.concatenate([lines, rest], axis=1)
        final = cum_ref[0][length - 1 :, :]
        at_end = sums[0:1, :] + jnp.exp(final) * sums[2:3, :]
        d_total = d_cum[...] + over_rows[...].T
        position = lax.broadcasted_iota(jnp.int32, (length, 1), 0)
        d_total = d_total + jnp.where(position == length - 1, at_end, 0.0)
        d_decay = dot_exact(lower(length).T.astype(f32), d_total)
        rate = jnp.exp(heads_ref[1:2, :])
        size = step_ref[0]
        d_raw = (d_step[...] - d_decay * rate) * sigmoid(raw_ref[0] + heads_ref[0:1, :])
        d_raw_low = d_raw.astype(bf16)
        grads_ref[0] = jnp.concatenate([inside, d_raw_low, jnp.zeros_like(d_raw_low)], axis=1)
        heads_out_ref[0] = jnp.concatenate(
            [
                jnp.sum(d_raw, axis=0, keepdims=True),
                jnp.sum(d_decay * (-size * rate), axis=0, keepdims=True),
                sums[1:2, :],
                jnp.zeros((5, LANES), f32),
            ],
            axis=0,
        )

    @pl.when(number == SLOTS * (NB + 1) - 1)
    def _():
        relay.close()
        for given in range(edge.pieces):
            edge.take(given)
            its_turn, its_block = divmod(given, NB + 1)
            late_ref[SLOTS - 1 - its_turn, :, its_block * BLK : (its_block + 1) * BLK] = edge.landed[given]
        edge.close()


def unmix(proj, edge, taps, raw, heads, skip_row, dy, state, local, decay, cum, size, act, count, carry=None, identity=None):
    length = proj.shape[1]
    relay = Along(-1, count * NB, (NSTATE, BLK), bf16)
    border = Along(-1, SLOTS * (NB + 1), (8, BLK), f32)
    of = lambda s: SLOTS - 1 - s
    known = lambda s: jnp.minimum(of(s), count - 1)
    inside = lambda b: jnp.minimum(b, NB - 1)
    return launch(
        functools.partial(unmix_kernel, relay, border, carry is None, count),
        "unmix",
        (SLOTS, NB + 1),
        [
            pl.BlockSpec((1, length, BLK), lambda s, b: (of(s), 0, inside(b))),
            pl.BlockSpec((1, 8, BLK), lambda s, b: (of(s), 0, inside(b))),
            pl.BlockSpec((8, BLK), lambda s, b: (0, inside(b))),
            pl.BlockSpec((1, length, MAPS), lambda s, b: (of(s), 0, INNER // MAPS)),
            pl.BlockSpec((1, 8, MAPS), lambda s, b: (of(s), 0, INNER // MAPS)),
            pl.BlockSpec((8, MAPS), lambda s, b: (0, INNER // MAPS)),
            pl.BlockSpec((1, length, LANES), lambda s, b: (of(s), 0, 0)),
            pl.BlockSpec((8, LANES), lambda s, b: (0, 0)),
            pl.BlockSpec((1, BLK), lambda s, b: (0, inside(b))),
            pl.BlockSpec((1, length, BLK), lambda s, b: (of(s), 0, inside(b))),
            pl.BlockSpec((1, 1, NSTATE, BLK), lambda s, b: (known(s), inside(b), 0, 0)),
            pl.BlockSpec((count, NB, NSTATE, BLK), lambda s, b: (0, 0, 0, 0)),
            pl.BlockSpec((SLOTS, NB, 8, BLK), lambda s, b: (0, 0, 0, 0)),
            pl.BlockSpec((1, length, LANES), lambda s, b: (of(s), 0, 0)),
            pl.BlockSpec((1, length, LANES), lambda s, b: (of(s), 0, 0)),
            pl.BlockSpec((1, length, MAPS), lambda s, b: (of(s), 0, 0)),
        ],
        [
            pl.BlockSpec((1, length, BLK), lambda s, b: (of(s), 0, b)),
            pl.BlockSpec((SLOTS, 8, TAIL), lambda s, b: (0, 0, 0)),
            pl.BlockSpec((1, 8, BLK), lambda s, b: (of(s), 0, b)),
            pl.BlockSpec((1, 8, LANES), lambda s, b: (of(s), 0, 0)),
        ],
        [
            jax.ShapeDtypeStruct((SLOTS, length, TAIL), bf16),
            jax.ShapeDtypeStruct((SLOTS, 8, TAIL), f32),
            jax.ShapeDtypeStruct((SLOTS, 8, TAIL), f32),
            jax.ShapeDtypeStruct((SLOTS, 8, LANES), f32),
        ],
        (proj, edge, taps, proj, edge, taps, raw, heads, skip_row, dy, state, local, decay, cum, size, act),
        scratch=[
            pltpu.VMEM((length + 8, BLK), f32),
            pltpu.VMEM((length + 8, MAPS), f32),
            pltpu.VMEM((length, length), f32),
            pltpu.VMEM((length, length), f32),
            pltpu.VMEM((16 * HEADS, length), bf16),
            pltpu.VMEM((16 * HEADS, length), bf16),
            pltpu.VMEM((6 * length, LANES), bf16),
            pltpu.VMEM((length + 16, BLK), f32),
            pltpu.VMEM((length + 16, MAPS), f32),
            pltpu.VMEM((length, 2 * NSTATE), f32),
            pltpu.VMEM((length, LANES), f32),
            pltpu.VMEM((length, LANES), f32),
            pltpu.VMEM((LANES, length), f32),
            pltpu.VMEM((8, LANES), f32),
        ]
        + relay.scratch
        + border.scratch,
        cost=(2 * 10**10, 2 * 10**7, 10**7),
        carry=carry,
        identity=identity,
        relay=True,
    )


def unproject_kernel(
    grads_ref, late_ref, w_ref, normed_ref, h_ref, g_ref, gain_ref, back_ref,
    out_ref, gain_out_ref, w_out_ref,
    total, turned, mended,
):
    step = pl.program_id(0)
    rows = h_ref.shape[0]
    length = rows // SLOTS

    @pl.when(step == 0)
    def _():
        total[...] = back_ref[...]
        turned[...] = normed_ref[...].T

    mended[...] = grads_ref[...]
    for slot in range(SLOTS):
        span = slice((slot + 1) * length - 16, (slot + 1) * length)
        extra = jnp.concatenate([jnp.zeros((8, COLS), f32), late_ref[slot]], axis=0)
        mended[span, :] = (grads_ref[span, :].astype(f32) + extra).astype(bf16)
    w_out_ref[...] = dot(turned[...], mended[...]).astype(bf16)
    total[...] += dot_nt(mended[...], w_ref[...])

    @pl.when(step == pl.num_programs(0) - 1)
    def _():
        gain_out_ref[...] = jnp.zeros_like(gain_out_ref)

        def one(span):
            h = h_ref[span, :]
            inverse = lax.rsqrt(jnp.mean(h * h, axis=-1, keepdims=True) + epsilon)
            back = total[span, :]
            unit = h * inverse
            gain_out_ref[0:1, :] += jnp.sum(back * unit, axis=0, keepdims=True)
            wanted = back * gain_ref[...]
            mean = jnp.mean(unit * wanted, axis=-1, keepdims=True)
            out_ref[span, :] = g_ref[span, :] + inverse * (wanted - unit * mean)

        for_rows(rows, 32, one)


def unproject(grads, late, weight, normed, h, g, gain_row, back, carry=None, identity=None):
    rows = h.shape[0]
    return launch(
        unproject_kernel,
        "unproject",
        (TAIL // COLS,),
        [
            pl.BlockSpec((rows, COLS), lambda n: (0, n)),
            pl.BlockSpec((SLOTS, 8, COLS), lambda n: (0, 0, n)),
            pl.BlockSpec((D, COLS), lambda n: (0, n)),
            pl.BlockSpec((rows, D), lambda n: (0, 0)),
            pl.BlockSpec((rows, D), lambda n: (0, 0)),
            pl.BlockSpec((rows, D), lambda n: (0, 0)),
            pl.BlockSpec((1, D), lambda n: (0, 0)),
            pl.BlockSpec((rows, D), lambda n: (0, 0)),
        ],
        [
            pl.BlockSpec((rows, D), lambda n: (0, 0)),
            pl.BlockSpec((8, D), lambda n: (0, 0)),
            pl.BlockSpec((D, COLS), lambda n: (0, n)),
        ],
        [
            jax.ShapeDtypeStruct((rows, D), f32),
            jax.ShapeDtypeStruct((8, D), f32),
            jax.ShapeDtypeStruct((D, TAIL), bf16),
        ],
        (grads, late, weight, normed, h, g, gain_row, back),
        scratch=[
            pltpu.VMEM((rows, D), f32),
            pltpu.VMEM((D, rows), bf16),
            pltpu.VMEM((rows, COLS), bf16),
        ],
        cost=(4 * rows * D * TAIL, 4 * D * TAIL, 0),
        carry=carry,
        identity=identity,
    )


MESH = pl.DeviceIdType.MESH
ANY = pl.BlockSpec(memory_space=pl.ANY)
DP_BITS = {"core": 1, "x": 2, "y": 4}
STEPS = ("z1", "z2", "x", "y", "core")


def place():
    dp, z = lax.axis_index("dp"), lax.axis_index("seq")
    return {"y": dp // 4, "x": lax.rem(dp // 2, 2), "core": lax.rem(dp, 2), "z": z, "dp": dp}


def partner(here, step):
    if step == "z1":
        return (here["dp"], here["z"] + 1 - 2 * lax.rem(here["z"], 2))
    if step == "z2":
        return (here["dp"], here["z"] + 2 - 4 * (here["z"] // 2))
    if step == "middle":
        return (here["dp"], 3 - here["z"])
    return (here["dp"] + DP_BITS[step] * (1 - 2 * here[step]), here["z"])


def greet(here, along=False):
    peers = STEPS + ("middle",) if along else STEPS
    barrier = pltpu.get_barrier_semaphore()
    for step in peers:
        pl.semaphore_signal(barrier, inc=1, device_id=partner(here, step), device_id_type=MESH)
    pl.semaphore_wait(barrier, len(peers))


class Exchange:
    def __init__(self, shapes, split, pace):
        self.shapes, self.pace = shapes, pace
        self.jobs, self.waves = [], []
        for index, (rows, columns) in enumerate(shapes):
            parts, pieces = split[index]
            height, width = rows // parts, columns // pieces
            for part in range(parts):
                for piece in range(pieces):
                    if piece % 2 == 0:
                        self.waves.append([])
                    job = (index, piece % 2, part * height, height, piece * width, width)
                    self.jobs.append(job)
                    self.waves[-1].append(job)

    def plan(self):
        last = len(self.waves) - 1 + self.pace * len(STEPS)
        ticks = [[] for _ in range(last + 1)]
        for stage in reversed(range(len(STEPS) + 1)):
            for wave, jobs in enumerate(self.waves):
                ticks[wave + self.pace * stage] += [(stage, job) for job in jobs]
        return ticks


class Gather(Exchange):
    def __init__(self, shards, split, pace):
        super().__init__(tuple(shard.shape for shard in shards), split, pace)
        self.shards, self.wholes = list(shards), {}
        self.entries = self.plan()

    def done(self, index):
        return max(t for t, entries in enumerate(self.entries) for _, job in entries if job[0] == index)

    def whole(self, index):
        found = self.wholes[index]
        return found.reshape(-1, found.shape[-1])

    def until(self, last):
        first = getattr(self, "reached", 0)
        self.reached = last + 1
        return Run(self, first, last)


class Run:
    def __init__(self, gather, first, last):
        self.gather = gather
        self.entries = gather.entries[first : last + 1]
        live = sorted({job[0] for entries in self.entries for stage, job in entries if stage < len(STEPS)})
        self.live = live
        self.fresh = [index for index in live if index not in gather.wholes]
        self.old = [index for index in live if index in gather.wholes]
        needed = {job[0] for entries in self.entries for stage, job in entries if stage == 0}
        self.sources = sorted(needed | set(self.fresh))
        self.args = [gather.shards[i] for i in self.sources] + [gather.wholes[i] for i in self.old]
        self.in_specs = [ANY] * len(self.args)
        self.out_specs = [ANY] * len(live)
        self.out_shape = [
            jax.ShapeDtypeStruct((2, 2, 2, 4) + gather.shapes[i], gather.shards[i].dtype) for i in live
        ]
        self.aliases = {len(self.sources) + k: live.index(i) for k, i in enumerate(self.old)}
        self.started = [
            (stage, job) for entries in self.entries for stage, job in entries if stage < len(STEPS)
        ]
        self.scratch = [
            pltpu.SemaphoreType.DMA((max(1, len(self.fresh)),)),
            pltpu.SemaphoreType.DMA((len(self.started),)),
            pltpu.SemaphoreType.DMA((len(self.started),)),
        ]

    def results(self, wholes):
        for index, whole in zip(self.live, wholes):
            self.gather.wholes[index] = whole
        return None

    def ticks(self, ins, outs, scratch, along=False):
        local_sems, send_sems, recv_sems = scratch
        here = place()
        shards = dict(zip(self.sources, ins))
        wholes = dict(zip(self.live, outs))
        own = [
            pltpu.make_async_copy(
                shards[i], wholes[i].at[here["y"], here["x"], here["core"], here["z"]], local_sems.at[k]
            )
            for k, i in enumerate(self.fresh)
        ]

        def make(stage, job):
            index, colour, top, height, left, width = job
            order = ("z1", "z2", "x", "y", "core") if colour == 0 else ("z1", "z2", "y", "x", "core")
            done = order[:stage]
            axis = lambda name: slice(None) if name in done else here[name]
            depth = here["z"]
            if "z2" in done:
                depth = slice(None)
            elif "z1" in done:
                depth = pl.ds(here["z"] // 2 * 2, 2)
            rows, columns = pl.ds(top, height), pl.ds(left, width)
            target = wholes[index].at[axis("y"), axis("x"), axis("core"), depth, rows, columns]
            source = shards[index].at[rows, columns] if stage == 0 else target
            number = self.started.index((stage, job))
            return pltpu.make_async_remote_copy(
                src_ref=source,
                dst_ref=target,
                send_sem=send_sems.at[number],
                recv_sem=recv_sems.at[number],
                device_id=partner(here, order[stage]),
                device_id_type=MESH,
            )

        ended = set()

        def steps(number, entries):
            actions = []
            if number == 0:
                actions.append(lambda: greet(here, along))
                actions += [copy.start for copy in own]
            if number == 1:
                actions += [copy.wait for copy in own]
            for stage, job in entries:
                before = (stage - 1, job)
                if before in self.started:
                    actions.append(lambda before=before: make(*before).wait())
                    ended.add(before)
                if stage < len(STEPS):
                    actions.append(lambda stage=stage, job=job: make(stage, job).start())
            return actions

        lists = [steps(number, entries) for number, entries in enumerate(self.entries)]
        last = [lambda key=key: make(*key).wait() for key in self.started if key not in ended]
        if len(lists) == 1:
            last = [copy.wait for copy in own] + last
        lists.append(last)

        def run(actions):
            for action in actions:
                action()

        return [functools.partial(run, actions) for actions in lists]


class Reduce(Exchange):
    def __init__(self, partials, split, pace=2, heads=None):
        super().__init__(tuple(partial.shape[1:] for partial in partials), split, pace)
        self.heads = heads is not None
        self.aliases = {}
        self.args = [partial.reshape((2, 2, 2, 4) + partial.shape[1:]) for partial in partials]
        count, number = len(partials), len(self.jobs)
        self.in_specs = [ANY] * count
        outs = list(self.shapes)
        if self.heads:
            self.args.append(heads)
            self.in_specs.append(pl.BlockSpec(heads.shape, lambda *_: (0, 0)))
            outs.append(heads.shape)
        self.out_specs = [pl.BlockSpec(shape, lambda *_: (0, 0)) for shape in outs]
        self.out_shape = [jax.ShapeDtypeStruct(shape, f32) for shape in outs]
        kept, landed = [], [[] for _ in STEPS]
        for index, _, _, height, _, width in self.jobs:
            kind = partials[index].dtype
            kept.append(pltpu.VMEM((2, 2, 4, height, width), kind))
            for stage, lead in enumerate(((2, 2, 4), (2, 4), (4,), (2,), ())):
                landed[stage].append(pltpu.VMEM(lead + (height, width), kind))
        tile = pltpu.SemaphoreType.DMA((number, len(STEPS)))
        self.scratch = kept + sum(landed, []) + [pltpu.SemaphoreType.DMA((number,)), tile, tile]
        if self.heads:
            line = pltpu.SemaphoreType.DMA((len(STEPS),))
            self.scratch += [pltpu.VMEM((len(STEPS),) + heads.shape, f32), line, line]

    def results(self, totals):
        return list(totals)

    def ticks(self, partials, totals, scratch, along=False):
        jobs, number, stages = self.jobs, len(self.jobs), len(STEPS)
        kept, landed = scratch[:number], scratch[number : 6 * number]
        local_sems, send_sems, recv_sems = scratch[6 * number : 6 * number + 3]
        here = place()
        y, x, core, z = here["y"], here["x"], here["core"], here["z"]
        half, odd = z // 2, lax.rem(z, 2)

        def order(job):
            return ("core", "y", "x", "z2", "z1") if job[1] == 0 else ("core", "x", "y", "z2", "z1")

        def leaving(job, stage):
            if stage == 1:
                return (1 - y, slice(None), slice(None)) if job[1] == 0 else (slice(None), 1 - x, slice(None))
            if stage == 2:
                return (y, 1 - x, slice(None)) if job[1] == 0 else (1 - y, x, slice(None))
            if stage == 3:
                return (y, x, pl.ds((1 - half) * 2, 2))
            return (y, x, half * 2 + 1 - odd)

        def cut(job, side):
            index, _, top, height, left, width = job
            return partials[index].at[:, :, side, :, pl.ds(top, height), pl.ds(left, width)]

        def load(job):
            k = jobs.index(job)
            return pltpu.make_async_copy(cut(job, core), kept[k], local_sems.at[k])

        def make(job, stage):
            k = jobs.index(job)
            return pltpu.make_async_remote_copy(
                src_ref=cut(job, 1 - core) if stage == 0 else kept[k].at[leaving(job, stage)],
                dst_ref=landed[stage * number + k],
                send_sem=send_sems.at[k, stage],
                recv_sem=recv_sems.at[k, stage],
                device_id=partner(here, order(job)[stage]),
                device_id_type=MESH,
            )

        def add(job, stage, mine):
            k = jobs.index(job)
            into, came = kept[k], landed[(stage - 1) * number + k]
            pick = lambda value: value if mine else 1 - value
            first = job[1] == 0

            def accumulate(target, source):
                into[target] = (into[target].astype(f32) + came[source].astype(f32)).astype(into.dtype)

            if stage == 1:
                def one(i, carry):
                    a, b = i // 4, lax.rem(i, 4)
                    where = (pick(y), a, b) if first else (a, pick(x), b)
                    accumulate(where, where)
                    return carry

                lax.fori_loop(0, 8, one, 0)
            elif stage == 2:
                def one(b, carry):
                    if first:
                        accumulate((y, pick(x), b), (pick(x), b))
                    else:
                        accumulate((pick(y), x, b), (pick(y), b))
                    return carry

                lax.fori_loop(0, 4, one, 0)
            elif stage == 3:
                for b in range(2):
                    accumulate((y, x, pick(half) * 2 + b), (pick(half) * 2 + b,))
            else:
                accumulate((y, x, half * 2 + pick(odd)), (pick(odd),))

        def finish(job):
            index, _, top, height, left, width = job
            k = jobs.index(job)
            summed = kept[k][y, x, z].astype(f32) + landed[4 * number + k][...].astype(f32)
            totals[index][top : top + height, left : left + width] = summed

        def heads_copy(stage):
            heads_landed, head_send, head_recv = scratch[6 * number + 3 :]
            return pltpu.make_async_remote_copy(
                src_ref=totals[-1],
                dst_ref=heads_landed.at[stage],
                send_sem=head_send.at[stage],
                recv_sem=head_recv.at[stage],
                device_id=partner(here, STEPS[stage]),
                device_id_type=MESH,
            )

        def tick(moment, entries):
            if moment == 0:
                greet(here, along)
                if self.heads:
                    totals[-1][...] = partials[-1][...]
            if self.heads and 0 < moment <= stages:
                heads_copy(moment - 1).wait()
                totals[-1][...] = totals[-1][...] + scratch[6 * number + 3][moment - 1]
            if self.heads and moment < stages:
                heads_copy(moment).start()
            for stage, job in entries:
                if stage == 0:
                    make(job, 0).start()
                    load(job).start()
                    continue
                if stage == 1:
                    load(job).wait()
                make(job, stage - 1).wait()
                if stage == stages:
                    finish(job)
                else:
                    add(job, stage, False)
                    make(job, stage).start()
                    add(job, stage, True)

        return [functools.partial(tick, moment, entries) for moment, entries in enumerate(self.plan())]


def alone(exchange, name, identity):
    ins, outs = len(exchange.in_specs), len(exchange.out_specs)

    def kernel(*refs):
        for tick in exchange.ticks(refs[:ins], refs[ins : ins + outs], refs[ins + outs :]):
            tick()

    found = pl.pallas_call(
        kernel,
        name=name,
        grid=(1,),
        in_specs=exchange.in_specs,
        out_specs=exchange.out_specs,
        out_shape=exchange.out_shape,
        scratch_shapes=exchange.scratch,
        input_output_aliases=exchange.aliases,
        compiler_params=params(collective_id=identity, has_side_effects=True),
    )(*exchange.args)
    return exchange.results(found)


def spaced(first, last, weights):
    marks, sum_so_far = [], 0
    for weight in weights:
        sum_so_far += weight
        marks.append(first + (last - first) * sum_so_far // sum(weights))
    return marks


def padded_rows(array, rows):
    return jnp.pad(array, ((0, rows - array.shape[0]), (0, 0)))


def pack_small(norm_gain, conv_weight, gate_gain):
    pieces = [norm_gain, conv_weight.reshape(LAYERS, -1), gate_gain]
    flat = jnp.concatenate(pieces, axis=1).reshape(-1)
    size = flat.shape[0]
    tiles = -(-size // (16 * LANES)) * 16
    return jnp.pad(flat, (0, tiles * LANES - size)).reshape(tiles, LANES)


def unpack_small(everything, norm_gain, conv_weight, gate_gain):
    count = everything.shape[0]
    size = LAYERS * (norm_gain.shape[1] + conv_weight.shape[1] * conv_weight.shape[2] + gate_gain.shape[1])
    everything = everything.reshape(count, -1)[:, :size].reshape(count, LAYERS, -1)
    everything = jnp.swapaxes(everything, 0, 1).astype(f32)
    first = norm_gain.shape[1]
    second = first + conv_weight.shape[1] * conv_weight.shape[2]
    norm = everything[..., :first].reshape(LAYERS, -1)
    conv = everything[..., first:second].reshape(LAYERS, count, CONV, -1)
    conv = jnp.swapaxes(conv, 1, 2).reshape(LAYERS, CONV, -1)
    gate = everything[..., second:].reshape(LAYERS, -1)
    return norm, conv, gate


def share_small(norm, conv, gate):
    count = lax.axis_size("dp") * lax.axis_size("seq")
    conv = jnp.swapaxes(conv.reshape(LAYERS, CONV, count, -1), 1, 2).reshape(LAYERS, count, -1)
    pieces = [norm.reshape(LAYERS, count, -1), conv, gate.reshape(LAYERS, count, -1)]
    flat = jnp.swapaxes(jnp.concatenate(pieces, axis=-1), 0, 1).reshape(count, -1)
    size = flat.shape[1]
    tiles = -(-size // (16 * LANES)) * 16
    return jnp.pad(flat, ((0, 0), (0, tiles * LANES - size))).reshape(count, tiles, LANES)


def own_small(mine, norm_gain, conv_weight, gate_gain):
    first = norm_gain.shape[1]
    second = first + conv_weight.shape[1] * conv_weight.shape[2]
    width = second + gate_gain.shape[1]
    mine = mine.reshape(-1)[: LAYERS * width].reshape(LAYERS, width)
    return mine[:, :first], mine[:, first:second].reshape(LAYERS, CONV, -1), mine[:, second:]


def body(
    hidden,
    out_grad,
    lengths,
    norm_gain,
    in_proj,
    conv_weight,
    gate_gain,
    out_proj,
    dt_bias,
    a_log,
    d_skip,
):
    length = hidden.shape[1]
    rows = SLOTS * length
    count = 1 if length >= SHORT else SLOTS
    swap = lengths[0] < lengths[1]

    def ordered(array):
        return jnp.where(swap, array[::-1], array)

    positions = lax.axis_index("seq") * length + jnp.arange(length, dtype=jnp.int32)
    valid = (positions[None, :] < ordered(lengths)[:, None]).astype(f32).reshape(rows, 1)
    valid = jnp.broadcast_to(valid, (rows, LANES))
    gates = in_proj[..., :INNER]
    tails = jnp.pad(in_proj[..., INNER:], ((0, 0), (0, 0), (0, TAIL - (PROJ - INNER))))
    ours = lax.axis_size("dp") == 8 and lax.axis_size("seq") == 4
    packed = pack_small(norm_gain, conv_weight, gate_gain)
    shards = [packed]
    for layer in range(LAYERS):
        shards += [tails[layer], gates[layer], out_proj[layer]]
    ids = iter(range(100))
    if ours:
        moving = Gather(shards, [(1, 1)] + [(3, 2)] * (3 * LAYERS), 1)
        tail_done, gate_done, out_done = [[moving.done(1 + 3 * layer + k) for layer in range(LAYERS)] for k in range(3)]
        end = len(moving.entries) - 1
        run = lambda last: moving.until(min(last, end)) if min(last, end) >= moving.reached else None
        alone(moving.until(tail_done[0]), "gather", next(ids))
        everything = moving.wholes[0].reshape((-1,) + packed.shape)
        whole = moving.whole
    else:
        gathered = [lax.all_gather(shard, ("dp", "seq"), axis=0, tiled=True) for shard in shards]
        everything = gathered[0].reshape((-1,) + packed.shape)
        whole = lambda index: gathered[index]
        run = lambda last: None
        tail_done = gate_done = out_done = [0] * LAYERS
    norm_all, conv_all, gate_all = unpack_small(everything, norm_gain, conv_weight, gate_gain)
    h = ordered(hidden).reshape(rows, D)
    kept = []
    for layer in range(LAYERS):
        gain_row = norm_all[layer].reshape(1, D)
        gate_row = gate_all[layer].reshape(1, INNER)
        taps = jnp.pad(conv_all[layer], ((0, 8 - CONV), (0, TAIL - CONVCH)))
        heads = padded_rows(
            jnp.pad(
                jnp.stack([dt_bias[layer], a_log[layer]]), ((0, 0), (0, LANES - HEADS))
            ),
            8,
        )
        skip_row = jnp.repeat(d_skip[layer], HEADDIM).reshape(1, INNER)
        base = 1 + 3 * layer
        more = tail_done[layer + 1] if layer + 1 < LAYERS else out_done[layer]
        marks = spaced(tail_done[layer], more, (16, 30, 11, 30) if layer + 1 < LAYERS else (18, 30, 11, 0))
        marks[1] = max(marks[1], gate_done[layer])
        marks[2] = max(marks[2], out_done[layer])
        proj, raw, normed, edge, *_ = project(h, gain_row, whole(base), run(marks[0]), next(ids))
        cube = proj.reshape(SLOTS, length, TAIL)
        raw = raw.reshape(SLOTS, length, LANES)
        y, state, cum, size, act, decay, *_ = mix(
            cube, edge, taps, raw, heads, skip_row, count, run(marks[1]), next(ids)
        )
        state = state.reshape(count, NB, NSTATE, BLK)
        gate, *_ = project_gate(normed, whole(base + 1), run(marks[2]), next(ids))
        flat = lambda array: array.reshape(rows, -1)
        h_next, mixture, inverse, *_ = branch(
            flat(y), gate, flat(act), flat(cum), state, gate_row, whole(base + 2), h, valid, run(marks[3]), next(ids)
        )
        kept.append(
            (h, gain_row, gate_row, taps, heads, skip_row, proj, gate, raw, normed, edge, cum, size, act,
             decay, state, mixture, inverse, whole(base), whole(base + 1), whole(base + 2))
        )
        h = h_next
    result = ordered(h.reshape(SLOTS, length, D))

    g = ordered(out_grad).reshape(rows, D)
    small = [None] * LAYERS
    partials = [None] * LAYERS
    totals = [[None] * 3 for _ in range(LAYERS)]
    waiting = None
    cut = lambda partial: partial.reshape(lax.axis_size("dp") * lax.axis_size("seq"), -1, partial.shape[-1])

    def summing(arrays):
        if not ours or arrays[0] is None:
            return None
        return Reduce([cut(array) for array in arrays], [(3, 4)] * len(arrays), 2)

    for layer in reversed(range(LAYERS)):
        (h, gain_row, gate_row, taps, heads, skip_row, proj, gate, raw, normed, edge, cum, size, act,
         decay, state, mixture, inverse, weight_tail, weight_gate, weight_out) = kept[layer]
        cube = proj.reshape(SLOTS, length, TAIL)
        flat = lambda array: array.reshape(rows, -1)
        shaped = lambda array: array.reshape(SLOTS, length, -1)
        grad_gate, partial_out, dy, local, back, partial_gate, *sums = turn(
            g, valid, mixture, gate, inverse, gate_row, weight_out, flat(act), flat(cum), normed, weight_gate, count,
            summing([waiting]), next(ids),
        )
        if waiting is not None and ours:
            totals[layer + 1][0] = sums[0][0]
        grads, late, grad_taps, grad_heads, *sums = unmix(
            cube, edge, taps, raw, heads, skip_row, shaped(dy), state, local, decay, cum, size, act, count,
            summing([partial_gate, partial_out]), next(ids),
        )
        if ours:
            totals[layer][1], totals[layer][2] = sums[0]
        g, grad_norm, waiting = unproject(flat(grads), late, weight_tail, normed, h, g, gain_row, back)
        partials[layer] = (waiting, partial_gate, partial_out)
        small[layer] = (
            grad_norm[0], jnp.sum(grad_taps, axis=0)[:CONV, :CONVCH], grad_gate[0],
            jnp.sum(grad_heads, axis=0)[:3, :HEADS],
        )
    grad_hidden = ordered(g.reshape(SLOTS, length, D))
    stacked = [jnp.stack([small[layer][member] for layer in range(LAYERS)]) for member in range(4)]
    shares = share_small(*stacked[:3])
    head_sums = jnp.pad(stacked[3].reshape(-1, HEADS), ((0, 8 - 3 * LAYERS), (0, LANES - HEADS)))
    if ours:
        totals[0][0], mine, head_sums = alone(
            Reduce([cut(waiting), shares], [(3, 2), (1, 1)], heads=head_sums), "reduce", next(ids)
        )
    else:
        totals = [
            [
                lax.optimization_barrier(
                    lax.psum_scatter(partial, ("dp", "seq"), scatter_dimension=0, tiled=True)
                ).astype(f32)
                for partial in members
            ]
            for members in partials
        ]
        mine = lax.psum_scatter(shares, ("dp", "seq"), scatter_dimension=0, tiled=True)
        head_sums = lax.psum(head_sums, ("dp", "seq"))
    grad_norm, grad_conv, grad_gate = own_small(mine, norm_gain, conv_weight, gate_gain)
    grad_heads = head_sums[: 3 * LAYERS, :HEADS].reshape(LAYERS, 3, HEADS)
    return (
        result,
        grad_hidden,
        grad_norm,
        jnp.stack([jnp.concatenate([gate, tail[:, : PROJ - INNER]], axis=1) for tail, gate, _ in totals]),
        grad_conv,
        grad_gate,
        jnp.stack([members[2] for members in totals]),
        grad_heads[:, 0],
        grad_heads[:, 1],
        grad_heads[:, 2],
    )


def solution(mesh):
    tokens = P("dp", "seq", None)
    every = ("dp", "seq")
    weights = (P(None, every), P(None, every, None), P(None, None, every), P(None, every), P(None, every, None))
    return jax.shard_map(
        body,
        mesh=mesh,
        in_specs=(tokens, tokens, P("dp")) + weights + (P(), P(), P()),
        out_specs=(tokens, tokens) + weights + (P(), P(), P()),
        check_vma=False,
    )
```

```python
import functools

import jax
import jax.numpy as jnp
from jax import lax
from jax.experimental import pallas as pl
from jax.experimental.pallas import tpu as pltpu
from jax.sharding import PartitionSpec as P

D = 1536
HEADS = 48
HEADDIM = 64
NSTATE = 128
CONV = 4
LAYERS = 2
INNER = 3072
CONVCH = 3328
PROJ = 6448
SLOTS = 2
SHORT = 256

LANES = 128
TAIL = 3584
BLK = 512
MAPS = 2 * NSTATE
NB = INNER // BLK
COLS = 512
PER = BLK // HEADDIM

f32 = jnp.float32
bf16 = jnp.bfloat16
epsilon = 1e-05
VMEM_LIMIT = 60 << 20


def launch(
    kernel, name, grid, in_specs, out_specs, out_shape, args, scratch=(), cost=None, carry=None, identity=None,
    relay=False, points=1,
):
    options = {"compiler_params": params()}
    if cost is not None:
        options["cost_estimate"] = pl.CostEstimate(flops=cost[0], bytes_accessed=cost[1], transcendentals=cost[2])
    if carry is not None or relay:
        options["compiler_params"] = params(collective_id=identity, has_side_effects=True)
    if carry is None:
        if points > 1:
            kernel = functools.partial(kernel, lambda point, keep=None: None)
        return pl.pallas_call(
            kernel, name=name, grid=grid, in_specs=in_specs, out_specs=out_specs, out_shape=out_shape,
            scratch_shapes=list(scratch), **options,
        )(*args)
    sizes = [len(in_specs), len(carry.in_specs), len(out_specs), len(carry.out_specs), len(scratch)]
    if carry.aliases:
        options["input_output_aliases"] = {sizes[0] + i: sizes[2] + o for i, o in carry.aliases.items()}

    def wrapped(*refs):
        groups, at = [], 0
        for size in sizes:
            groups.append(refs[at : at + size])
            at += size
        step, total = 0, 1
        for axis, extent in enumerate(grid):
            step, total = step * extent + pl.program_id(axis), total * extent
        ticks = carry.ticks(groups[1], groups[3], refs[at:], relay)
        plan = {}
        for number, tick in enumerate(ticks[:-1]):
            moment, point = divmod(number * total * points // (len(ticks) - 1), points)
            plan.setdefault((moment, point), []).append(tick)

        def pump(point, keep=None):
            for (moment, at_point), members in plan.items():
                if at_point == point and (keep is None or keep(moment)):
                    @pl.when(step == moment)
                    def _(members=members):
                        for member in members:
                            member()

        own = (*groups[0], *groups[2], *groups[4])
        if points > 1:
            kernel(pump, *own)
        else:
            pump(0)
            kernel(*own)

        @pl.when(step == total - 1)
        def _():
            ticks[-1]()

    found = pl.pallas_call(
        wrapped, name=name, grid=grid, in_specs=list(in_specs) + carry.in_specs,
        out_specs=list(out_specs) + carry.out_specs, out_shape=list(out_shape) + carry.out_shape,
        scratch_shapes=list(scratch) + carry.scratch, **options,
    )(*args, *carry.args)
    return list(found[: sizes[2]]) + [carry.results(found[sizes[2] :])]


def params(**more):
    return pltpu.CompilerParams(vmem_limit_bytes=VMEM_LIMIT, **more)


def for_rows(total, size, function):
    def step(index, carry):
        function(pl.ds(pl.multiple_of(index * size, size), size))
        return carry

    lax.fori_loop(0, total // size, step, 0)


def dot(left, right):
    return jnp.dot(left, right, preferred_element_type=f32)


def dot_nt(left, right):
    return lax.dot_general(left, right, (((1,), (1,)), ((), ())), preferred_element_type=f32)


def dot_tn(left, right):
    return lax.dot_general(left, right, (((0,), (0,)), ((), ())), preferred_element_type=f32)


def dot_exact(left, right):
    return jnp.dot(left, right, preferred_element_type=f32, precision=lax.Precision.HIGHEST)


def halves(array):
    high = array.astype(bf16)
    return high, (array - high.astype(f32)).astype(bf16)


def dot_halves(left, right, product=dot):
    left_high, left_low = left
    right_high, right_low = right
    return product(left_high, right_high) + product(left_high, right_low) + product(left_low, right_high)


def dot_member(array, member):
    high, low = halves(array)
    return dot(high, member) + dot(low, member)


def sigmoid(vector):
    return 0.5 + 0.5 * jnp.tanh(0.5 * vector)


def softplus(vector):
    return jnp.maximum(vector, 0.0) + jnp.log1p(jnp.exp(-jnp.abs(vector)))


def spread(columns):
    length = columns.shape[0]
    return jnp.concatenate(
        [jnp.broadcast_to(columns[:, j : j + 1], (length, HEADDIM)) for j in range(PER)], axis=1
    )


def heads_first(columns, block):
    return pltpu.roll(columns, lax.rem(LANES - PER * block, LANES), 1)


def fold(array):
    return functools.reduce(jnp.add, [array[:, at : at + LANES] for at in range(0, array.shape[1], LANES)])


def expander(block):
    head = lax.broadcasted_iota(jnp.int32, (LANES, BLK), 0)
    mine = lax.broadcasted_iota(jnp.int32, (LANES, BLK), 1) // HEADDIM + block * PER
    return (head == mine).astype(bf16)


def stack_halves(scratch, arrays):
    length = arrays[0].shape[0]
    for number, array in enumerate(arrays):
        high, low = halves(array)
        scratch[2 * number * length : (2 * number + 1) * length, :] = high
        scratch[(2 * number + 1) * length : (2 * number + 2) * length, :] = low


def spread_all(scratch, block, length):
    wide = dot(scratch[...], expander(block))
    return [
        wide[at : at + length] + wide[at + length : at + 2 * length] for at in range(0, wide.shape[0], 2 * length)
    ]


def split_rows(cum_t, minus, plus):
    rows, length = HEADS, cum_t.shape[1]
    first = cum_t[:rows].astype(bf16).astype(f32)
    rest = cum_t[:rows] - first
    second = rest.astype(bf16).astype(f32)
    third = rest - second
    index = lax.broadcasted_iota(jnp.int32, (rows, 16, length), 1)
    wide = lambda array: jnp.broadcast_to(array[:, None, :], (rows, 16, length))

    def pick(offset, sign, ones):
        found = jnp.where(jnp.logical_and(index >= ones, index < ones + 3), 1.0, 0.0)
        for number, part in enumerate((first, second, third)):
            found = jnp.where(index == offset + number, wide(sign * part), found)
        return found.astype(bf16).reshape(rows * 16, length)

    minus[...] = pick(0, -1.0, 3)
    plus[...] = pick(3, 1.0, 0)


def head_pairs(array, pair):
    columns = array[:, pair * LANES : (pair + 1) * LANES]
    lane = lax.broadcasted_iota(jnp.int32, columns.shape, 1)
    zero = jnp.zeros_like(columns)
    return jnp.where(lane < HEADDIM, columns, zero), jnp.where(lane < HEADDIM, zero, columns)


def load_extended(scratch, edge_ref, rows_ref):
    scratch[0:8, :] = edge_ref[0]
    scratch[8:, :] = rows_ref[0]


def convolve(scratch, taps, length):
    total = taps[0:1] * scratch[5 : 5 + length, :]
    for k in range(1, CONV):
        total = total + taps[k : k + 1] * scratch[5 + k : 5 + k + length, :]
    return total


def lower(length):
    first = lax.broadcasted_iota(jnp.int32, (length, length), 0)
    second = lax.broadcasted_iota(jnp.int32, (length, length), 1)
    return first >= second


class Along:
    def __init__(self, steps, pieces, shape, kind):
        self.steps, self.pieces, self.shape, self.kind = steps, pieces, shape, kind
        self.scratch = [
            pltpu.VMEM((pieces + 1,) + shape, kind),
            pltpu.VMEM((pieces,) + shape, kind),
            pltpu.SemaphoreType.DMA((pieces,)),
            pltpu.SemaphoreType.DMA((pieces,)),
        ]

    def bind(self, landed, sent, send_sems, recv_sems):
        self.landed, self.sent, self.send_sems, self.recv_sems = landed, sent, send_sems, recv_sems
        self.me, last = lax.axis_index("seq"), lax.axis_size("seq") - 1
        ahead, behind = self.me < last, self.me > 0
        self.sends, self.receives = (ahead, behind) if self.steps > 0 else (behind, ahead)

    def peer(self, steps):
        return (lax.axis_index("dp"), self.me + steps)

    def greet(self):
        barrier = pltpu.get_barrier_semaphore()

        @pl.when(self.receives)
        def _():
            pl.semaphore_signal(barrier, inc=1, device_id=self.peer(-self.steps), device_id_type=pl.DeviceIdType.MESH)

        @pl.when(self.sends)
        def _():
            pl.semaphore_wait(barrier, 1)

    def open(self):
        self.landed[self.pieces] = jnp.zeros(self.shape, self.kind)

        @pl.when(jnp.logical_not(self.receives))
        def _():
            for piece in range(self.pieces):
                self.landed[piece] = jnp.zeros(self.shape, self.kind)

    def copy(self, piece):
        return pltpu.make_async_remote_copy(
            src_ref=self.sent.at[piece],
            dst_ref=self.landed.at[piece],
            send_sem=self.send_sems.at[piece],
            recv_sem=self.recv_sems.at[piece],
            device_id=self.peer(self.steps),
            device_id_type=pl.DeviceIdType.MESH,
        )

    def take(self, piece):
        @pl.when(self.receives)
        def _():
            self.copy(piece).wait_recv()

    def give(self, piece, value):
        @pl.when(self.sends)
        def _():
            self.sent[piece] = value()
            self.copy(piece).start()

    def grow(self, piece, local, decay):
        self.take(piece)
        self.give(piece, lambda: (decay * self.landed[piece].astype(f32) + local).astype(bf16))

    def close(self):
        @pl.when(self.sends)
        def _():
            for piece in range(self.pieces):
                self.copy(piece).wait_send()


def project_kernel(edge, alone, h_ref, gain_ref, w_ref, proj_ref, raw_ref, normed_ref, edge_ref, *flow):
    step = pl.program_id(0)
    total = h_ref.shape[0]
    length = total // SLOTS
    edge.bind(*flow)

    @pl.when(step == 0)
    def _():
        if alone:
            edge.greet()
        edge.open()

        def one(rows):
            h = h_ref[rows, :]
            inverse = lax.rsqrt(jnp.mean(h * h, axis=-1, keepdims=True) + epsilon)
            normed_ref[rows, :] = (h * inverse * gain_ref[...]).astype(bf16)

        for_rows(total, 32, one)

    product = dot(normed_ref[...], w_ref[...])
    proj_ref[...] = product
    for slot in range(SLOTS):
        edge.give(step * SLOTS + slot, lambda slot=slot: product[(slot + 1) * length - 8 : (slot + 1) * length])

    @pl.when(step == pl.num_programs(0) - 1)
    def _():
        raw_ref[...] = product[:, COLS - 2 * LANES : COLS - LANES]
        for piece in range(edge.pieces):
            edge.take(piece)
            number, slot = divmod(piece, SLOTS)
            edge_ref[slot, :, number * COLS : (number + 1) * COLS] = edge.landed[piece]
        edge.close()


def project(h, gain_row, weight, carry=None, identity=None):
    total = h.shape[0]
    edge = Along(1, SLOTS * (TAIL // COLS), (8, COLS), f32)
    return launch(
        functools.partial(project_kernel, edge, carry is None),
        "project",
        (TAIL // COLS,),
        [
            pl.BlockSpec((total, D), lambda n: (0, 0)),
            pl.BlockSpec((1, D), lambda n: (0, 0)),
            pl.BlockSpec((D, COLS), lambda n: (0, n)),
        ],
        [
            pl.BlockSpec((total, COLS), lambda n: (0, n)),
            pl.BlockSpec((total, LANES), lambda n: (0, 0)),
            pl.BlockSpec((total, D), lambda n: (0, 0)),
            pl.BlockSpec((SLOTS, 8, TAIL), lambda n: (0, 0, 0)),
        ],
        [
            jax.ShapeDtypeStruct((total, TAIL), f32),
            jax.ShapeDtypeStruct((total, LANES), f32),
            jax.ShapeDtypeStruct((total, D), bf16),
            jax.ShapeDtypeStruct((SLOTS, 8, TAIL), f32),
        ],
        (h, gain_row, weight),
        scratch=edge.scratch,
        cost=(2 * total * D * TAIL, 2 * D * TAIL, 0),
        carry=carry,
        identity=identity,
        relay=True,
    )


def mix_kernel(
    relay, alone, count, rows_ref, edge_ref, taps_ref, maps_ref, maps_edge_ref, maps_taps_ref, raw_ref, heads_ref, skip_ref,
    y_ref, state_ref, cum_ref, step_ref, act_ref, decay_ref,
    extended, maps_extended, inner, minus, plus, input_t, scales, local, decay, *flow,
):
    slot, block = pl.program_id(0), pl.program_id(1)
    number = slot * NB + block
    length = rows_ref.shape[1]
    relay.bind(*flow)

    @pl.when(number == 0)
    def _():
        if alone:
            relay.greet()
        relay.open()

    def grow(piece):
        relay.grow(piece, local[piece], decay[piece, 0:1, :])

    due = number - 1 - 2 * relay.me

    @pl.when(jnp.logical_and(due >= 0, due < NB))
    def _():
        grow(due)

    @pl.when(block == 0)
    def _():
        load_extended(maps_extended, maps_edge_ref, maps_ref)
        convolved = convolve(maps_extended, maps_taps_ref[...], length)
        maps = convolved * sigmoid(convolved)
        act_ref[0] = maps
        products = dot_halves(halves(maps[:, NSTATE:]), halves(maps[:, :NSTATE]), dot_nt)
        input_t[0], input_t[1] = halves(maps[:, :NSTATE].T)
        causal = lower(length)
        inner[...] = jnp.where(causal, products, 0.0)
        size = softplus(raw_ref[0] + heads_ref[0:1, :])
        decay = -size * jnp.exp(heads_ref[1:2, :])
        cum = dot_exact(causal.astype(f32), decay)
        cum_ref[0] = cum
        step_ref[0] = size
        split_rows(cum.T, minus, plus)
        stack_halves(scales, [size, jnp.exp(cum[length - 1 :, :] - cum)])

    load_extended(extended, edge_ref, rows_ref)
    convolved = convolve(extended, taps_ref[...], length)
    values = convolved * sigmoid(convolved)
    wide_step, remaining = spread_all(scales, block, length)
    stepped = values * wide_step
    low = stepped.astype(bf16)
    parts = []
    for pair in range(PER // 2):
        members = head_pairs(low, pair)
        pieces = []
        for first in range(0, length, LANES):
            end = first + LANES
            weights = []
            for j in range(2):
                rows = pl.ds(pl.multiple_of((block * PER + 2 * pair + j) * 16, 16), 16)
                change = dot_tn(plus[rows, first:end], minus[rows, :end])
                weights.append((inner[first:end, :end] * jnp.exp(jnp.minimum(change, 0.0))).astype(bf16))
            pieces.append(
                dot(jnp.concatenate(weights, axis=1), jnp.concatenate([member[:end] for member in members], axis=0))
            )
        parts.append(jnp.concatenate(pieces, axis=0))
    y_ref[0] = jnp.concatenate(parts, axis=1) + skip_ref[...] * values
    final = heads_first(cum_ref[0][length - 8 :, :], block)
    rate = jnp.broadcast_to(spread(jnp.exp(final))[7:], (8, BLK))
    decay_ref[0, 0] = rate

    @pl.when(slot < count)
    def _():
        local[number] = dot_halves((input_t[0], input_t[1]), halves(stepped * remaining))
        decay[number] = rate

    @pl.when(number == SLOTS * NB - 1)
    def _():
        for piece in range(relay.pieces):
            @pl.when(jnp.logical_or(piece >= NB, piece > due))
            def _():
                grow(piece)

            state_ref[piece] = relay.landed[piece]
        relay.close()


def mix(proj, edge, taps, raw, heads, skip_row, count, carry=None, identity=None):
    length = proj.shape[1]
    relay = Along(1, count * NB, (NSTATE, BLK), bf16)
    return launch(
        functools.partial(mix_kernel, relay, carry is None, count),
        "mix",
        (SLOTS, NB),
        [
            pl.BlockSpec((1, length, BLK), lambda s, b: (s, 0, b)),
            pl.BlockSpec((1, 8, BLK), lambda s, b: (s, 0, b)),
            pl.BlockSpec((8, BLK), lambda s, b: (0, b)),
            pl.BlockSpec((1, length, MAPS), lambda s, b: (s, 0, INNER // MAPS)),
            pl.BlockSpec((1, 8, MAPS), lambda s, b: (s, 0, INNER // MAPS)),
            pl.BlockSpec((8, MAPS), lambda s, b: (0, INNER // MAPS)),
            pl.BlockSpec((1, length, LANES), lambda s, b: (s, 0, 0)),
            pl.BlockSpec((8, LANES), lambda s, b: (0, 0)),
            pl.BlockSpec((1, BLK), lambda s, b: (0, b)),
        ],
        [
            pl.BlockSpec((1, length, BLK), lambda s, b: (s, 0, b)),
            pl.BlockSpec((count * NB, NSTATE, BLK), lambda s, b: (0, 0, 0)),
            pl.BlockSpec((1, length, LANES), lambda s, b: (s, 0, 0)),
            pl.BlockSpec((1, length, LANES), lambda s, b: (s, 0, 0)),
            pl.BlockSpec((1, length, MAPS), lambda s, b: (s, 0, 0)),
            pl.BlockSpec((1, 1, 8, BLK), lambda s, b: (s, b, 0, 0)),
        ],
        [
            jax.ShapeDtypeStruct((SLOTS, length, INNER), f32),
            jax.ShapeDtypeStruct((count * NB, NSTATE, BLK), bf16),
            jax.ShapeDtypeStruct((SLOTS, length, LANES), f32),
            jax.ShapeDtypeStruct((SLOTS, length, LANES), f32),
            jax.ShapeDtypeStruct((SLOTS, length, MAPS), f32),
            jax.ShapeDtypeStruct((SLOTS, NB, 8, BLK), f32),
        ],
        (proj, edge, taps, proj, edge, taps, raw, heads, skip_row),
        scratch=[
            pltpu.VMEM((length + 8, BLK), f32),
            pltpu.VMEM((length + 8, MAPS), f32),
            pltpu.VMEM((length, length), f32),
            pltpu.VMEM((16 * HEADS, length), bf16),
            pltpu.VMEM((16 * HEADS, length), bf16),
            pltpu.VMEM((2, NSTATE, length), bf16),
            pltpu.VMEM((4 * length, LANES), bf16),
            pltpu.VMEM((count * NB, NSTATE, BLK), f32),
            pltpu.VMEM((count * NB, 8, BLK), f32),
        ]
        + relay.scratch,
        cost=(6 * 10**9, 10**7, 10**7),
        carry=carry,
        identity=identity,
        relay=True,
    )


def project_gate_kernel(normed_ref, w_ref, gate_ref):
    gate_ref[...] = dot(normed_ref[...], w_ref[...])


def project_gate(normed, weight, carry=None, identity=None):
    total = normed.shape[0]
    return launch(
        project_gate_kernel,
        "project_gate",
        (INNER // COLS,),
        [pl.BlockSpec((total, D), lambda n: (0, 0)), pl.BlockSpec((D, COLS), lambda n: (0, n))],
        [pl.BlockSpec((total, COLS), lambda n: (0, n))],
        [jax.ShapeDtypeStruct((total, INNER), f32)],
        (normed, weight),
        cost=(2 * total * D * INNER, 2 * D * INNER, 0),
        carry=carry,
        identity=identity,
    )


def branch_kernel(
    y_ref, gate_ref, act_ref, cum_ref, state_ref, gain_ref, w_ref, h_ref, valid_ref,
    out_ref, mixture_ref, inverse_ref,
    total, squares, gated_low,
):
    block = pl.program_id(0)
    count = state_ref.shape[0]
    rows = y_ref.shape[0]
    length = rows // SLOTS

    @pl.when(block == 0)
    def _():
        total[...] = jnp.zeros_like(total)
        squares[...] = jnp.zeros_like(squares)

    for slot in range(SLOTS):
        span = slice(slot * length, (slot + 1) * length)
        mixture = y_ref[span, :]
        if slot < count:
            cum = heads_first(cum_ref[span, :], block)
            carried = dot_member(act_ref[span, NSTATE:], state_ref[slot, 0])
            mixture = mixture + carried * spread(jnp.exp(cum))
        gate = gate_ref[span, :]
        gated = mixture * gate * sigmoid(gate)
        mixture_ref[span, :] = mixture
        square = gated * gated
        squares[span, :] += fold(square)
        gated_low[span, :] = (gated * gain_ref[...]).astype(bf16)
    total[...] += dot(gated_low[...], w_ref[...])

    @pl.when(block == NB - 1)
    def _():
        def one(span):
            mean = jnp.sum(squares[span, :], axis=-1, keepdims=True) / INNER
            inverse = lax.rsqrt(mean + epsilon)
            inverse_ref[span, :] = jnp.broadcast_to(inverse, (32, LANES))
            factor = inverse * valid_ref[span, 0:1]
            out_ref[span, :] = h_ref[span, :] + factor * total[span, :]

        for_rows(rows, 32, one)


def branch(y, gate, act, cum, state, gain_row, weight, h, valid, carry=None, identity=None):
    rows = h.shape[0]
    count = state.shape[0]
    return launch(
        branch_kernel,
        "branch",
        (NB,),
        [
            pl.BlockSpec((rows, BLK), lambda b: (0, b)),
            pl.BlockSpec((rows, BLK), lambda b: (0, b)),
            pl.BlockSpec((rows, MAPS), lambda b: (0, 0)),
            pl.BlockSpec((rows, LANES), lambda b: (0, 0)),
            pl.BlockSpec((count, 1, NSTATE, BLK), lambda b: (0, b, 0, 0)),
            pl.BlockSpec((1, BLK), lambda b: (0, b)),
            pl.BlockSpec((BLK, D), lambda b: (b, 0)),
            pl.BlockSpec((rows, D), lambda b: (0, 0)),
            pl.BlockSpec((rows, LANES), lambda b: (0, 0)),
        ],
        [
            pl.BlockSpec((rows, D), lambda b: (0, 0)),
            pl.BlockSpec((rows, BLK), lambda b: (0, b)),
            pl.BlockSpec((rows, LANES), lambda b: (0, 0)),
        ],
        [
            jax.ShapeDtypeStruct((rows, D), f32),
            jax.ShapeDtypeStruct((rows, INNER), f32),
            jax.ShapeDtypeStruct((rows, LANES), f32),
        ],
        (y, gate, act, cum, state, gain_row, weight, h, valid),
        scratch=[
            pltpu.VMEM((rows, D), f32),
            pltpu.VMEM((rows, LANES), f32),
            pltpu.VMEM((rows, BLK), bf16),
        ],
        cost=(2 * rows * D * INNER, 2 * D * INNER, 10**6),
        carry=carry,
        identity=identity,
    )


def turn_kernel(
    g_ref, valid_ref, mixture_ref, gate_ref, inverse_ref, gain_ref, w_ref, act_ref, cum_ref, normed_ref, w_gate_ref,
    gain_out_ref, w_out_ref, dy_ref, state_ref, back_ref, w_gate_out_ref,
    low, norm_low, held, mean, output_t, turned,
):
    step = pl.program_id(0)
    rows = g_ref.shape[0]
    length = rows // SLOTS
    count = state_ref.shape[0]

    @pl.when(step == 0)
    def _():
        def one(span):
            low[span, :] = (valid_ref[span, 0:1] * g_ref[span, :]).astype(bf16)

        for_rows(rows, 32, one)
        mean[...] = jnp.zeros_like(mean)
        turned[...] = normed_ref[...].T
        for slot in range(count):
            span = slice(slot * length, (slot + 1) * length)
            output_t[slot, 0], output_t[slot, 1] = halves(act_ref[span, NSTATE:].T)

    @pl.when(step < NB)
    def _():
        held[step] = dot_nt(low[...], w_ref[...])
        gain_out_ref[...] = jnp.zeros_like(gain_out_ref)

        def one(span):
            gate = gate_ref[span, :]
            gated = mixture_ref[span, :] * gate * sigmoid(gate)
            back = held[step, span, :]
            unit = gated * inverse_ref[span, 0:1]
            norm_low[span, :] = (unit * gain_ref[...]).astype(bf16)
            gain_out_ref[0:1, :] += jnp.sum(back * unit, axis=0, keepdims=True)
            mean[span, :] += fold(gated * back * gain_ref[...])

        for_rows(rows, 128, one)
        w_out_ref[...] = dot_tn(norm_low[...], low[...]).astype(bf16)

    @pl.when(step == NB - 1)
    def _():
        mean[...] = jnp.broadcast_to(jnp.sum(mean[...], axis=-1, keepdims=True) / INNER, mean.shape)

    @pl.when(jnp.logical_and(step >= NB, step < 2 * NB))
    def _():
        block = step - NB
        for slot in range(SLOTS):
            span = slice(slot * length, (slot + 1) * length)
            gate = gate_ref[span, :]
            curve = sigmoid(gate)
            mixture = mixture_ref[span, :]
            swish = gate * curve
            inverse = inverse_ref[span, 0:1]
            back = held[block, span, :] * gain_ref[...]
            pull = inverse * inverse * inverse * mean[span, 0:1]
            grad = inverse * back - (mixture * swish) * pull
            dy = grad * swish
            dy_ref[span, :] = dy
            held[block, span, :] = grad * mixture * curve * (1.0 + gate * (1.0 - curve))
            if slot < count:
                grown = spread(jnp.exp(heads_first(cum_ref[span, :], block)))
                state_ref[slot, 0] = dot_halves((output_t[slot, 0], output_t[slot, 1]), halves(dy * grown))

    @pl.when(step >= 2 * NB)
    def _():
        grads = held[step - 2 * NB].astype(bf16)
        w_gate_out_ref[...] = dot(turned[...], grads).astype(bf16)
        product = dot_nt(grads, w_gate_ref[...])

        @pl.when(step == 2 * NB)
        def _():
            back_ref[...] = product

        @pl.when(step > 2 * NB)
        def _():
            back_ref[...] += product


def turn(
    g, valid, mixture, gate, inverse, gain_row, weight, act, cum, normed, weight_gate, count, carry=None, identity=None
):
    rows = g.shape[0]
    length = rows // SLOTS
    first = lambda n: jnp.minimum(n, NB - 1)
    second = lambda n: jnp.clip(n - NB, 0, NB - 1)
    third = lambda n: jnp.maximum(n - 2 * NB, 0)
    both = lambda n: jnp.where(n < NB, n, second(n))
    once = dict(pipeline_mode=pl.Buffered(1))
    return launch(
        turn_kernel,
        "turn",
        (3 * NB,),
        [
            pl.BlockSpec((rows, D), lambda n: (0, 0), **once),
            pl.BlockSpec((rows, LANES), lambda n: (0, 0), **once),
            pl.BlockSpec((rows, BLK), lambda n: (0, both(n))),
            pl.BlockSpec((rows, BLK), lambda n: (0, both(n))),
            pl.BlockSpec((rows, LANES), lambda n: (0, 0), **once),
            pl.BlockSpec((1, BLK), lambda n: (0, both(n))),
            pl.BlockSpec((BLK, D), lambda n: (first(n), 0)),
            pl.BlockSpec((rows, MAPS), lambda n: (0, 0), **once),
            pl.BlockSpec((rows, LANES), lambda n: (0, 0), **once),
            pl.BlockSpec((rows, D), lambda n: (0, 0), **once),
            pl.BlockSpec((D, BLK), lambda n: (0, third(n))),
        ],
        [
            pl.BlockSpec((8, BLK), lambda n: (0, first(n))),
            pl.BlockSpec((BLK, D), lambda n: (first(n), 0)),
            pl.BlockSpec((rows, BLK), lambda n: (0, second(n))),
            pl.BlockSpec((count, 1, NSTATE, BLK), lambda n: (0, second(n), 0, 0)),
            pl.BlockSpec((rows, D), lambda n: (0, 0)),
            pl.BlockSpec((D, BLK), lambda n: (0, third(n))),
        ],
        [
            jax.ShapeDtypeStruct((8, INNER), f32),
            jax.ShapeDtypeStruct((INNER, D), bf16),
            jax.ShapeDtypeStruct((rows, INNER), f32),
            jax.ShapeDtypeStruct((count, NB, NSTATE, BLK), f32),
            jax.ShapeDtypeStruct((rows, D), f32),
            jax.ShapeDtypeStruct((D, INNER), bf16),
        ],
        (g, valid, mixture, gate, inverse, gain_row, weight, act, cum, normed, weight_gate),
        scratch=[
            pltpu.VMEM((rows, D), bf16),
            pltpu.VMEM((rows, BLK), bf16),
            pltpu.VMEM((NB, rows, BLK), f32),
            pltpu.VMEM((rows, LANES), f32),
            pltpu.VMEM((count, 2, NSTATE, length), bf16),
            pltpu.VMEM((D, rows), bf16),
        ],
        cost=(8 * rows * D * INNER, 8 * D * INNER, 10**7),
        carry=carry,
        identity=identity,
    )


def unmix_kernel(
    relay, edge, alone, count, pump, rows_ref, edge_ref, taps_ref, maps_ref, maps_edge_ref, maps_taps_ref, raw_ref, heads_ref, skip_ref,
    dy_ref, state_ref, local_ref, decay_ref, cum_ref, step_ref, act_ref,
    grads_ref, late_ref, taps_out_ref, heads_out_ref,
    extended, maps_extended, inner, d_inner, minus, plus, scales, grad_ext, maps_grad_ext, d_maps, d_cum, d_step, over_rows, sums, *flow,
):
    pump(0)
    turn, block = pl.program_id(0), pl.program_id(1)
    slot = SLOTS - 1 - turn
    length = rows_ref.shape[1]
    relay.bind(*flow[:4])
    edge.bind(*flow[4:])
    reached = slot < count
    piece = jnp.where(reached, slot * NB + block, relay.pieces)
    number = turn * (NB + 1) + block

    @pl.when(number == 0)
    def _():
        if alone:
            relay.greet()
        relay.open()
        edge.open()

    def grow(member):
        its_slot, its_block = member // NB, lax.rem(member, NB)
        relay.grow(member, local_ref[its_slot, its_block], decay_ref[its_slot, its_block, 0:1, :])

    due = number - jnp.minimum(2 * (lax.axis_size("seq") - 1 - relay.me), NB)

    @pl.when(jnp.logical_and(due >= 0, due < NB))
    def _():
        grow(due)

    if count == SLOTS:
        @pl.when(jnp.logical_and(turn == 0, block < NB))
        def _():
            grow(NB + block)

    def conv_back(gradient, taps, given, padded):
        padded[8 : 8 + length, :] = gradient
        back = taps[0:1] * padded[3 : 3 + length + 8, :]
        for k in range(1, CONV):
            back = back + taps[k : k + 1] * padded[3 - k : 3 - k + length + 8, :]
        lines = [
            jnp.sum(gradient * given[5 + k : 5 + k + length, :], axis=0, keepdims=True) for k in range(CONV)
        ]
        lines.append(jnp.zeros((8 - CONV, gradient.shape[1]), f32))
        return back[:8], back[8:].astype(bf16), jnp.concatenate(lines, axis=0)

    @pl.when(block == 0)
    def _():
        for padded in (grad_ext, maps_grad_ext):
            padded[0:8, :] = jnp.zeros((8, padded.shape[1]), f32)
            padded[8 + length :, :] = jnp.zeros((8, padded.shape[1]), f32)
        maps = act_ref[0]
        products = dot_halves(halves(maps[:, :NSTATE]), halves(maps[:, NSTATE:]), dot_nt)
        inner[...] = jnp.where(lower(length).T, products, 0.0)
        cum = cum_ref[0]
        split_rows(cum.T, minus, plus)
        stack_halves(scales, [step_ref[0], jnp.exp(cum[length - 1 :, :] - cum), jnp.exp(cum)])
        d_inner[...] = jnp.zeros_like(d_inner)
        d_maps[...] = jnp.zeros_like(d_maps)
        d_cum[...] = jnp.zeros_like(d_cum)
        d_step[...] = jnp.zeros_like(d_step)
        over_rows[...] = jnp.zeros_like(over_rows)
        sums[...] = jnp.zeros_like(sums)

    @pl.when(block < NB)
    def _():
        load_extended(extended, edge_ref, rows_ref)
        convolved = convolve(extended, taps_ref[...], length)
        curve = sigmoid(convolved)
        values = convolved * curve
        size, remaining, grown = spread_all(scales, block, length)
        stepped = values * size
        low = stepped.astype(bf16)
        dy = dy_ref[0]
        dy_low = dy.astype(bf16)
        dy_t = dy.T.astype(bf16)
        parts = []
        moved_all = {first: [] for first in range(0, length, LANES)}
        for pair in range(PER // 2):
            low_pair = head_pairs(low, pair)
            dy_pair = head_pairs(dy_low, pair)
            dy_pair_t = dy_t[pair * LANES : (pair + 1) * LANES, :]
            pieces = []
            column_sums = [None, None]
            for first in range(0, length, LANES):
                end = first + LANES
                weights = []
                products = inner[first:end, first:]
                grads_sum = None
                for j in range(2):
                    rows = pl.ds(pl.multiple_of((block * PER + 2 * pair + j) * 16, 16), 16)
                    change = dot_tn(minus[rows, first:end], plus[rows, first:])
                    decays = jnp.exp(jnp.minimum(change, 0.0))
                    weights.append((products * decays).astype(bf16))
                    grads = dot(low_pair[j][first:end], dy_pair_t[:, first:]) * decays
                    grads_sum = grads if grads_sum is None else grads_sum + grads
                    moved = (grads * products).astype(bf16)
                    moved_all[first].append(moved)
                    found = jnp.sum(moved.astype(f32), axis=0, keepdims=True)
                    if first:
                        found = jnp.concatenate([jnp.zeros((1, first), f32), found], axis=1)
                    column_sums[j] = found if column_sums[j] is None else column_sums[j] + found
                d_inner[first:end, first:] += grads_sum
                pieces.append(
                    dot(jnp.concatenate(weights, axis=1), jnp.concatenate([part[first:] for part in dy_pair], axis=0))
                )
            parts.append(jnp.concatenate(pieces, axis=0))
            for j in range(2):
                over_rows[pl.ds(block * PER + 2 * pair + j, 1), :] = column_sums[j]
            pump(1 + pair, lambda moment: moment % (NB + 1) < NB)
        intra = jnp.concatenate(parts, axis=1)
        for first, moved in moved_all.items():
            span = length - first
            head = lax.broadcasted_iota(jnp.int32, (PER * span, LANES), 0) // span + block * PER
            chosen = (lax.broadcasted_iota(jnp.int32, (PER * span, LANES), 1) == head).astype(bf16)
            d_cum[first : first + LANES, :] -= dot(jnp.concatenate(moved, axis=1), chosen)
        which = lax.broadcasted_iota(jnp.int32, (BLK, LANES), 0) // HEADDIM + block * PER
        chosen = which == lax.broadcasted_iota(jnp.int32, (BLK, LANES), 1)
        member = chosen.astype(f32)
        member_low = chosen.astype(bf16)
        state = jnp.where(reached, state_ref[0, 0].astype(f32), 0.0).astype(bf16)
        later = relay.landed[piece]
        maps = act_ref[0]
        from_later = dot_member(maps[:, :NSTATE], later) * remaining
        d_stepped = intra + from_later
        left = stepped * remaining
        grown_dy = dy * grown
        used = stepped * from_later
        d_cum[...] += dot_member(
            grown_dy * dot_member(maps[:, NSTATE:], state) - used, member_low
        )
        d_maps[:, :NSTATE] += dot_nt(left.astype(bf16), later)
        d_maps[:, NSTATE:] += dot_nt(grown_dy.astype(bf16), state)
        d_step[...] += dot_member(d_stepped * values, member_low)
        lines = jnp.concatenate(
            [
                jnp.sum(used, axis=0, keepdims=True),
                jnp.sum(dy * values, axis=0, keepdims=True),
                jnp.sum(later.astype(f32) * state.astype(f32), axis=0, keepdims=True),
                jnp.zeros((5, BLK), f32),
            ],
            axis=0,
        )
        sums[...] += dot_exact(lines, member)
        d_values = d_stepped * size + skip_ref[...] * dy
        before, grads_ref[0], taps_out_ref[0] = conv_back(
            d_values * curve * (1.0 + convolved * (1.0 - curve)), taps_ref[...], extended, grad_ext
        )
        edge.give(number, lambda: before)

    @pl.when(block == NB)
    def _():
        for point in range(1, 1 + PER // 2):
            pump(point, lambda moment: moment % (NB + 1) == NB)
        load_extended(maps_extended, maps_edge_ref, maps_ref)
        convolved = convolve(maps_extended, maps_taps_ref[...], length)
        curve = sigmoid(convolved)
        maps = act_ref[0]
        masked = jnp.where(lower(length).T, d_inner[...], 0.0)
        d_input = d_maps[:, :NSTATE] + dot_halves(halves(masked), halves(maps[:, NSTATE:]))
        d_output = d_maps[:, NSTATE:] + dot_halves(halves(masked.T), halves(maps[:, :NSTATE]))
        d_both = jnp.concatenate([d_input, d_output], axis=1)
        before, inside, lines = conv_back(
            d_both * curve * (1.0 + convolved * (1.0 - curve)), maps_taps_ref[...], maps_extended, maps_grad_ext
        )
        rest = jnp.zeros((8, BLK - MAPS), f32)
        edge.give(number, lambda: jnp.concatenate([before, rest], axis=1))
        taps_out_ref[0] = jnp.concatenate([lines, rest], axis=1)
        final = cum_ref[0][length - 1 :, :]
        at_end = sums[0:1, :] + jnp.exp(final) * sums[2:3, :]
        d_total = d_cum[...] + over_rows[...].T
        position = lax.broadcasted_iota(jnp.int32, (length, 1), 0)
        d_total = d_total + jnp.where(position == length - 1, at_end, 0.0)
        d_decay = dot_exact(lower(length).T.astype(f32), d_total)
        rate = jnp.exp(heads_ref[1:2, :])
        size = step_ref[0]
        d_raw = (d_step[...] - d_decay * rate) * sigmoid(raw_ref[0] + heads_ref[0:1, :])
        d_raw_low = d_raw.astype(bf16)
        grads_ref[0] = jnp.concatenate([inside, d_raw_low, jnp.zeros_like(d_raw_low)], axis=1)
        heads_out_ref[0] = jnp.concatenate(
            [
                jnp.sum(d_raw, axis=0, keepdims=True),
                jnp.sum(d_decay * (-size * rate), axis=0, keepdims=True),
                sums[1:2, :],
                jnp.zeros((5, LANES), f32),
            ],
            axis=0,
        )

    @pl.when(number == SLOTS * (NB + 1) - 1)
    def _():
        relay.close()
        for given in range(edge.pieces):
            edge.take(given)
            its_turn, its_block = divmod(given, NB + 1)
            late_ref[SLOTS - 1 - its_turn, :, its_block * BLK : (its_block + 1) * BLK] = edge.landed[given]
        edge.close()


def unmix(proj, edge, taps, raw, heads, skip_row, dy, state, local, decay, cum, size, act, count, carry=None, identity=None):
    length = proj.shape[1]
    relay = Along(-1, count * NB, (NSTATE, BLK), bf16)
    border = Along(-1, SLOTS * (NB + 1), (8, BLK), f32)
    of = lambda s: SLOTS - 1 - s
    known = lambda s: jnp.minimum(of(s), count - 1)
    inside = lambda b: jnp.minimum(b, NB - 1)
    return launch(
        functools.partial(unmix_kernel, relay, border, carry is None, count),
        "unmix",
        (SLOTS, NB + 1),
        [
            pl.BlockSpec((1, length, BLK), lambda s, b: (of(s), 0, inside(b))),
            pl.BlockSpec((1, 8, BLK), lambda s, b: (of(s), 0, inside(b))),
            pl.BlockSpec((8, BLK), lambda s, b: (0, inside(b))),
            pl.BlockSpec((1, length, MAPS), lambda s, b: (of(s), 0, INNER // MAPS)),
            pl.BlockSpec((1, 8, MAPS), lambda s, b: (of(s), 0, INNER // MAPS)),
            pl.BlockSpec((8, MAPS), lambda s, b: (0, INNER // MAPS)),
            pl.BlockSpec((1, length, LANES), lambda s, b: (of(s), 0, 0)),
            pl.BlockSpec((8, LANES), lambda s, b: (0, 0)),
            pl.BlockSpec((1, BLK), lambda s, b: (0, inside(b))),
            pl.BlockSpec((1, length, BLK), lambda s, b: (of(s), 0, inside(b))),
            pl.BlockSpec((1, 1, NSTATE, BLK), lambda s, b: (known(s), inside(b), 0, 0)),
            pl.BlockSpec((count, NB, NSTATE, BLK), lambda s, b: (0, 0, 0, 0)),
            pl.BlockSpec((SLOTS, NB, 8, BLK), lambda s, b: (0, 0, 0, 0)),
            pl.BlockSpec((1, length, LANES), lambda s, b: (of(s), 0, 0)),
            pl.BlockSpec((1, length, LANES), lambda s, b: (of(s), 0, 0)),
            pl.BlockSpec((1, length, MAPS), lambda s, b: (of(s), 0, 0)),
        ],
        [
            pl.BlockSpec((1, length, BLK), lambda s, b: (of(s), 0, b)),
            pl.BlockSpec((SLOTS, 8, TAIL), lambda s, b: (0, 0, 0)),
            pl.BlockSpec((1, 8, BLK), lambda s, b: (of(s), 0, b)),
            pl.BlockSpec((1, 8, LANES), lambda s, b: (of(s), 0, 0)),
        ],
        [
            jax.ShapeDtypeStruct((SLOTS, length, TAIL), bf16),
            jax.ShapeDtypeStruct((SLOTS, 8, TAIL), f32),
            jax.ShapeDtypeStruct((SLOTS, 8, TAIL), f32),
            jax.ShapeDtypeStruct((SLOTS, 8, LANES), f32),
        ],
        (proj, edge, taps, proj, edge, taps, raw, heads, skip_row, dy, state, local, decay, cum, size, act),
        scratch=[
            pltpu.VMEM((length + 8, BLK), f32),
            pltpu.VMEM((length + 8, MAPS), f32),
            pltpu.VMEM((length, length), f32),
            pltpu.VMEM((length, length), f32),
            pltpu.VMEM((16 * HEADS, length), bf16),
            pltpu.VMEM((16 * HEADS, length), bf16),
            pltpu.VMEM((6 * length, LANES), bf16),
            pltpu.VMEM((length + 16, BLK), f32),
            pltpu.VMEM((length + 16, MAPS), f32),
            pltpu.VMEM((length, 2 * NSTATE), f32),
            pltpu.VMEM((length, LANES), f32),
            pltpu.VMEM((length, LANES), f32),
            pltpu.VMEM((LANES, length), f32),
            pltpu.VMEM((8, LANES), f32),
        ]
        + relay.scratch
        + border.scratch,
        cost=(2 * 10**10, 2 * 10**7, 10**7),
        carry=carry,
        identity=identity,
        relay=True,
        points=1 + PER // 2,
    )


def unproject_kernel(
    grads_ref, late_ref, w_ref, normed_ref, h_far, g_far, gain_ref, back_far,
    out_ref, gain_out_ref, w_out_ref,
    total, turned, mended, h_ref, g_ref, back_ref, sems,
):
    step = pl.program_id(0)
    rows = h_ref.shape[0]
    copies = [
        pltpu.make_async_copy(far, near, sems.at[number])
        for number, (far, near) in enumerate(((h_far, h_ref), (g_far, g_ref), (back_far, back_ref)))
    ]
    length = rows // SLOTS

    @pl.when(step == 0)
    def _():
        for copy in copies:
            copy.start()
        total[...] = jnp.zeros_like(total)
        turned[...] = normed_ref[...].T

    mended[...] = grads_ref[...]
    for slot in range(SLOTS):
        span = slice((slot + 1) * length - 16, (slot + 1) * length)
        extra = jnp.concatenate([jnp.zeros((8, COLS), f32), late_ref[slot]], axis=0)
        mended[span, :] = (grads_ref[span, :].astype(f32) + extra).astype(bf16)
    w_out_ref[...] = dot(turned[...], mended[...]).astype(bf16)
    total[...] += dot_nt(mended[...], w_ref[...])

    @pl.when(step == pl.num_programs(0) - 1)
    def _():
        for copy in copies:
            copy.wait()
        gain_out_ref[...] = jnp.zeros_like(gain_out_ref)

        def one(span):
            h = h_ref[span, :]
            inverse = lax.rsqrt(jnp.mean(h * h, axis=-1, keepdims=True) + epsilon)
            back = total[span, :] + back_ref[span, :]
            unit = h * inverse
            gain_out_ref[0:1, :] += jnp.sum(back * unit, axis=0, keepdims=True)
            wanted = back * gain_ref[...]
            mean = jnp.mean(unit * wanted, axis=-1, keepdims=True)
            out_ref[span, :] = g_ref[span, :] + inverse * (wanted - unit * mean)

        for_rows(rows, 32, one)


def unproject(grads, late, weight, normed, h, g, gain_row, back, carry=None, identity=None):
    rows = h.shape[0]
    return launch(
        unproject_kernel,
        "unproject",
        (TAIL // COLS,),
        [
            pl.BlockSpec((rows, COLS), lambda n: (0, n)),
            pl.BlockSpec((SLOTS, 8, COLS), lambda n: (0, 0, n)),
            pl.BlockSpec((D, COLS), lambda n: (0, n)),
            pl.BlockSpec((rows, D), lambda n: (0, 0)),
            pl.BlockSpec(memory_space=pl.ANY),
            pl.BlockSpec(memory_space=pl.ANY),
            pl.BlockSpec((1, D), lambda n: (0, 0)),
            pl.BlockSpec(memory_space=pl.ANY),
        ],
        [
            pl.BlockSpec((rows, D), lambda n: (0, 0)),
            pl.BlockSpec((8, D), lambda n: (0, 0)),
            pl.BlockSpec((D, COLS), lambda n: (0, n)),
        ],
        [
            jax.ShapeDtypeStruct((rows, D), f32),
            jax.ShapeDtypeStruct((8, D), f32),
            jax.ShapeDtypeStruct((D, TAIL), bf16),
        ],
        (grads, late, weight, normed, h, g, gain_row, back),
        scratch=[
            pltpu.VMEM((rows, D), f32),
            pltpu.VMEM((D, rows), bf16),
            pltpu.VMEM((rows, COLS), bf16),
            pltpu.VMEM((rows, D), f32),
            pltpu.VMEM((rows, D), f32),
            pltpu.VMEM((rows, D), f32),
            pltpu.SemaphoreType.DMA((3,)),
        ],
        cost=(4 * rows * D * TAIL, 4 * D * TAIL, 0),
        carry=carry,
        identity=identity,
    )


MESH = pl.DeviceIdType.MESH
ANY = pl.BlockSpec(memory_space=pl.ANY)
DP_BITS = {"core": 1, "x": 2, "y": 4}
STEPS = ("z1", "z2", "x", "y", "core")


def place():
    dp, z = lax.axis_index("dp"), lax.axis_index("seq")
    return {"y": dp // 4, "x": lax.rem(dp // 2, 2), "core": lax.rem(dp, 2), "z": z, "dp": dp}


def partner(here, step):
    if step == "z1":
        return (here["dp"], here["z"] + 1 - 2 * lax.rem(here["z"], 2))
    if step == "z2":
        return (here["dp"], here["z"] + 2 - 4 * (here["z"] // 2))
    if step == "middle":
        return (here["dp"], 3 - here["z"])
    return (here["dp"] + DP_BITS[step] * (1 - 2 * here[step]), here["z"])


def greet(here, along=False):
    peers = STEPS + ("middle",) if along else STEPS
    barrier = pltpu.get_barrier_semaphore()
    for step in peers:
        pl.semaphore_signal(barrier, inc=1, device_id=partner(here, step), device_id_type=MESH)
    pl.semaphore_wait(barrier, len(peers))


class Exchange:
    def __init__(self, shapes, split, pace):
        self.shapes, self.pace = shapes, pace
        self.jobs, self.waves = [], []
        for index, (rows, columns) in enumerate(shapes):
            parts, pieces = split[index]
            height, width = rows // parts, columns // pieces
            for part in range(parts):
                for piece in range(pieces):
                    if piece % 2 == 0:
                        self.waves.append([])
                    job = (index, piece % 2, part * height, height, piece * width, width)
                    self.jobs.append(job)
                    self.waves[-1].append(job)

    def plan(self):
        last = len(self.waves) - 1 + self.pace * len(STEPS)
        ticks = [[] for _ in range(last + 1)]
        for stage in reversed(range(len(STEPS) + 1)):
            for wave, jobs in enumerate(self.waves):
                ticks[wave + self.pace * stage] += [(stage, job) for job in jobs]
        return ticks


class Gather(Exchange):
    def __init__(self, shards, split, pace):
        super().__init__(tuple(shard.shape for shard in shards), split, pace)
        self.shards, self.wholes = list(shards), {}
        self.entries = self.plan()

    def done(self, index):
        return max(t for t, entries in enumerate(self.entries) for _, job in entries if job[0] == index)

    def whole(self, index):
        found = self.wholes[index]
        return found.reshape(-1, found.shape[-1])

    def until(self, last):
        first = getattr(self, "reached", 0)
        self.reached = last + 1
        return Run(self, first, last)


class Run:
    def __init__(self, gather, first, last):
        self.gather = gather
        self.entries = gather.entries[first : last + 1]
        live = sorted({job[0] for entries in self.entries for stage, job in entries if stage < len(STEPS)})
        self.live = live
        self.fresh = [index for index in live if index not in gather.wholes]
        self.old = [index for index in live if index in gather.wholes]
        needed = {job[0] for entries in self.entries for stage, job in entries if stage == 0}
        self.sources = sorted(needed | set(self.fresh))
        self.args = [gather.shards[i] for i in self.sources] + [gather.wholes[i] for i in self.old]
        self.in_specs = [ANY] * len(self.args)
        self.out_specs = [ANY] * len(live)
        self.out_shape = [
            jax.ShapeDtypeStruct((2, 2, 2, 4) + gather.shapes[i], gather.shards[i].dtype) for i in live
        ]
        self.aliases = {len(self.sources) + k: live.index(i) for k, i in enumerate(self.old)}
        self.started = [
            (stage, job) for entries in self.entries for stage, job in entries if stage < len(STEPS)
        ]
        self.scratch = [
            pltpu.SemaphoreType.DMA((max(1, len(self.fresh)),)),
            pltpu.SemaphoreType.DMA((len(self.started),)),
            pltpu.SemaphoreType.DMA((len(self.started),)),
        ]

    def results(self, wholes):
        for index, whole in zip(self.live, wholes):
            self.gather.wholes[index] = whole
        return None

    def ticks(self, ins, outs, scratch, along=False):
        local_sems, send_sems, recv_sems = scratch
        here = place()
        shards = dict(zip(self.sources, ins))
        wholes = dict(zip(self.live, outs))
        own = [
            pltpu.make_async_copy(
                shards[i], wholes[i].at[here["y"], here["x"], here["core"], here["z"]], local_sems.at[k]
            )
            for k, i in enumerate(self.fresh)
        ]

        def make(stage, job):
            index, colour, top, height, left, width = job
            order = ("z1", "z2", "x", "y", "core") if colour == 0 else ("z1", "z2", "y", "x", "core")
            done = order[:stage]
            axis = lambda name: slice(None) if name in done else here[name]
            depth = here["z"]
            if "z2" in done:
                depth = slice(None)
            elif "z1" in done:
                depth = pl.ds(here["z"] // 2 * 2, 2)
            rows, columns = pl.ds(top, height), pl.ds(left, width)
            target = wholes[index].at[axis("y"), axis("x"), axis("core"), depth, rows, columns]
            source = shards[index].at[rows, columns] if stage == 0 else target
            number = self.started.index((stage, job))
            return pltpu.make_async_remote_copy(
                src_ref=source,
                dst_ref=target,
                send_sem=send_sems.at[number],
                recv_sem=recv_sems.at[number],
                device_id=partner(here, order[stage]),
                device_id_type=MESH,
            )

        ended = set()

        def steps(number, entries):
            actions = []
            if number == 0:
                actions.append(lambda: greet(here, along))
                actions += [copy.start for copy in own]
            if number == 1:
                actions += [copy.wait for copy in own]
            for stage, job in entries:
                before = (stage - 1, job)
                if before in self.started:
                    actions.append(lambda before=before: make(*before).wait())
                    ended.add(before)
                if stage < len(STEPS):
                    actions.append(lambda stage=stage, job=job: make(stage, job).start())
            return actions

        lists = [steps(number, entries) for number, entries in enumerate(self.entries)]
        last = [lambda key=key: make(*key).wait() for key in self.started if key not in ended]
        if len(lists) == 1:
            last = [copy.wait for copy in own] + last
        lists.append(last)

        def run(actions):
            for action in actions:
                action()

        return [functools.partial(run, actions) for actions in lists]


class Reduce(Exchange):
    def __init__(self, partials, split, pace=2, heads=None):
        super().__init__(tuple(partial.shape[1:] for partial in partials), split, pace)
        self.heads = heads is not None
        self.aliases = {}
        self.args = [partial.reshape((2, 2, 2, 4) + partial.shape[1:]) for partial in partials]
        count, number = len(partials), len(self.jobs)
        self.in_specs = [ANY] * count
        outs = list(self.shapes)
        if self.heads:
            self.args.append(heads)
            self.in_specs.append(pl.BlockSpec(heads.shape, lambda *_: (0, 0)))
            outs.append(heads.shape)
        self.out_specs = [pl.BlockSpec(shape, lambda *_: (0, 0)) for shape in outs]
        self.out_shape = [jax.ShapeDtypeStruct(shape, f32) for shape in outs]
        kept, landed = [], [[] for _ in STEPS]
        for index, _, _, height, _, width in self.jobs:
            kind = partials[index].dtype
            kept.append(pltpu.VMEM((2, 2, 4, height, width), kind))
            for stage, lead in enumerate(((2, 2, 4), (2, 4), (4,), (2,), ())):
                landed[stage].append(pltpu.VMEM(lead + (height, width), kind))
        tile = pltpu.SemaphoreType.DMA((number, len(STEPS)))
        self.scratch = kept + sum(landed, []) + [pltpu.SemaphoreType.DMA((number,)), tile, tile]
        if self.heads:
            line = pltpu.SemaphoreType.DMA((len(STEPS),))
            self.scratch += [pltpu.VMEM((len(STEPS),) + heads.shape, f32), line, line]

    def results(self, totals):
        return list(totals)

    def ticks(self, partials, totals, scratch, along=False):
        jobs, number, stages = self.jobs, len(self.jobs), len(STEPS)
        kept, landed = scratch[:number], scratch[number : 6 * number]
        local_sems, send_sems, recv_sems = scratch[6 * number : 6 * number + 3]
        here = place()
        y, x, core, z = here["y"], here["x"], here["core"], here["z"]
        half, odd = z // 2, lax.rem(z, 2)

        def order(job):
            return ("core", "y", "x", "z2", "z1") if job[1] == 0 else ("core", "x", "y", "z2", "z1")

        def leaving(job, stage):
            if stage == 1:
                return (1 - y, slice(None), slice(None)) if job[1] == 0 else (slice(None), 1 - x, slice(None))
            if stage == 2:
                return (y, 1 - x, slice(None)) if job[1] == 0 else (1 - y, x, slice(None))
            if stage == 3:
                return (y, x, pl.ds((1 - half) * 2, 2))
            return (y, x, half * 2 + 1 - odd)

        def cut(job, side):
            index, _, top, height, left, width = job
            return partials[index].at[:, :, side, :, pl.ds(top, height), pl.ds(left, width)]

        def load(job):
            k = jobs.index(job)
            return pltpu.make_async_copy(cut(job, core), kept[k], local_sems.at[k])

        def make(job, stage):
            k = jobs.index(job)
            return pltpu.make_async_remote_copy(
                src_ref=cut(job, 1 - core) if stage == 0 else kept[k].at[leaving(job, stage)],
                dst_ref=landed[stage * number + k],
                send_sem=send_sems.at[k, stage],
                recv_sem=recv_sems.at[k, stage],
                device_id=partner(here, order(job)[stage]),
                device_id_type=MESH,
            )

        def add(job, stage, mine):
            k = jobs.index(job)
            into, came = kept[k], landed[(stage - 1) * number + k]
            pick = lambda value: value if mine else 1 - value
            first = job[1] == 0

            def accumulate(target, source):
                into[target] = (into[target].astype(f32) + came[source].astype(f32)).astype(into.dtype)

            if stage == 1:
                def one(i, carry):
                    a, b = i // 4, lax.rem(i, 4)
                    where = (pick(y), a, b) if first else (a, pick(x), b)
                    accumulate(where, where)
                    return carry

                lax.fori_loop(0, 8, one, 0)
            elif stage == 2:
                def one(b, carry):
                    if first:
                        accumulate((y, pick(x), b), (pick(x), b))
                    else:
                        accumulate((pick(y), x, b), (pick(y), b))
                    return carry

                lax.fori_loop(0, 4, one, 0)
            elif stage == 3:
                for b in range(2):
                    accumulate((y, x, pick(half) * 2 + b), (pick(half) * 2 + b,))
            else:
                accumulate((y, x, half * 2 + pick(odd)), (pick(odd),))

        def finish(job):
            index, _, top, height, left, width = job
            k = jobs.index(job)
            summed = kept[k][y, x, z].astype(f32) + landed[4 * number + k][...].astype(f32)
            totals[index][top : top + height, left : left + width] = summed

        def heads_copy(stage):
            heads_landed, head_send, head_recv = scratch[6 * number + 3 :]
            return pltpu.make_async_remote_copy(
                src_ref=totals[-1],
                dst_ref=heads_landed.at[stage],
                send_sem=head_send.at[stage],
                recv_sem=head_recv.at[stage],
                device_id=partner(here, STEPS[stage]),
                device_id_type=MESH,
            )

        def tick(moment, entries):
            if moment == 0:
                greet(here, along)
                if self.heads:
                    totals[-1][...] = partials[-1][...]
            if self.heads and 0 < moment <= stages:
                heads_copy(moment - 1).wait()
                totals[-1][...] = totals[-1][...] + scratch[6 * number + 3][moment - 1]
            if self.heads and moment < stages:
                heads_copy(moment).start()
            for stage, job in entries:
                if stage == 0:
                    make(job, 0).start()
                    load(job).start()
                    continue
                if stage == 1:
                    load(job).wait()
                make(job, stage - 1).wait()
                if stage == stages:
                    finish(job)
                else:
                    add(job, stage, False)
                    make(job, stage).start()
                    add(job, stage, True)

        return [functools.partial(tick, moment, entries) for moment, entries in enumerate(self.plan())]


def alone(exchange, name, identity):
    ins, outs = len(exchange.in_specs), len(exchange.out_specs)

    def kernel(*refs):
        for tick in exchange.ticks(refs[:ins], refs[ins : ins + outs], refs[ins + outs :]):
            tick()

    found = pl.pallas_call(
        kernel,
        name=name,
        grid=(1,),
        in_specs=exchange.in_specs,
        out_specs=exchange.out_specs,
        out_shape=exchange.out_shape,
        scratch_shapes=exchange.scratch,
        input_output_aliases=exchange.aliases,
        compiler_params=params(collective_id=identity, has_side_effects=True),
    )(*exchange.args)
    return exchange.results(found)


def spaced(first, last, weights):
    marks, sum_so_far = [], 0
    for weight in weights:
        sum_so_far += weight
        marks.append(first + (last - first) * sum_so_far // sum(weights))
    return marks


def padded_rows(array, rows):
    return jnp.pad(array, ((0, rows - array.shape[0]), (0, 0)))


def pack_small(norm_gain, conv_weight, gate_gain):
    pieces = [norm_gain, conv_weight.reshape(LAYERS, -1), gate_gain]
    flat = jnp.concatenate(pieces, axis=1).reshape(-1)
    size = flat.shape[0]
    tiles = -(-size // (16 * LANES)) * 16
    return jnp.pad(flat, (0, tiles * LANES - size)).reshape(tiles, LANES)


def unpack_small(everything, norm_gain, conv_weight, gate_gain):
    count = everything.shape[0]
    size = LAYERS * (norm_gain.shape[1] + conv_weight.shape[1] * conv_weight.shape[2] + gate_gain.shape[1])
    everything = everything.reshape(count, -1)[:, :size].reshape(count, LAYERS, -1)
    everything = jnp.swapaxes(everything, 0, 1).astype(f32)
    first = norm_gain.shape[1]
    second = first + conv_weight.shape[1] * conv_weight.shape[2]
    norm = everything[..., :first].reshape(LAYERS, -1)
    conv = everything[..., first:second].reshape(LAYERS, count, CONV, -1)
    conv = jnp.swapaxes(conv, 1, 2).reshape(LAYERS, CONV, -1)
    gate = everything[..., second:].reshape(LAYERS, -1)
    return norm, conv, gate


def share_small(norm, conv, gate):
    count = lax.axis_size("dp") * lax.axis_size("seq")
    conv = jnp.swapaxes(conv.reshape(LAYERS, CONV, count, -1), 1, 2).reshape(LAYERS, count, -1)
    pieces = [norm.reshape(LAYERS, count, -1), conv, gate.reshape(LAYERS, count, -1)]
    flat = jnp.swapaxes(jnp.concatenate(pieces, axis=-1), 0, 1).reshape(count, -1)
    size = flat.shape[1]
    tiles = -(-size // (16 * LANES)) * 16
    return jnp.pad(flat, ((0, 0), (0, tiles * LANES - size))).reshape(count, tiles, LANES)


def own_small(mine, norm_gain, conv_weight, gate_gain):
    first = norm_gain.shape[1]
    second = first + conv_weight.shape[1] * conv_weight.shape[2]
    width = second + gate_gain.shape[1]
    mine = mine.reshape(-1)[: LAYERS * width].reshape(LAYERS, width)
    return mine[:, :first], mine[:, first:second].reshape(LAYERS, CONV, -1), mine[:, second:]


def body(
    hidden,
    out_grad,
    lengths,
    norm_gain,
    in_proj,
    conv_weight,
    gate_gain,
    out_proj,
    dt_bias,
    a_log,
    d_skip,
):
    length = hidden.shape[1]
    rows = SLOTS * length
    count = 1 if length >= SHORT else SLOTS
    swap = lengths[0] < lengths[1]

    def ordered(array):
        return jnp.where(swap, array[::-1], array)

    positions = lax.axis_index("seq") * length + jnp.arange(length, dtype=jnp.int32)
    valid = (positions[None, :] < ordered(lengths)[:, None]).astype(f32).reshape(rows, 1)
    valid = jnp.broadcast_to(valid, (rows, LANES))
    gates = in_proj[..., :INNER]
    tails = jnp.pad(in_proj[..., INNER:], ((0, 0), (0, 0), (0, TAIL - (PROJ - INNER))))
    ours = lax.axis_size("dp") == 8 and lax.axis_size("seq") == 4
    packed = pack_small(norm_gain, conv_weight, gate_gain)
    shards = [packed]
    for layer in range(LAYERS):
        shards += [tails[layer], gates[layer], out_proj[layer]]
    ids = iter(range(100))
    if ours:
        moving = Gather(shards, [(1, 1)] + [(3, 2)] * (3 * LAYERS), 1)
        tail_done, gate_done, out_done = [[moving.done(1 + 3 * layer + k) for layer in range(LAYERS)] for k in range(3)]
        end = len(moving.entries) - 1
        run = lambda last: moving.until(min(last, end)) if min(last, end) >= moving.reached else None
        alone(moving.until(tail_done[0]), "gather", next(ids))
        everything = moving.wholes[0].reshape((-1,) + packed.shape)
        whole = moving.whole
    else:
        gathered = [lax.all_gather(shard, ("dp", "seq"), axis=0, tiled=True) for shard in shards]
        everything = gathered[0].reshape((-1,) + packed.shape)
        whole = lambda index: gathered[index]
        run = lambda last: None
        tail_done = gate_done = out_done = [0] * LAYERS
    norm_all, conv_all, gate_all = unpack_small(everything, norm_gain, conv_weight, gate_gain)
    h = ordered(hidden).reshape(rows, D)
    kept = []
    for layer in range(LAYERS):
        gain_row = norm_all[layer].reshape(1, D)
        gate_row = gate_all[layer].reshape(1, INNER)
        taps = jnp.pad(conv_all[layer], ((0, 8 - CONV), (0, TAIL - CONVCH)))
        heads = padded_rows(
            jnp.pad(
                jnp.stack([dt_bias[layer], a_log[layer]]), ((0, 0), (0, LANES - HEADS))
            ),
            8,
        )
        skip_row = jnp.repeat(d_skip[layer], HEADDIM).reshape(1, INNER)
        base = 1 + 3 * layer
        more = tail_done[layer + 1] if layer + 1 < LAYERS else out_done[layer]
        marks = spaced(tail_done[layer], more, (16, 30, 11, 30) if layer + 1 < LAYERS else (18, 30, 11, 0))
        marks[1] = max(marks[1], gate_done[layer])
        marks[2] = max(marks[2], out_done[layer])
        proj, raw, normed, edge, *_ = project(h, gain_row, whole(base), run(marks[0]), next(ids))
        cube = proj.reshape(SLOTS, length, TAIL)
        raw = raw.reshape(SLOTS, length, LANES)
        y, state, cum, size, act, decay, *_ = mix(
            cube, edge, taps, raw, heads, skip_row, count, run(marks[1]), next(ids)
        )
        state = state.reshape(count, NB, NSTATE, BLK)
        gate, *_ = project_gate(normed, whole(base + 1), run(marks[2]), next(ids))
        flat = lambda array: array.reshape(rows, -1)
        h_next, mixture, inverse, *_ = branch(
            flat(y), gate, flat(act), flat(cum), state, gate_row, whole(base + 2), h, valid, run(marks[3]), next(ids)
        )
        kept.append(
            (h, gain_row, gate_row, taps, heads, skip_row, proj, gate, raw, normed, edge, cum, size, act,
             decay, state, mixture, inverse, whole(base), whole(base + 1), whole(base + 2))
        )
        h = h_next
    result = ordered(h.reshape(SLOTS, length, D))

    g = ordered(out_grad).reshape(rows, D)
    small = [None] * LAYERS
    partials = [None] * LAYERS
    totals = [[None] * 3 for _ in range(LAYERS)]
    waiting = None
    cut = lambda partial: partial.reshape(lax.axis_size("dp") * lax.axis_size("seq"), -1, partial.shape[-1])

    def summing(arrays):
        if not ours or arrays[0] is None:
            return None
        return Reduce([cut(array) for array in arrays], [(3, 4)] * len(arrays), 2)

    for layer in reversed(range(LAYERS)):
        (h, gain_row, gate_row, taps, heads, skip_row, proj, gate, raw, normed, edge, cum, size, act,
         decay, state, mixture, inverse, weight_tail, weight_gate, weight_out) = kept[layer]
        cube = proj.reshape(SLOTS, length, TAIL)
        flat = lambda array: array.reshape(rows, -1)
        shaped = lambda array: array.reshape(SLOTS, length, -1)
        grad_gate, partial_out, dy, local, back, partial_gate, *sums = turn(
            g, valid, mixture, gate, inverse, gate_row, weight_out, flat(act), flat(cum), normed, weight_gate, count,
            summing([waiting]), next(ids),
        )
        if waiting is not None and ours:
            totals[layer + 1][0] = sums[0][0]
        grads, late, grad_taps, grad_heads, *sums = unmix(
            cube, edge, taps, raw, heads, skip_row, shaped(dy), state, local, decay, cum, size, act, count,
            summing([partial_gate, partial_out]), next(ids),
        )
        if ours:
            totals[layer][1], totals[layer][2] = sums[0]
        g, grad_norm, waiting = unproject(flat(grads), late, weight_tail, normed, h, g, gain_row, back)
        partials[layer] = (waiting, partial_gate, partial_out)
        small[layer] = (
            grad_norm[0], jnp.sum(grad_taps, axis=0)[:CONV, :CONVCH], grad_gate[0],
            jnp.sum(grad_heads, axis=0)[:3, :HEADS],
        )
    grad_hidden = ordered(g.reshape(SLOTS, length, D))
    stacked = [jnp.stack([small[layer][member] for layer in range(LAYERS)]) for member in range(4)]
    shares = share_small(*stacked[:3])
    head_sums = jnp.pad(stacked[3].reshape(-1, HEADS), ((0, 8 - 3 * LAYERS), (0, LANES - HEADS)))
    if ours:
        totals[0][0], mine, head_sums = alone(
            Reduce([cut(waiting), shares], [(3, 4), (1, 1)], heads=head_sums), "reduce", next(ids)
        )
    else:
        totals = [
            [
                lax.optimization_barrier(
                    lax.psum_scatter(partial, ("dp", "seq"), scatter_dimension=0, tiled=True)
                ).astype(f32)
                for partial in members
            ]
            for members in partials
        ]
        mine = lax.psum_scatter(shares, ("dp", "seq"), scatter_dimension=0, tiled=True)
        head_sums = lax.psum(head_sums, ("dp", "seq"))
    grad_norm, grad_conv, grad_gate = own_small(mine, norm_gain, conv_weight, gate_gain)
    grad_heads = head_sums[: 3 * LAYERS, :HEADS].reshape(LAYERS, 3, HEADS)
    return (
        result,
        grad_hidden,
        grad_norm,
        jnp.stack([jnp.concatenate([gate, tail[:, : PROJ - INNER]], axis=1) for tail, gate, _ in totals]),
        grad_conv,
        grad_gate,
        jnp.stack([members[2] for members in totals]),
        grad_heads[:, 0],
        grad_heads[:, 1],
        grad_heads[:, 2],
    )


def solution(mesh):
    tokens = P("dp", "seq", None)
    every = ("dp", "seq")
    weights = (P(None, every), P(None, every, None), P(None, None, every), P(None, every), P(None, every, None))
    return jax.shard_map(
        body,
        mesh=mesh,
        in_specs=(tokens, tokens, P("dp")) + weights + (P(), P(), P()),
        out_specs=(tokens, tokens) + weights + (P(), P(), P()),
        check_vma=False,
    )
```
